512 devices in a mesh: tm: 32 (over x_lo, z), space: 8 (over y, core), head: 2 (over x_hi).
Axes of the slice: x: 4 (x_hi: 2, x_lo: 2; x = x_hi * 2 + x_lo), y: 4, z: 16, core: 2. Of those that a mesh axis runs over, the one named last changes fastest.
Arguments:
- query_raw: bfloat16 [32, 8, 256, 1536], P('tm', 'space', None, 'head'), may hold values from -40 to 40
- key_raw: bfloat16 [32, 8, 256, 1536], P('tm', 'space', None, 'head'), may hold values from -40 to 40
- values: bfloat16 [32, 8, 256, 1536], P('tm', 'space', None, 'head'), may hold values from -6 to 6
- out_grad: bfloat16 [32, 8, 256, 1536], P('tm', 'space', None, 'head'), may hold values from -192 to 192
- query_gain: float32 [128], replicated, may hold values from 0.1 to 1.9
- key_gain: float32 [128], replicated, may hold values from 0.1 to 1.9
- window_extent: int32 [12, 3], P('head'), may hold values from 0 to 1, as said below
- tile_counts: int32 [4, 8, 8], replicated, may hold values from 64 to 256, as said below
Outputs:
- query_raw_grad: bfloat16 [32, 8, 256, 1536], P('tm', 'space', None, 'head')
- key_raw_grad: bfloat16 [32, 8, 256, 1536], P('tm', 'space', None, 'head')
- value_grads: bfloat16 [32, 8, 256, 1536], P('tm', 'space', None, 'head')
- gain_grads: float32 [2, 128], replicated
The draws below stay inside these ranges and needn't reach their ends.
Inputs may be any that keep to these rules, and one draw needn't show every extreme that they name: `window_extent`: each head's reaches (time, tile columns, tile rows) are (0, 0, 0), (1, 0, 0) or (0, 1, 1); in each of the 2 runs of 6 consecutive heads each of the three occurs exactly 6 // 3 times. `tile_counts`: tiles off the last time tile and off the last tile row are full.
All inputs are finite; a program needn't handle non-finite values.
Results may differ from the reference program's by a relative error of at most 0.009.
Values may be sent and summed in bfloat16 or wider, within the bound.
A program may use at most 64 MiB of HBM per device.

```python
import jax
import jax.numpy as jnp
from jax import lax

HEADS = 12
HD = 128
TILE = 256
TIME_TILES = 4
FEAT = 1536
HEAD_GROUP = 6
COL_TILES = 8
ROW_TILES = 8


def row_column_scales(key):
    row_key, column_key = jax.random.split(key)
    row_scale = jnp.exp(jax.random.uniform(row_key, (TIME_TILES * COL_TILES, ROW_TILES, TILE, HEADS, 1), minval=-1.15, maxval=1.15))
    column_scale = jnp.exp(jax.random.uniform(column_key, (HEADS, HD), minval=-1.15, maxval=1.15))
    return row_scale * column_scale


def scaled_entries(key):
    scale_key, base_key = jax.random.split(key)
    shape_full = (TIME_TILES * COL_TILES, ROW_TILES, TILE, HEADS, HD)
    base = jnp.clip(jax.random.normal(base_key, shape_full), -3.9, 3.9)
    return (base * row_column_scales(scale_key)).reshape(TIME_TILES * COL_TILES, ROW_TILES, TILE, FEAT)


def draw_query_raw(key, part):
    key = jax.random.fold_in(key, 3)
    return scaled_entries(key).astype(jnp.bfloat16)


def draw_key_raw(key, part):
    key = jax.random.fold_in(key, 5)
    return scaled_entries(key).astype(jnp.bfloat16)


def draw_window_extent(key, part):
    key = jax.random.fold_in(key, 7)
    scores = jax.random.randint(key, (HEADS // HEAD_GROUP, HEAD_GROUP), 0, 1 << 20, dtype=jnp.int32)
    scores = scores * HEAD_GROUP + jnp.arange(HEAD_GROUP, dtype=jnp.int32)[None, :]
    kinds = (jnp.argsort(scores, axis=1).astype(jnp.int32) % 3).reshape(HEADS)
    return jnp.stack([kinds == 1, kinds == 2, kinds == 2], axis=1).astype(jnp.int32)


def draw_tile_counts(key, part):
    key = jax.random.fold_in(key, 11)
    drawn = jax.random.randint(key, (TIME_TILES, COL_TILES, ROW_TILES), TILE // 4, TILE + 1, dtype=jnp.int32)
    time_at = jnp.arange(TIME_TILES, dtype=jnp.int32)[:, None, None]
    row_at = jnp.arange(ROW_TILES, dtype=jnp.int32)[None, None, :]
    edge = (time_at == TIME_TILES - 1) | (row_at == ROW_TILES - 1)
    return jnp.where(edge, drawn, TILE).astype(jnp.int32)


def levels(own_key, dims, pieces, smallest, high):
    def one(axis_at, blocks):
        steps = jax.random.uniform(jax.random.fold_in(jax.random.fold_in(own_key, 6), axis_at), (blocks,), jnp.float32, smallest / len(pieces), high / len(pieces))
        return jnp.repeat(jnp.exp(steps), dims[axis_at] // blocks).reshape((-1,) + (1,) * (len(dims) - axis_at - 1))

    gain = one(*pieces[0])
    for cut in pieces[1:]:
        gain = gain * one(*cut)
    return gain


def centred(own_key, extent, spread, reach, cuts=(), held_as=jnp.bfloat16):
    factor_of = levels(own_key, extent, cuts, -0.22, 0.18) if cuts else 1.0
    values = jax.random.normal(own_key, extent, jnp.float32) * spread * factor_of
    return jnp.minimum(jnp.maximum(values, -reach), reach).astype(held_as)


def setup_inputs(seed: int = 0) -> dict:
    key_list = jax.random.split(jax.random.key(seed), 9)
    return {
        "query_raw": draw_query_raw(jax.random.fold_in(key_list[8], 71), 0),
        "key_raw": draw_key_raw(jax.random.fold_in(key_list[8], 71), 0),
        "values": centred(key_list[2], (TIME_TILES * COL_TILES, ROW_TILES, TILE, FEAT), 1.0, 6.0, ((0, 32), (1, 8), (3, 2))),
        "out_grad": centred(key_list[3], (TIME_TILES * COL_TILES, ROW_TILES, TILE, FEAT), 32.0, 192.0, ((0, 32), (1, 8), (3, 2))),
        "query_gain": jnp.clip(1.0 + 0.18 * jax.random.normal(key_list[4], (HD,), jnp.float32), 0.1, 1.9),
        "key_gain": jnp.clip(1.0 + 0.18 * jax.random.normal(key_list[5], (HD,), jnp.float32), 0.1, 1.9),
        "window_extent": draw_window_extent(jax.random.fold_in(key_list[8], 71), 0),
        "tile_counts": draw_tile_counts(jax.random.fold_in(key_list[8], 71), 0),
    }


OFFSETS_BY_KIND = (((0, 0, 0),), ((0, 0, 0), (-1, 0, 0), (1, 0, 0)), ((0, 0, 0), (0, -1, -1), (0, -1, 0), (0, -1, 1), (0, 0, -1), (0, 0, 1), (0, 1, -1), (0, 1, 0), (0, 1, 1)))

def product(pattern, left_op, right_op):
    return jnp.einsum(pattern, left_op.astype(jnp.float32), right_op.astype(jnp.float32))

def normalize(raw_rows, gain_vec, head_count):
    row_count = raw_rows.shape[0]
    entries = raw_rows.astype(jnp.float32).reshape(row_count, head_count, -1)
    inverse = lax.rsqrt(lax.optimization_barrier(jnp.mean(entries * entries, axis=2, keepdims=True)) + 1e-06)
    unit_rows = entries * inverse
    normed = (unit_rows * gain_vec).astype(jnp.bfloat16)
    return (normed, unit_rows, inverse)

def norm_backward(upstream, unit_rows, inverse, gain_vec):
    scaled = upstream * gain_vec
    inner_mean = lax.optimization_barrier(jnp.mean(scaled * unit_rows, axis=2, keepdims=True))
    return (inverse * (scaled - unit_rows * inner_mean), lax.optimization_barrier(jnp.sum(upstream * unit_rows, axis=(0, 1))))

def key_mask(key_count, tile_len):
    return (jnp.arange(tile_len, dtype=jnp.int32) < key_count)[None, None, :]

def forward_stats(product, query_n, key_tiles, value_tiles, window_masks, query_ok, upstream, score_scale):
    logits = [product('qhe,khe->hqk', query_n, key_tile) * score_scale for key_tile in key_tiles]
    totals = jnp.zeros(logits[0].shape[:2], jnp.float32)
    for logit_block, window_mask in zip(logits, window_masks):
        totals = totals + lax.optimization_barrier(jnp.sum(jnp.where(window_mask, jnp.exp(logit_block), 0.0), axis=2))
    log_total = jnp.log(totals)
    row_mask = query_ok[None, :, None]
    weights = [jnp.where(window_mask & row_mask, jnp.exp(logit_block - log_total[:, :, None]), 0.0) for logit_block, window_mask in zip(logits, window_masks)]
    weights_b = [weight_block.astype(jnp.bfloat16) for weight_block in weights]
    attended = jnp.zeros(query_n.shape, jnp.float32)
    for weight_b, value_tile in zip(weights_b, value_tiles):
        attended = attended + product('hqk,khe->qhe', weight_b, value_tile)
    out_dot = jnp.einsum('qhe,qhe->hq', upstream.astype(jnp.float32), attended)
    return (log_total, out_dot, weights, weights_b)

def query_grads(product, query_n, key_tiles, value_tiles, upstream, out_dot, weights, weights_b, score_scale, part_count):
    query_grad = jnp.zeros(query_n.shape, jnp.float32)
    key_parts, value_parts = ([], [])
    for block_idx in range(len(key_tiles)):
        prob_grad = product('qhe,khe->hqk', upstream, value_tiles[block_idx])
        logit_grad = (weights[block_idx] * (prob_grad - out_dot[:, :, None])).astype(jnp.bfloat16)
        query_grad = query_grad + product('hqk,khe->qhe', logit_grad, key_tiles[block_idx]) * score_scale
        if block_idx < part_count:
            key_parts.append(product('hqk,qhe->khe', logit_grad, query_n) * score_scale)
            value_parts.append(product('hqk,qhe->khe', weights_b[block_idx], upstream))
    return (query_grad, key_parts, value_parts)

def key_pass(product, key_here, value_here, near_query, near_upstream, log_total, out_dot, own_mask, near_ok, score_scale):
    logit_block = product('qhe,khe->hqk', near_query, key_here) * score_scale
    weight_block = jnp.where(own_mask & near_ok[None, :, None], jnp.exp(logit_block - log_total[:, :, None]), 0.0)
    prob_grad = product('qhe,khe->hqk', near_upstream, value_here)
    logit_grad = (weight_block * (prob_grad - out_dot[:, :, None])).astype(jnp.bfloat16)
    key_term = product('hqk,qhe->khe', logit_grad, near_query) * score_scale
    value_term = product('hqk,qhe->khe', weight_block.astype(jnp.bfloat16), near_upstream)
    return (key_term, value_term)

def rounded(term):
    return lax.optimization_barrier(term.astype(jnp.bfloat16)).astype(jnp.float32)

def tile_at(padded, time_at, col_at, row_at):
    starts = [time_at, col_at, row_at] + [jnp.int32(0)] * (padded.ndim - 3)
    return lax.dynamic_slice(padded, starts, (1, 1, 1) + padded.shape[3:])[0, 0, 0]

def reference(query_raw, key_raw, values, out_grad, query_gain, key_gain, window_extent, tile_counts):
    score_scale = HD ** (-0.5)
    kind_size = HEADS // 3
    grid = (TIME_TILES, COL_TILES, ROW_TILES, TILE, HEADS, HD)
    pad_widths = ((1, 1), (1, 1), (1, 1), (0, 0), (0, 0), (0, 0))
    query_n, query_unit, query_inv = normalize(query_raw.reshape(-1, FEAT), query_gain, HEADS)
    key_n, key_unit, key_inv = normalize(key_raw.reshape(-1, FEAT), key_gain, HEADS)
    kind_code = (window_extent[:, 0] + 2 * window_extent[:, 1]).astype(jnp.int32)
    head_order = jnp.argsort(kind_code * HEADS + jnp.arange(HEADS, dtype=jnp.int32)).astype(jnp.int32)
    inverse = jnp.argsort(head_order).astype(jnp.int32)
    count_pad = jnp.pad(tile_counts, 1)
    lanes_idx = jnp.arange(TILE, dtype=jnp.int32)
    tile_ids = jnp.arange(TIME_TILES * COL_TILES * ROW_TILES, dtype=jnp.int32)

    def padded_group(normed, kind_idx):
        chosen = head_order[kind_idx * kind_size:(kind_idx + 1) * kind_size]
        return jnp.pad(jnp.take(normed.reshape(grid), chosen, axis=4), pad_widths)

    def position(flat):
        time_at = (flat // (COL_TILES * ROW_TILES) + 1).astype(jnp.int32)
        col_at = (flat // ROW_TILES % COL_TILES + 1).astype(jnp.int32)
        row_at = (flat % ROW_TILES + 1).astype(jnp.int32)
        return (time_at, col_at, row_at)
    query_lists, key_lists, value_lists = ([], [], [])
    for kind_idx in range(3):
        offsets = OFFSETS_BY_KIND[kind_idx]
        query_pad = padded_group(query_n, kind_idx)
        key_pad = padded_group(key_n, kind_idx)
        value_pad = padded_group(values, kind_idx)
        upstream_pad = padded_group(out_grad, kind_idx)

        def neighbours(time_at, col_at, row_at):
            key_tiles, value_tiles, window_masks = ([], [], [])
            for offset in offsets:
                near_t, near_c, near_r = (time_at + offset[0], col_at + offset[1], row_at + offset[2])
                key_tiles.append(tile_at(key_pad, near_t, near_c, near_r))
                value_tiles.append(tile_at(value_pad, near_t, near_c, near_r))
                window_masks.append(key_mask(count_pad[near_t, near_c, near_r], TILE))
            return (key_tiles, value_tiles, window_masks)

        def stats_of(flat):
            time_at, col_at, row_at = position(flat)
            key_tiles, value_tiles, window_masks = neighbours(time_at, col_at, row_at)
            query_ok = lanes_idx < count_pad[time_at, col_at, row_at]
            log_total, out_dot, weights, weights_b = forward_stats(product, tile_at(query_pad, time_at, col_at, row_at), key_tiles, value_tiles, window_masks, query_ok, tile_at(upstream_pad, time_at, col_at, row_at), score_scale)
            return (log_total, out_dot)
        log_all, dot_all = lax.map(stats_of, tile_ids)
        stat_pad = jnp.pad(jnp.stack([log_all, dot_all], axis=1).reshape(TIME_TILES, COL_TILES, ROW_TILES, 2, kind_size, TILE), pad_widths)

        def grads_of(flat):
            time_at, col_at, row_at = position(flat)
            key_tiles, value_tiles, window_masks = neighbours(time_at, col_at, row_at)
            own_count = count_pad[time_at, col_at, row_at]
            query_ok = lanes_idx < own_count
            query_here = tile_at(query_pad, time_at, col_at, row_at)
            upstream_here = tile_at(upstream_pad, time_at, col_at, row_at)
            log_total, out_dot, weights, weights_b = forward_stats(product, query_here, key_tiles, value_tiles, window_masks, query_ok, upstream_here, score_scale)
            query_grad, key_parts, value_parts = query_grads(product, query_here, key_tiles, value_tiles, upstream_here, out_dot, weights, weights_b, score_scale, 0)
            key_here = tile_at(key_pad, time_at, col_at, row_at)
            value_here = tile_at(value_pad, time_at, col_at, row_at)
            own_mask = key_mask(own_count, TILE)
            key_grad = jnp.zeros((TILE, kind_size, HD), jnp.float32)
            value_grad = jnp.zeros((TILE, kind_size, HD), jnp.float32)
            for offset in offsets:
                near_t, near_c, near_r = (time_at + offset[0], col_at + offset[1], row_at + offset[2])
                near_stats = tile_at(stat_pad, near_t, near_c, near_r)
                near_ok = lanes_idx < count_pad[near_t, near_c, near_r]
                key_term, value_term = key_pass(product, key_here, value_here, tile_at(query_pad, near_t, near_c, near_r), tile_at(upstream_pad, near_t, near_c, near_r), near_stats[0], near_stats[1], own_mask, near_ok, score_scale)
                if offset == (0, 0, 0):
                    key_grad = key_grad + key_term
                    value_grad = value_grad + value_term
                else:
                    key_grad = key_grad + rounded(key_term)
                    value_grad = value_grad + rounded(value_term)
            return (query_grad, key_grad, value_grad)
        query_part, key_part, value_part = lax.map(grads_of, tile_ids)
        query_lists.append(query_part)
        key_lists.append(key_part)
        value_lists.append(value_part)

    def restore(parts):
        joined = jnp.concatenate(parts, axis=2)
        return jnp.take(joined, inverse, axis=2).reshape(-1, HEADS, HD)
    query_all = restore(query_lists)
    key_all = restore(key_lists)
    value_all = restore(value_lists)
    query_back, query_gain_grad = norm_backward(query_all, query_unit, query_inv, query_gain)
    key_back, key_gain_grad = norm_backward(key_all, key_unit, key_inv, key_gain)
    shape_out = (TIME_TILES * COL_TILES, ROW_TILES, TILE, FEAT)
    return (query_back.astype(jnp.bfloat16).reshape(shape_out), key_back.astype(jnp.bfloat16).reshape(shape_out), value_all.astype(jnp.bfloat16).reshape(shape_out), jnp.stack([query_gain_grad, key_gain_grad]))
```

```python
import functools

import jax
import jax.numpy as jnp
from jax import lax
from jax.experimental import pallas as pl
from jax.experimental.pallas import tpu as pltpu
from jax.sharding import PartitionSpec as P

MESH = pl.DeviceIdType.MESH
HD = 128
F32 = jnp.float32
BF16 = jnp.bfloat16
SCALE = HD**-0.5
LOG2E = 1.4426950408889634
NT = (((1,), (1,)), ((), ()))
NN = (((1,), (0,)), ((), ()))
TN = (((0,), (0,)), ((), ()))

LOCAL, TIME, SPACE = 0, 2, 4


def dot(a, b, dims):
    return lax.dot_general(a, b, dims, preferred_element_type=F32)


def unit_of(raw):
    x = raw.astype(F32)
    inv = lax.rsqrt(jnp.mean(x * x, axis=1, keepdims=True) + 1e-6)
    return x * inv, inv


def fold(x):
    return jnp.sum(x.reshape(x.shape[0] // 8, 8, x.shape[1]), axis=0)


def kernel(
    T, C, R, H, tile, chunk,
    we, counts, qgain, kgain, qraw, kraw, vals, ograd,
    oq, ok, ov, og,
    hq, hk, hv, ho, qs, dos, kvl, kvt, kvs, pp, dd, stats, dqt, fk, fv,
    tacc, xout, xin, zout, zin, sacc, rowo, rowi, colo, coli,
    resq, resk, resv, gacc, gbuf,
    zf_s, zf_r, xf_s, xf_r, cf_s, cf_r, rf_s, rf_r,
    zb_s, zb_r, xb_s, xb_r, cb_s, cb_r, rb_s, rb_r, g_s, g_r,
):
    tm = lax.axis_index("tm")
    r = lax.axis_index("space")
    hd = lax.axis_index("head")
    t = lax.div(tm, C)
    c = lax.rem(tm, C)
    tz = t + 1 - 2 * lax.rem(t, 2)
    tx = lax.rem(t + 2, T)
    td = lax.rem(tz + 2, T)

    def dev(t_, c_, r_, h_):
        return (t_ * C + c_, r_, h_)

    G0 = T * H
    gi = t * H + hd

    def peer0(j):
        g = lax.rem(gi + j, G0)
        return dev(lax.div(g, H), c, r, lax.rem(g, H))

    def peer1(j):
        return dev(t, lax.rem(c + j, C), r, hd)

    def peer2(j):
        return dev(t, c, lax.rem(r + j, R), hd)

    groups = ((G0, gi, peer0), (C, c, peer1), (R, r, peer2))
    barrier = pltpu.get_barrier_semaphore()
    for size, _, peer in groups:
        for j in range(1, size):
            pl.semaphore_signal(barrier, inc=1, device_id=peer(j), device_id_type=MESH)

    kinds = [we[h, 0] + 2 * we[h, 1] for h in range(6)]
    head_of = []
    for kind in range(3):
        low, high = jnp.int32(5), jnp.int32(0)
        for h in range(6):
            low = jnp.minimum(low, jnp.where(kinds[h] == kind, h, 5))
            high = jnp.maximum(high, jnp.where(kinds[h] == kind, h, 0))
        head_of += [low, high]
    slot_of = []
    for h in range(6):
        before = jnp.int32(0)
        for g in range(h):
            before = before + jnp.where(kinds[g] == kinds[h], 1, 0)
        slot_of.append(2 * kinds[h] + before)

    for by_head, whole in ((hk, kraw), (hv, vals), (hq, qraw), (ho, ograd)):
        for h in range(6):
            by_head[h] = whole[:, h * HD : (h + 1) * HD]

    def raw(ref, slot):
        return ref[head_of[slot]]

    def normed(ref, slot, gain):
        unit, _ = unit_of(raw(ref, slot))
        return (unit * gain[...]).astype(BF16)

    def count_at(t_, c_, r_):
        inside = (c_ >= 0) & (c_ < C) & (r_ >= 0) & (r_ < R)
        got = counts[t_, lax.rem(c_ + C, C), lax.rem(r_ + R, R)]
        return jnp.where(inside, got, 0)

    own_count = count_at(t, c, r)
    lanes = lax.broadcasted_iota(jnp.int32, (1, tile), 1)
    query_ok = lanes < own_count
    rows_iota = lax.broadcasted_iota(jnp.int32, (chunk, tile), 0)

    def side(step):
        return (step + 1) // 2

    def c_ok(step):
        return (c + step >= 0) & (c + step < C)

    def r_ok(step):
        return (r + step >= 0) & (r + step < R)

    def c_dev(step):
        return dev(t, lax.rem(c + step + C, C), r, hd)

    def r_dev(step):
        return dev(t, c, lax.rem(r + step + R, R), hd)

    def copy(src, dst, send, recv, where):
        return pltpu.make_async_remote_copy(
            src_ref=src, dst_ref=dst, send_sem=send, recv_sem=recv, device_id=where, device_id_type=MESH
        )

    def col_fwd(step):
        return copy(kvs.at[1, 1], kvs.at[1, 1 - step], cf_s.at[side(step)], cf_r.at[side(-step)], c_dev(step))

    def row_fwd(step, dc):
        return copy(
            kvs.at[1, 1 + dc], kvs.at[1 - step, 1 + dc],
            rf_s.at[side(step), 1 + dc], rf_r.at[side(-step), 1 + dc], r_dev(step),
        )

    def z_fwd(h):
        return copy(kvt.at[0, h], kvt.at[1, h], zf_s.at[h], zf_r.at[h], dev(tz, c, r, hd))

    def x_fwd(h):
        return copy(kvt.at[1, h], kvt.at[2, h], xf_s.at[h], xf_r.at[h], dev(tx, c, r, hd))

    def x_bwd(h):
        return copy(xout.at[h], xin.at[h], xb_s.at[h], xb_r.at[h], dev(tx, c, r, hd))

    def z_bwd(h):
        return copy(zout.at[h], zin.at[h], zb_s.at[h], zb_r.at[h], dev(tz, c, r, hd))

    def row_bwd(step, h):
        return copy(
            rowo.at[h, side(step)], rowi.at[h, side(-step)],
            rb_s.at[h, side(step)], rb_r.at[h, side(-step)], r_dev(step),
        )

    def col_bwd(step, h):
        return copy(
            colo.at[h, side(step)], coli.at[h, side(-step)],
            cb_s.at[h, side(step)], cb_r.at[h, side(-step)], c_dev(step),
        )

    def on(condition, action):
        pl.when(condition)(action)

    STEPS = (-1, 1)

    for h in range(2):
        kvs[1, 1, h, 0] = normed(hk, SPACE + h, kgain)
        kvs[1, 1, h, 1] = raw(hv, SPACE + h)
    pl.semaphore_wait(barrier, G0 - 1 + C - 1 + R - 1)
    for step in STEPS:
        on(c_ok(step), col_fwd(step).start)
    for step in STEPS:
        on(r_ok(step), row_fwd(step, 0).start)
    for h in range(2):
        kvt[0, h, 0] = normed(hk, TIME + h, kgain)
        kvt[0, h, 1] = raw(hv, TIME + h)
        z_fwd(h).start()

    nothing = jnp.zeros((2, 2, tile, HD), BF16)
    for step in STEPS:

        def blank_column(step=step):
            for dr in range(3):
                kvs[dr, 1 + step] = nothing

        def blank_row(step=step):
            for dc in range(3):
                kvs[1 + step, dc] = nothing

        on(jnp.logical_not(c_ok(step)), blank_column)
        on(jnp.logical_not(r_ok(step)), blank_row)

    for h in range(2):
        kvl[h, 0] = normed(hk, LOCAL + h, kgain)
        kvl[h, 1] = raw(hv, LOCAL + h)
    for s in range(6):
        qs[s] = normed(hq, s, qgain)
        dos[s] = raw(ho, s)
    stats[...] = jnp.zeros_like(stats)
    dqt[...] = jnp.zeros_like(dqt)
    gacc[...] = jnp.zeros_like(gacc)
    sacc[...] = jnp.zeros_like(sacc)

    def pass_one(idx, slot, kv, count):
        query, up = qs[slot], dos[slot]
        sum_l, sum_d = stats[slot, 0:8], stats[slot, 8:16]
        for j in range(0, tile, chunk):
            s = dot(kv[0, j : j + chunk], query, NT)
            p = jnp.where(rows_iota < count - j, jnp.exp2(s * (SCALE * LOG2E)), 0.0)
            dp = dot(kv[1, j : j + chunk], up, NT)
            pp[idx, j : j + chunk] = p
            dd[idx, j : j + chunk] = dp
            sum_l = sum_l + fold(p)
            sum_d = sum_d + fold(p * dp)
        stats[slot, 0:8] = sum_l
        stats[slot, 8:16] = sum_d

    def finish_stats(slot):
        inv = 1.0 / jnp.sum(stats[slot, 0:8], axis=0, keepdims=True)
        out_dot = jnp.sum(stats[slot, 8:16], axis=0, keepdims=True) * inv
        stats[slot, 0:8] = jnp.broadcast_to(jnp.where(query_ok, inv, 0.0), (8, tile))
        stats[slot, 8:16] = jnp.broadcast_to(out_dot, (8, tile))

    def pass_two(idx, slot, kv, emit):
        query, up = qs[slot], dos[slot]
        inv, out_dot = stats[slot, 0:1], stats[slot, 8:9]
        key_sum = gacc[slot]
        dq = dqt[slot]
        for j in range(0, tile, chunk):
            w = pp[idx, j : j + chunk] * inv
            g = (w * (dd[idx, j : j + chunk] - out_dot)).astype(BF16)
            keys = kv[0, j : j + chunk]
            dk = dot(g, query, NN)
            dv = dot(w.astype(BF16), up, NN)
            dq = dq + dot(keys, g, TN)
            key_sum = key_sum + fold(dk * keys.astype(F32))
            emit(j, dk, dv)
        gacc[slot] = key_sum
        dqt[slot] = dq

    def at_time(h, b):
        return 2 + 3 * h + b

    def at_space(h, dr, dc):
        return 8 + 9 * h + 3 * dr + dc

    def space_one(dr, dc):
        count = count_at(t, c + dc - 1, r + dr - 1)
        for h in range(2):
            pass_one(at_space(h, dr, dc), SPACE + h, kvs.at[dr, dc, h], count)

    def loop(n, body):
        def step(i, carry):
            body(i)
            return carry

        lax.fori_loop(0, n, step, 0)

    space_one(1, 1)
    for h in range(2):
        pass_one(h, LOCAL + h, kvl.at[h], own_count)
        finish_stats(LOCAL + h)
    for h in range(2):

        def emit_local(j, dk, dv, h=h):
            fk[LOCAL + h, j : j + chunk] = dk
            fv[LOCAL + h, j : j + chunk] = dv

        pass_two(h, LOCAL + h, kvl.at[h], emit_local)
    for h in range(2):
        pass_one(at_time(h, 0), TIME + h, kvt.at[0, h], own_count)

    for dc in STEPS:
        on(c_ok(dc), col_fwd(-dc).wait_recv)
    for dc in STEPS:
        for step in STEPS:
            on(c_ok(dc) & r_ok(step), row_fwd(step, dc).start)
    loop(2, lambda i: space_one(1, 2 * i))
    for dr in STEPS:
        on(r_ok(dr), row_fwd(-dr, 0).wait_recv)
    loop(2, lambda i: space_one(2 * i, 1))

    z_fwd(0).wait_recv()
    x_fwd(0).start()

    for dr in STEPS:
        for dc in STEPS:
            on(r_ok(dr) & c_ok(dc), row_fwd(-dr, dc).wait_recv)

    def corner(i):
        dr = lax.div(i, 2)
        space_one(2 * dr, 2 * (i - 2 * dr))

    loop(4, corner)
    for h in range(2):
        finish_stats(SPACE + h)

    for h in range(2):

        def outer_rows(i, h=h):
            d = lax.div(i, 3)
            dc = i - 3 * d

            def emit(j, dk, dv):
                rowo[h, d, dc, 0, pl.ds(j, chunk)] = dk.astype(BF16)
                rowo[h, d, dc, 1, pl.ds(j, chunk)] = dv.astype(BF16)

            pass_two(at_space(h, 2 * d, dc), SPACE + h, kvs.at[2 * d, dc, h], emit)

        loop(6, outer_rows)
        for step in STEPS:
            on(r_ok(step), row_bwd(step, h).start)

    time_counts = (own_count, count_at(tz, c, r), jnp.where((td - t) * (td - t) == 1, count_at(td, c, r), 0))

    def time_head(h):
        pass_one(at_time(h, 1), TIME + h, kvt.at[1, h], time_counts[1])
        x_fwd(h).wait_recv()
        pass_one(at_time(h, 2), TIME + h, kvt.at[2, h], time_counts[2])
        finish_stats(TIME + h)

        def emit_far(j, dk, dv):
            xout[h, 0, j : j + chunk] = dk.astype(BF16)
            xout[h, 1, j : j + chunk] = dv.astype(BF16)

        def emit_near(j, dk, dv):
            tacc[h, 0, j : j + chunk] = dk
            tacc[h, 1, j : j + chunk] = dv

        def emit_own(j, dk, dv):
            fk[TIME + h, j : j + chunk] = dk
            fv[TIME + h, j : j + chunk] = dv

        pass_two(at_time(h, 2), TIME + h, kvt.at[2, h], emit_far)
        x_bwd(h).start()
        pass_two(at_time(h, 1), TIME + h, kvt.at[1, h], emit_near)
        pass_two(at_time(h, 0), TIME + h, kvt.at[0, h], emit_own)
        x_bwd(h).wait_recv()
        zout[h] = (tacc[h] + xin[h].astype(F32)).astype(BF16)
        z_bwd(h).start()

    time_head(0)

    def middle_row(i):
        for h in range(2):

            def emit(j, dk, dv, h=h):
                sacc[i, h, 0, pl.ds(j, chunk)] = dk
                sacc[i, h, 1, pl.ds(j, chunk)] = dv

            pass_two(at_space(h, 1, i), SPACE + h, kvs.at[1, i, h], emit)

    loop(3, middle_row)

    z_fwd(1).wait_recv()
    x_fwd(1).start()

    for h in range(2):
        for dr in STEPS:

            def add_row(dr=dr, h=h):
                row_bwd(-dr, h).wait_recv()
                for dc in range(3):
                    sacc[dc, h] = sacc[dc, h] + rowi[h, side(dr), dc].astype(F32)

            on(r_ok(dr), add_row)
        for step in STEPS:

            def send_column(step=step, h=h):
                colo[h, side(step)] = sacc[1 + step, h].astype(BF16)
                col_bwd(step, h).start()

            on(c_ok(step), send_column)

    time_head(1)

    query_sum = jnp.zeros((8, HD), F32)
    for s in range(6):
        grad = jnp.transpose(dqt[s]) * SCALE
        unit, inv = unit_of(raw(hq, s))
        scaled = grad * qgain[...]
        mean = jnp.mean(scaled * unit, axis=1, keepdims=True)
        resq[s] = (inv * (scaled - unit * mean)).astype(BF16)
        query_sum = query_sum + fold(grad * unit)
    key_sum = gacc[0]
    for s in range(1, 6):
        key_sum = key_sum + gacc[s]

    def gain_copy(n, j):
        _, mine, peer = groups[n]
        return copy(gbuf.at[n, mine], gbuf.at[n, mine], g_s.at[n, j], g_r.at[n, mine], peer(j))

    def gain_send(n, value):
        size, mine, _ = groups[n]
        gbuf[n, mine] = value
        for j in range(1, size):
            gain_copy(n, j).start()

    def gain_sum(n):
        size, mine, peer = groups[n]
        for j in range(1, size):
            other = lax.rem(mine + j, size)
            copy(gbuf.at[n, other], gbuf.at[n, other], g_s.at[n, j], g_r.at[n, other], peer(j)).wait_recv()
        total = gbuf[n, 0]
        for i in range(1, size):
            total = total + gbuf[n, i]
        return total

    pair = jnp.concatenate(
        [
            jnp.sum(query_sum, axis=0, keepdims=True),
            jnp.sum(key_sum, axis=0, keepdims=True) * SCALE / kgain[...],
            jnp.zeros((6, HD), F32),
        ],
        axis=0,
    )
    gain_send(0, pair)

    def key_out(s):
        grad = fk[s] * SCALE
        unit, inv = unit_of(raw(hk, s))
        scaled = grad * kgain[...]
        mean = jnp.mean(scaled * unit, axis=1, keepdims=True)
        resk[s] = (inv * (scaled - unit * mean)).astype(BF16)
        resv[s] = fv[s].astype(BF16)

    for h in range(2):
        key_out(LOCAL + h)
    gain_send(1, gain_sum(0))

    for h in range(6):
        oq[:, h * HD : (h + 1) * HD] = resq[slot_of[h]]
    for h in range(2):
        for dc in STEPS:

            def add_column(dc=dc, h=h):
                col_bwd(-dc, h).wait_recv()
                sacc[1, h] = sacc[1, h] + coli[h, side(dc)].astype(F32)

            on(c_ok(dc), add_column)
        fk[SPACE + h] = sacc[1, h, 0]
        fv[SPACE + h] = sacc[1, h, 1]
        key_out(SPACE + h)
    gain_send(2, gain_sum(1))

    for h in range(2):
        z_bwd(h).wait_recv()
        fk[TIME + h] = fk[TIME + h] + zin[h, 0].astype(F32)
        fv[TIME + h] = fv[TIME + h] + zin[h, 1].astype(F32)
        key_out(TIME + h)
    for h in range(6):
        ok[:, h * HD : (h + 1) * HD] = resk[slot_of[h]]
        ov[:, h * HD : (h + 1) * HD] = resv[slot_of[h]]
    og[...] = gain_sum(2)[0:2]

    for h in range(2):
        z_fwd(h).wait_send()
        x_fwd(h).wait_send()
        x_bwd(h).wait_send()
        z_bwd(h).wait_send()
    for step in STEPS:
        on(c_ok(step), col_fwd(step).wait_send)
        on(r_ok(step), row_fwd(step, 0).wait_send)
        for dc in STEPS:
            on(c_ok(dc) & r_ok(step), row_fwd(step, dc).wait_send)
        for h in range(2):
            on(r_ok(step), row_bwd(step, h).wait_send)
            on(c_ok(step), col_bwd(step, h).wait_send)
    for n, (size, _, _) in enumerate(groups):
        for j in range(1, size):
            gain_copy(n, j).wait_send()


def on_device(T, C, R, H, query_raw, key_raw, values, out_grad, query_gain, key_gain, window_extent, tile_counts):
    tile, width = query_raw.shape[2], query_raw.shape[3]
    chunk = min(128, tile)
    flat = lambda x: x.reshape(tile, width)
    most = max(T * H, C, R)
    dma = pltpu.SemaphoreType.DMA
    vmem = pl.BlockSpec(memory_space=pltpu.VMEM)
    smem = pl.BlockSpec(memory_space=pltpu.SMEM)
    blocks = 2 + 6 + 18
    scratch = [
        pltpu.VMEM((6, tile, HD), BF16),
        pltpu.VMEM((6, tile, HD), BF16),
        pltpu.VMEM((6, tile, HD), BF16),
        pltpu.VMEM((6, tile, HD), BF16),
        pltpu.VMEM((6, tile, HD), BF16),
        pltpu.VMEM((6, tile, HD), BF16),
        pltpu.VMEM((2, 2, tile, HD), BF16),
        pltpu.VMEM((3, 2, 2, tile, HD), BF16),
        pltpu.VMEM((3, 3, 2, 2, tile, HD), BF16),
        pltpu.VMEM((blocks, tile, tile), F32),
        pltpu.VMEM((blocks, tile, tile), F32),
        pltpu.VMEM((6, 16, tile), F32),
        pltpu.VMEM((6, HD, tile), F32),
        pltpu.VMEM((6, tile, HD), F32),
        pltpu.VMEM((6, tile, HD), F32),
        pltpu.VMEM((2, 2, tile, HD), F32),
        pltpu.VMEM((2, 2, tile, HD), BF16),
        pltpu.VMEM((2, 2, tile, HD), BF16),
        pltpu.VMEM((2, 2, tile, HD), BF16),
        pltpu.VMEM((2, 2, tile, HD), BF16),
        pltpu.VMEM((3, 2, 2, tile, HD), F32),
        pltpu.VMEM((2, 2, 3, 2, tile, HD), BF16),
        pltpu.VMEM((2, 2, 3, 2, tile, HD), BF16),
        pltpu.VMEM((2, 2, 2, tile, HD), BF16),
        pltpu.VMEM((2, 2, 2, tile, HD), BF16),
        pltpu.VMEM((6, tile, HD), BF16),
        pltpu.VMEM((6, tile, HD), BF16),
        pltpu.VMEM((6, tile, HD), BF16),
        pltpu.VMEM((6, 8, HD), F32),
        pltpu.VMEM((3, most, 8, HD), F32),
        dma((2,)), dma((2,)), dma((2,)), dma((2,)),
        dma((2,)), dma((2,)), dma((2, 3)), dma((2, 3)),
        dma((2,)), dma((2,)), dma((2,)), dma((2,)),
        dma((2, 2)), dma((2, 2)), dma((2, 2)), dma((2, 2)),
        dma((3, most)), dma((3, most)),
    ]
    wide = jax.ShapeDtypeStruct((tile, width), BF16)
    grad_q, grad_k, grad_v, gains = pl.pallas_call(
        functools.partial(kernel, T, C, R, H, tile, chunk),
        out_shape=(wide, wide, wide, jax.ShapeDtypeStruct((2, HD), F32)),
        in_specs=[smem, smem] + [vmem] * 6,
        out_specs=(vmem,) * 4,
        scratch_shapes=scratch,
        compiler_params=pltpu.CompilerParams(
            collective_id=0, has_side_effects=True, vmem_limit_bytes=60 * 1024 * 1024
        ),
    )(
        window_extent,
        tile_counts,
        query_gain.reshape(1, HD),
        key_gain.reshape(1, HD),
        flat(query_raw),
        flat(key_raw),
        flat(values),
        flat(out_grad),
    )
    shape = (1, 1, tile, width)
    return grad_q.reshape(shape), grad_k.reshape(shape), grad_v.reshape(shape), gains


def solution(mesh):
    tile_spec = P("tm", "space", None, "head")

    def program(*args):
        T = args[7].shape[0]
        C = mesh.shape["tm"] // T
        return on_device(T, C, mesh.shape["space"], mesh.shape["head"], *args)

    return jax.shard_map(
        program,
        mesh=mesh,
        in_specs=(tile_spec,) * 4 + (P(), P(), P("head", None), P()),
        out_specs=(tile_spec,) * 3 + (P(),),
        check_vma=False,
    )
```

```python
import functools

import jax
import jax.numpy as jnp
from jax import lax
from jax.experimental import pallas as pl
from jax.experimental.pallas import tpu as pltpu
from jax.sharding import PartitionSpec as P

MESH = pl.DeviceIdType.MESH
HD = 128
F32 = jnp.float32
BF16 = jnp.bfloat16
SCALE = HD**-0.5
LOG2E = 1.4426950408889634
NT = (((1,), (1,)), ((), ()))
NN = (((1,), (0,)), ((), ()))
TN = (((0,), (0,)), ((), ()))

LOCAL, TIME, SPACE = 0, 2, 4


def dot(a, b, dims):
    return lax.dot_general(a, b, dims, preferred_element_type=F32)


def unit_of(raw):
    x = raw.astype(F32)
    inv = lax.rsqrt(jnp.mean(x * x, axis=1, keepdims=True) + 1e-6)
    return x * inv, inv


def fold(x):
    return jnp.sum(x.reshape(x.shape[0] // 8, 8, x.shape[1]), axis=0)


def kernel(
    T, C, R, H, tile, chunk,
    we, counts, qgain, kgain, qraw, kraw, vals, ograd,
    oq, ok, ov, og,
    hq, hk, hv, ho, qs, kvl, kvh, qdt, kvs, pp, dd, stats, sto, sti, dqt, fk, fv,
    xout, xin, zout, zin, sacc, rowo, rowi, colo, coli, gacc, gbuf,
    zf_s, zf_r, xf_s, xf_r, cf_s, cf_r, rf_s, rf_r,
    zb_s, zb_r, xb_s, xb_r, cb_s, cb_r, rb_s, rb_r, st_s, st_r, g_s, g_r,
):
    tm = lax.axis_index("tm")
    r = lax.axis_index("space")
    hd = lax.axis_index("head")
    t = lax.div(tm, C)
    c = lax.rem(tm, C)
    tz = t + 1 - 2 * lax.rem(t, 2)
    tx = lax.rem(t + 2, T)
    td = lax.rem(tz + 2, T)

    def dev(t_, c_, r_, h_):
        return (t_ * C + c_, r_, h_)

    G0 = T * H
    gi = t * H + hd

    def peer0(j):
        g = lax.rem(gi + j, G0)
        return dev(lax.div(g, H), c, r, lax.rem(g, H))

    def peer1(j):
        return dev(t, lax.rem(c + j, C), r, hd)

    def peer2(j):
        return dev(t, c, lax.rem(r + j, R), hd)

    groups = ((G0, gi, peer0), (C, c, peer1), (R, r, peer2))
    barrier = pltpu.get_barrier_semaphore()
    for size, _, peer in groups:
        for j in range(1, size):
            pl.semaphore_signal(barrier, inc=1, device_id=peer(j), device_id_type=MESH)

    kinds = [we[0, h] + 2 * we[1, h] for h in range(6)]
    head_of = []
    for kind in range(3):
        low, high = jnp.int32(5), jnp.int32(0)
        for h in range(6):
            low = jnp.minimum(low, jnp.where(kinds[h] == kind, h, 5))
            high = jnp.maximum(high, jnp.where(kinds[h] == kind, h, 0))
        head_of += [low, high]
    for by_head, whole in ((hk, kraw), (hv, vals), (hq, qraw), (ho, ograd)):
        for h in range(6):
            by_head[h] = whole[:, h * HD : (h + 1) * HD]

    def raw(ref, slot):
        return ref[head_of[slot]]

    def normed(ref, slot, gain):
        unit, _ = unit_of(raw(ref, slot))
        return (unit * gain[...]).astype(BF16)

    def count_at(t_, c_, r_):
        inside = (c_ >= 0) & (c_ < C) & (r_ >= 0) & (r_ < R)
        got = counts[t_, lax.rem(c_ + C, C), lax.rem(r_ + R, R)]
        return jnp.where(inside, got, 0)

    own_count = count_at(t, c, r)
    lanes = lax.broadcasted_iota(jnp.int32, (1, tile), 1)
    query_ok = lanes < own_count
    rows_iota = lax.broadcasted_iota(jnp.int32, (chunk, tile), 0)

    def side(step):
        return (step + 1) // 2

    def c_ok(step):
        return (c + step >= 0) & (c + step < C)

    def r_ok(step):
        return (r + step >= 0) & (r + step < R)

    def c_dev(step):
        return dev(t, lax.rem(c + step + C, C), r, hd)

    def r_dev(step):
        return dev(t, c, lax.rem(r + step + R, R), hd)

    def copy(src, dst, send, recv, where):
        return pltpu.make_async_remote_copy(
            src_ref=src, dst_ref=dst, send_sem=send, recv_sem=recv, device_id=where, device_id_type=MESH
        )

    def col_fwd(step):
        return copy(kvs.at[1, 1], kvs.at[1, 1 - step], cf_s.at[side(step)], cf_r.at[side(-step)], c_dev(step))

    def row_fwd(step, dc):
        return copy(
            kvs.at[1, 1 + dc], kvs.at[1 - step, 1 + dc],
            rf_s.at[side(step), 1 + dc], rf_r.at[side(-step), 1 + dc], r_dev(step),
        )

    def z_fwd(h):
        return copy(qdt.at[0, h], qdt.at[1, h], zf_s.at[h], zf_r.at[h], dev(tz, c, r, hd))

    def x_fwd(h):
        return copy(qdt.at[1, h], qdt.at[2, h], xf_s.at[h], xf_r.at[h], dev(tx, c, r, hd))

    def x_bwd(h):
        return copy(xout.at[h], xin.at[h], xb_s.at[h], xb_r.at[h], dev(tx, c, r, hd))

    def z_bwd(h):
        return copy(zout.at[h], zin.at[h], zb_s.at[h], zb_r.at[h], dev(tz, c, r, hd))

    def row_bwd(step, h):
        return copy(
            rowo.at[h, side(step)], rowi.at[h, side(-step)],
            rb_s.at[h, side(step)], rb_r.at[h, side(-step)], r_dev(step),
        )

    def col_bwd(step, h):
        return copy(
            colo.at[h, side(step)], coli.at[h, side(-step)],
            cb_s.at[h, side(step)], cb_r.at[h, side(-step)], c_dev(step),
        )

    def on(condition, action):
        pl.when(condition)(action)

    others = (tz, tx, td)

    def stat_copy(h, n):
        return copy(sto.at[h], sti.at[h, n], st_s.at[h, n], st_r.at[h, n], dev(others[n], c, r, hd))

    STEPS = (-1, 1)

    for h in range(2):
        kvs[1, 1, h, 0] = normed(hk, SPACE + h, kgain)
        kvs[1, 1, h, 1] = raw(hv, SPACE + h)
    pl.semaphore_wait(barrier, G0 - 1 + C - 1 + R - 1)
    for step in STEPS:
        on(c_ok(step), col_fwd(step).start)
    for step in STEPS:
        on(r_ok(step), row_fwd(step, 0).start)
    for h in range(2):
        qdt[0, h, 0] = normed(hq, TIME + h, qgain)
        qdt[0, h, 1] = raw(ho, TIME + h)
        if h == 0:
            z_fwd(0).start()

    nothing = jnp.zeros((2, 2, tile, HD), BF16)
    for step in STEPS:

        def blank_column(step=step):
            for dr in range(3):
                kvs[dr, 1 + step] = nothing

        def blank_row(step=step):
            for dc in range(3):
                kvs[1 + step, dc] = nothing

        on(jnp.logical_not(c_ok(step)), blank_column)
        on(jnp.logical_not(r_ok(step)), blank_row)

    for h in range(2):
        kvl[h, 0] = normed(hk, LOCAL + h, kgain)
        kvl[h, 1] = raw(hv, LOCAL + h)
        kvh[h, 0] = normed(hk, TIME + h, kgain)
        kvh[h, 1] = raw(hv, TIME + h)
        for n, s in ((0, LOCAL + h), (2, SPACE + h)):
            qs[n + h, 0] = normed(hq, s, qgain)
            qs[n + h, 1] = raw(ho, s)
    stats[...] = jnp.zeros_like(stats)
    dqt[...] = jnp.zeros_like(dqt)
    gacc[...] = jnp.zeros_like(gacc)

    def at_time(h, b):
        return 4 + 3 * h + b

    def pass_one(idx, row, qd, kv, count):
        query, up = qd[0], qd[1]
        sum_l, sum_d = stats[row, 0:8], stats[row, 8:16]
        for j in range(0, tile, chunk):
            s = dot(kv[0, j : j + chunk], query, NT)
            p = jnp.where(rows_iota < count - j, jnp.exp2(s * (SCALE * LOG2E)), 0.0)
            dp = dot(kv[1, j : j + chunk], up, NT)
            pp[idx, j : j + chunk] = p
            dd[idx, j : j + chunk] = dp
            sum_l = sum_l + fold(p)
            sum_d = sum_d + fold(p * dp)
        stats[row, 0:8] = sum_l
        stats[row, 8:16] = sum_d

    def put_stats(row, total, dot_total, ok_lanes):
        inv = 1.0 / total
        stats[row, 0:8] = jnp.broadcast_to(jnp.where(ok_lanes, inv, 0.0), (8, tile))
        stats[row, 8:16] = jnp.broadcast_to(dot_total * inv, (8, tile))

    def partial(row):
        total = jnp.sum(stats[row, 0:8], axis=0, keepdims=True)
        return total, jnp.sum(stats[row, 8:16], axis=0, keepdims=True)

    def finish_stats(row):
        put_stats(row, *partial(row), query_ok)

    def pass_two(idx, row, qd, kv, slot, emit):
        query, up = qd[0], qd[1]
        inv, out_dot = stats[row, 0:1], stats[row, 8:9]
        key_sum = gacc[slot]
        dq = dqt[row]
        for j in range(0, tile, chunk):
            w = pp[idx, j : j + chunk] * inv
            g = (w * (dd[idx, j : j + chunk] - out_dot)).astype(BF16)
            keys = kv[0, j : j + chunk]
            dk = dot(g, query, NN)
            dv = dot(w.astype(BF16), up, NN)
            dq = dq + dot(keys, g, TN)
            key_sum = key_sum + fold(dk * keys.astype(F32))
            emit(j, dk, dv)
        gacc[slot] = key_sum
        dqt[row] = dq

    def at_space(h, dr, dc):
        return 10 + 9 * h + 3 * dr + dc

    def space_one(dr, dc):
        count = count_at(t, c + dc - 1, r + dr - 1)
        for h in range(2):
            pass_one(at_space(h, dr, dc), 2 + h, qs.at[2 + h], kvs.at[dr, dc, h], count)

    def space_two(dr, dc, h, emit):
        pass_two(at_space(h, dr, dc), 2 + h, qs.at[2 + h], kvs.at[dr, dc, h], SPACE + h, emit)

    far_count = jnp.where((td - t) * (td - t) == 1, own_count, 0)
    tile_ok = (query_ok, lanes < count_at(tz, c, r), lanes < count_at(td, c, r))

    def time_one(h, b):
        pass_one(at_time(h, b), at_time(h, b), qdt.at[b, h], kvh.at[h], far_count if b == 2 else own_count)

    def time_two(h, b):
        def emit(j, dk, dv):
            if b == 2:
                fk[TIME + h, j : j + chunk] = dk
                fv[TIME + h, j : j + chunk] = dv
            else:
                fk[TIME + h, j : j + chunk] += dk
                fv[TIME + h, j : j + chunk] += dv

        pass_two(at_time(h, b), at_time(h, b), qdt.at[b, h], kvh.at[h], TIME + h, emit)

    def time_partial(h):
        for b in range(3):
            total, dot_total = partial(at_time(h, b))
            sto[h, 2 * b : 2 * b + 1] = total
            sto[h, 2 * b + 1 : 2 * b + 2] = dot_total
        sto[h, 6:8] = jnp.zeros((2, tile), F32)
        for n in range(3):
            stat_copy(h, n).start()

    def time_total(h):
        for n in range(3):
            stat_copy(h, n).wait_recv()
        for b, (n, i), (m, k) in ((0, (0, 2), (2, 4)), (1, (0, 0), (1, 4)), (2, (2, 0), (1, 2))):

            def row(q, b=b, n=n, i=i, m=m, k=k):
                mine = sto[h, 2 * b + q : 2 * b + q + 1]
                return mine + sti[h, n, i + q : i + q + 1] + sti[h, m, k + q : k + q + 1]

            put_stats(at_time(h, b), row(0), row(1), tile_ok[b])

    def time_send_far(h):
        time_two(h, 2)
        xout[h] = dqt[at_time(h, 2)].astype(BF16)
        x_bwd(h).start()

    def time_send_back(h):
        x_bwd(h).wait_recv()
        zout[h] = (dqt[at_time(h, 1)] + xin[h].astype(F32)).astype(BF16)
        z_bwd(h).start()

    def loop(n, body):
        def step(i, carry):
            body(i)
            return carry

        lax.fori_loop(0, n, step, 0)

    def query_out(s, grad_t):
        grad = jnp.transpose(grad_t) * SCALE
        unit, inv = unit_of(raw(hq, s))
        scaled = grad * qgain[...]
        mean = jnp.mean(scaled * unit, axis=1, keepdims=True)
        oq[s] = (inv * (scaled - unit * mean)).astype(BF16)

    def key_out(s):
        grad = fk[s] * SCALE
        unit, inv = unit_of(raw(hk, s))
        scaled = grad * kgain[...]
        mean = jnp.mean(scaled * unit, axis=1, keepdims=True)
        ok[s] = (inv * (scaled - unit * mean)).astype(BF16)
        ov[s] = fv[s].astype(BF16)

    space_one(1, 1)
    for h in range(2):
        pass_one(h, h, qs.at[h], kvl.at[h], own_count)
        finish_stats(h)
    for h in range(2):

        def emit_local(j, dk, dv, h=h):
            fk[LOCAL + h, j : j + chunk] = dk
            fv[LOCAL + h, j : j + chunk] = dv

        pass_two(h, h, qs.at[h], kvl.at[h], LOCAL + h, emit_local)
    for h in range(2):
        time_one(h, 0)

    for dc in STEPS:
        on(c_ok(dc), col_fwd(-dc).wait_recv)
    for dc in STEPS:
        for step in STEPS:
            on(c_ok(dc) & r_ok(step), row_fwd(step, dc).start)
    loop(2, lambda i: space_one(1, 2 * i))
    for dr in STEPS:
        on(r_ok(dr), row_fwd(-dr, 0).wait_recv)
    z_fwd(0).wait_send()
    z_fwd(1).start()
    loop(2, lambda i: space_one(2 * i, 1))

    z_fwd(0).wait_recv()
    x_fwd(0).start()
    time_one(0, 1)
    for dr in STEPS:
        for dc in STEPS:
            on(r_ok(dr) & c_ok(dc), row_fwd(-dr, dc).wait_recv)

    def corner(i):
        dr = lax.div(i, 2)
        space_one(2 * dr, 2 * (i - 2 * dr))

    loop(4, corner)
    x_fwd(0).wait_recv()
    time_one(0, 2)
    time_partial(0)
    for h in range(2):
        finish_stats(2 + h)

    def outer_rows(h):
        def step(i):
            d = lax.div(i, 3)
            dc = i - 3 * d

            def emit(j, dk, dv):
                rowo[h, d, dc, 0, pl.ds(j, chunk)] = dk.astype(BF16)
                rowo[h, d, dc, 1, pl.ds(j, chunk)] = dv.astype(BF16)

            space_two(2 * d, dc, h, emit)

        loop(6, step)
        for step in STEPS:
            on(r_ok(step), row_bwd(step, h).start)

    outer_rows(0)
    time_total(0)
    time_send_far(0)
    time_two(0, 1)
    outer_rows(1)
    time_send_back(0)

    def middle_row(i):
        for h in range(2):

            def emit(j, dk, dv, h=h):
                sacc[i, h, 0, pl.ds(j, chunk)] = dk
                sacc[i, h, 1, pl.ds(j, chunk)] = dv

            space_two(1, i, h, emit)

    loop(3, middle_row)
    time_two(0, 0)
    for h in range(2):
        query_out(LOCAL + h, dqt[h])
        query_out(SPACE + h, dqt[2 + h])
        key_out(LOCAL + h)
    key_out(TIME)

    z_fwd(1).wait_recv()
    x_fwd(1).start()
    time_one(1, 1)
    x_fwd(1).wait_recv()
    time_one(1, 2)
    time_partial(1)

    def rows_back(h):
        for dr in STEPS:

            def add_row(dr=dr):
                row_bwd(-dr, h).wait_recv()
                for dc in range(3):
                    sacc[dc, h] = sacc[dc, h] + rowi[h, side(dr), dc].astype(F32)

            on(r_ok(dr), add_row)
        for step in STEPS:

            def send_column(step=step):
                colo[h, side(step)] = sacc[1 + step, h].astype(BF16)
                col_bwd(step, h).start()

            on(c_ok(step), send_column)

    for h in range(2):
        rows_back(h)

    time_total(1)
    time_send_far(1)
    time_two(1, 1)
    time_two(1, 0)
    time_send_back(1)

    pair_sum = gacc[0]
    for s in range(1, 6):
        pair_sum = pair_sum + gacc[s]

    def gain_copy(n, j):
        _, mine, peer = groups[n]
        return copy(gbuf.at[n, mine], gbuf.at[n, mine], g_s.at[n, j], g_r.at[n, mine], peer(j))

    def gain_send(n, value):
        size, mine, _ = groups[n]
        gbuf[n, mine] = value
        for j in range(1, size):
            gain_copy(n, j).start()

    def gain_sum(n):
        size, mine, peer = groups[n]
        for j in range(1, size):
            other = lax.rem(mine + j, size)
            copy(gbuf.at[n, other], gbuf.at[n, other], g_s.at[n, j], g_r.at[n, other], peer(j)).wait_recv()
        total = gbuf[n, 0]
        for i in range(1, size):
            total = total + gbuf[n, i]
        return total

    gain_send(0, pair_sum)
    key_out(TIME + 1)
    for h in range(2):
        for dc in STEPS:

            def add_column(dc=dc, h=h):
                col_bwd(-dc, h).wait_recv()
                sacc[1, h] = sacc[1, h] + coli[h, side(dc)].astype(F32)

            on(c_ok(dc), add_column)
        fk[SPACE + h] = sacc[1, h, 0]
        fv[SPACE + h] = sacc[1, h, 1]
        key_out(SPACE + h)
        if h == 0:
            gain_send(1, gain_sum(0))
    gain_send(2, gain_sum(1))
    for h in range(2):
        z_bwd(h).wait_recv()
        query_out(TIME + h, dqt[at_time(h, 0)] + zin[h].astype(F32))
    total = jnp.sum(gain_sum(2), axis=0, keepdims=True) * SCALE
    og[...] = jnp.concatenate([total / qgain[...], total / kgain[...]], axis=0)

    z_fwd(1).wait_send()
    for h in range(2):
        x_fwd(h).wait_send()
        x_bwd(h).wait_send()
        z_bwd(h).wait_send()
        for n in range(3):
            stat_copy(h, n).wait_send()
    for step in STEPS:
        on(c_ok(step), col_fwd(step).wait_send)
        on(r_ok(step), row_fwd(step, 0).wait_send)
        for dc in STEPS:
            on(c_ok(dc) & r_ok(step), row_fwd(step, dc).wait_send)
        for h in range(2):
            on(r_ok(step), row_bwd(step, h).wait_send)
            on(c_ok(step), col_bwd(step, h).wait_send)
    for n, (size, _, _) in enumerate(groups):
        for j in range(1, size):
            gain_copy(n, j).wait_send()


def hand_over(we, q, k, v, gains, oq, ok, ov, og):
    kinds = [we[0, h] + 2 * we[1, h] for h in range(6)]
    for h in range(6):
        slot = 2 * kinds[h]
        for g in range(h):
            slot = slot + jnp.where(kinds[g] == kinds[h], 1, 0)
        for src, dst in ((q, oq), (k, ok), (v, ov)):
            dst[:, h * HD : (h + 1) * HD] = src[slot]
    og[...] = gains[...]


def on_device(T, C, R, H, query_raw, key_raw, values, out_grad, query_gain, key_gain, window_extent, tile_counts):
    tile, width = query_raw.shape[2], query_raw.shape[3]
    chunk = min(128, tile)
    flat = lambda x: x.reshape(tile, width)
    most = max(T * H, C, R)
    dma = pltpu.SemaphoreType.DMA
    vmem = pl.BlockSpec(memory_space=pltpu.VMEM)
    smem = pl.BlockSpec(memory_space=pltpu.SMEM)
    heads = lambda n: pltpu.VMEM((n, tile, HD), BF16)
    pairs = lambda *n: pltpu.VMEM(n + (2, tile, HD), BF16)
    scratch = [
        heads(6), heads(6), heads(6), heads(6),
        pairs(4), pairs(2), pairs(2), pairs(3, 2), pairs(3, 3, 2),
        pltpu.VMEM((28, tile, tile), F32),
        pltpu.VMEM((28, tile, tile), F32),
        pltpu.VMEM((10, 16, tile), F32),
        pltpu.VMEM((2, 8, tile), F32),
        pltpu.VMEM((2, 3, 8, tile), F32),
        pltpu.VMEM((10, HD, tile), F32),
        pltpu.VMEM((6, tile, HD), F32),
        pltpu.VMEM((6, tile, HD), F32),
        pltpu.VMEM((2, HD, tile), BF16),
        pltpu.VMEM((2, HD, tile), BF16),
        pltpu.VMEM((2, HD, tile), BF16),
        pltpu.VMEM((2, HD, tile), BF16),
        pltpu.VMEM((3, 2, 2, tile, HD), F32),
        pairs(2, 2, 3), pairs(2, 2, 3), pairs(2, 2), pairs(2, 2),
        pltpu.VMEM((6, 8, HD), F32),
        pltpu.VMEM((3, most, 8, HD), F32),
        dma((2,)), dma((2,)), dma((2,)), dma((2,)),
        dma((2,)), dma((2,)), dma((2, 3)), dma((2, 3)),
        dma((2,)), dma((2,)), dma((2,)), dma((2,)),
        dma((2, 2)), dma((2, 2)), dma((2, 2)), dma((2, 2)),
        dma((2, 3)), dma((2, 3)),
        dma((3, most)), dma((3, most)),
    ]
    wide = jax.ShapeDtypeStruct((6, tile, HD), BF16)
    extent = window_extent.T
    grad_q, grad_k, grad_v, gains = pl.pallas_call(
        functools.partial(kernel, T, C, R, H, tile, chunk),
        out_shape=(wide, wide, wide, jax.ShapeDtypeStruct((2, HD), F32)),
        in_specs=[smem, smem] + [vmem] * 6,
        out_specs=(vmem,) * 4,
        scratch_shapes=scratch,
        compiler_params=pltpu.CompilerParams(
            collective_id=0, has_side_effects=True, vmem_limit_bytes=60 * 1024 * 1024
        ),
    )(
        extent,
        tile_counts,
        query_gain.reshape(1, HD),
        key_gain.reshape(1, HD),
        flat(query_raw),
        flat(key_raw),
        flat(values),
        flat(out_grad),
    )
    whole = jax.ShapeDtypeStruct((tile, width), BF16)
    outs = pl.pallas_call(
        hand_over,
        out_shape=(whole, whole, whole, jax.ShapeDtypeStruct((2, HD), F32)),
        in_specs=[smem] + [vmem] * 4,
        out_specs=(vmem,) * 4,
        compiler_params=pltpu.CompilerParams(vmem_limit_bytes=60 * 1024 * 1024),
    )(extent, grad_q, grad_k, grad_v, gains)
    shape = (1, 1, tile, width)
    return tuple(x.reshape(shape) for x in outs[:3]) + (outs[3],)


def solution(mesh):
    tile_spec = P("tm", "space", None, "head")

    def program(*args):
        T = args[7].shape[0]
        C = mesh.shape["tm"] // T
        return on_device(T, C, mesh.shape["space"], mesh.shape["head"], *args)

    return jax.shard_map(
        program,
        mesh=mesh,
        in_specs=(tile_spec,) * 4 + (P(), P(), P("head", None), P()),
        out_specs=(tile_spec,) * 3 + (P(),),
        check_vma=False,
    )
```

```python
import functools

import jax
import jax.numpy as jnp
from jax import lax
from jax.experimental import pallas as pl
from jax.experimental.pallas import tpu as pltpu
from jax.sharding import PartitionSpec as P

MESH = pl.DeviceIdType.MESH
HD = 128
F32 = jnp.float32
BF16 = jnp.bfloat16
SCALE = HD**-0.5
LOG2E = 1.4426950408889634
NT = (((1,), (1,)), ((), ()))
NN = (((1,), (0,)), ((), ()))
TN = (((0,), (0,)), ((), ()))

LOCAL, TIME, SPACE = 0, 2, 4


def dot(a, b, dims):
    return lax.dot_general(a, b, dims, preferred_element_type=F32)


def unit_of(raw):
    x = raw.astype(F32)
    inv = lax.rsqrt(jnp.mean(x * x, axis=1, keepdims=True) + 1e-6)
    return x * inv, inv


def fold(x):
    return jnp.sum(x.reshape(x.shape[0] // 8, 8, x.shape[1]), axis=0)


def kernel(
    T, C, R, H, tile, chunk,
    we, counts, qgain, kgain, qraw, kraw, vals, ograd,
    oq, ok, ov, og,
    hq, hk, hv, ho, qs, kvl, kvh, qdt, kvs, pp, dd, stats, sto, sti, dqt, fk, fv,
    xout, xin, zout, zin, rly, rlb, sacc, rowo, rowi, colo, coli, gacc, gbuf,
    z1_s, z1_r, z2_s, z2_r, xf_s, xf_r, cf_s, cf_r, rf_s, rf_r,
    y1_s, y1_r, y2_s, y2_r, xb_s, xb_r, cb_s, cb_r, rb_s, rb_r, st_s, st_r, g_s, g_r,
):
    tm = lax.axis_index("tm")
    r = lax.axis_index("space")
    hd = lax.axis_index("head")
    t = lax.div(tm, C)
    c = lax.rem(tm, C)
    tz = t + 1 - 2 * lax.rem(t, 2)
    tx = lax.rem(t + 2, T)
    td = lax.rem(tz + 2, T)

    def dev(t_, c_, r_, h_):
        return (t_ * C + c_, r_, h_)

    G0 = T * H
    gi = t * H + hd

    def peer0(j):
        g = lax.rem(gi + j, G0)
        return dev(lax.div(g, H), c, r, lax.rem(g, H))

    def peer1(j):
        return dev(t, lax.rem(c + j, C), r, hd)

    def peer2(j):
        return dev(t, c, lax.rem(r + j, R), hd)

    groups = ((G0, gi, peer0), (C, c, peer1), (R, r, peer2))
    near_half, far_half = C // 2, C - C // 2

    def ring(offset):
        place = lax.rem(lax.rem(t, 2) * C + c + offset + 2 * C, 2 * C)
        return (lax.div(t, 2) * (2 * C) + place, r, hd)

    relays = sorted({near_half, -near_half, far_half, -far_half})
    barrier = pltpu.get_barrier_semaphore()
    for offset in relays:
        pl.semaphore_signal(barrier, inc=1, device_id=ring(offset), device_id_type=MESH)
    for size, _, peer in groups:
        for j in range(1, size):
            pl.semaphore_signal(barrier, inc=1, device_id=peer(j), device_id_type=MESH)

    kinds = [we[0, h] + 2 * we[1, h] for h in range(6)]
    head_of = []
    for kind in range(3):
        low, high = jnp.int32(5), jnp.int32(0)
        for h in range(6):
            low = jnp.minimum(low, jnp.where(kinds[h] == kind, h, 5))
            high = jnp.maximum(high, jnp.where(kinds[h] == kind, h, 0))
        head_of += [low, high]
    for by_head, whole in ((hk, kraw), (hv, vals), (hq, qraw), (ho, ograd)):
        for h in range(6):
            by_head[h] = whole[:, h * HD : (h + 1) * HD]

    def raw(ref, slot):
        return ref[head_of[slot]]

    def normed(ref, slot, gain):
        unit, _ = unit_of(raw(ref, slot))
        return (unit * gain[...]).astype(BF16)

    def count_at(t_, c_, r_):
        inside = (c_ >= 0) & (c_ < C) & (r_ >= 0) & (r_ < R)
        got = counts[t_, lax.rem(c_ + C, C), lax.rem(r_ + R, R)]
        return jnp.where(inside, got, 0)

    own_count = count_at(t, c, r)
    lanes = lax.broadcasted_iota(jnp.int32, (1, tile), 1)
    query_ok = lanes < own_count
    rows_iota = lax.broadcasted_iota(jnp.int32, (chunk, tile), 0)

    def side(step):
        return (step + 1) // 2

    def c_ok(step):
        return (c + step >= 0) & (c + step < C)

    def r_ok(step):
        return (r + step >= 0) & (r + step < R)

    def c_dev(step):
        return dev(t, lax.rem(c + step + C, C), r, hd)

    def r_dev(step):
        return dev(t, c, lax.rem(r + step + R, R), hd)

    def copy(src, dst, send, recv, where):
        return pltpu.make_async_remote_copy(
            src_ref=src, dst_ref=dst, send_sem=send, recv_sem=recv, device_id=where, device_id_type=MESH
        )

    def col_fwd(step):
        return copy(kvs.at[1, 1], kvs.at[1, 1 - step], cf_s.at[side(step)], cf_r.at[side(-step)], c_dev(step))

    def row_fwd(step, dc):
        return copy(
            kvs.at[1, 1 + dc], kvs.at[1 - step, 1 + dc],
            rf_s.at[side(step), 1 + dc], rf_r.at[side(-step), 1 + dc], r_dev(step),
        )

    def z_first(h, n):
        return copy(qdt.at[0, h, n], rly.at[h, n], z1_s.at[h, n], z1_r.at[h, n], ring((1 - 2 * n) * near_half))

    def z_second(h, n):
        return copy(rly.at[h, n], qdt.at[1, h, n], z2_s.at[h, n], z2_r.at[h, n], ring((1 - 2 * n) * far_half))

    def back_first(h, n):
        return copy(zout.at[h, n], rlb.at[h, n], y1_s.at[h, n], y1_r.at[h, n], ring((1 - 2 * n) * near_half))

    def back_second(h, n):
        return copy(rlb.at[h, n], zin.at[h, n], y2_s.at[h, n], y2_r.at[h, n], ring((1 - 2 * n) * far_half))

    def begin(hop, h):
        for n in range(2):
            hop(h, n).start()

    def arrived(hop, h):
        for n in range(2):
            hop(h, n).wait_recv()

    def relay(first, second, h):
        for n in range(2):
            first(h, n).wait_recv()
            second(h, n).start()

    def x_fwd(h):
        return copy(qdt.at[1, h], qdt.at[2, h], xf_s.at[h], xf_r.at[h], dev(tx, c, r, hd))

    def x_bwd(h):
        return copy(xout.at[h], xin.at[h], xb_s.at[h], xb_r.at[h], dev(tx, c, r, hd))

    def row_bwd(step, h):
        return copy(
            rowo.at[h, side(step)], rowi.at[h, side(-step)],
            rb_s.at[h, side(step)], rb_r.at[h, side(-step)], r_dev(step),
        )

    def col_bwd(step, h):
        return copy(
            colo.at[h, side(step)], coli.at[h, side(-step)],
            cb_s.at[h, side(step)], cb_r.at[h, side(-step)], c_dev(step),
        )

    def on(condition, action):
        pl.when(condition)(action)

    others = (tz, tx, td)

    def stat_copy(h, n):
        return copy(sto.at[h], sti.at[h, n], st_s.at[h, n], st_r.at[h, n], dev(others[n], c, r, hd))

    STEPS = (-1, 1)

    for h in range(2):
        kvs[1, 1, h, 0] = normed(hk, SPACE + h, kgain)
        kvs[1, 1, h, 1] = raw(hv, SPACE + h)
    pl.semaphore_wait(barrier, len(relays) + G0 - 1 + C - 1 + R - 1)
    for step in STEPS:
        on(c_ok(step), col_fwd(step).start)
    for step in STEPS:
        on(r_ok(step), row_fwd(step, 0).start)
    for h in range(2):
        qdt[0, h, 0] = normed(hq, TIME + h, qgain)
        qdt[0, h, 1] = raw(ho, TIME + h)
        if h == 0:
            begin(z_first, 0)

    nothing = jnp.zeros((2, 2, tile, HD), BF16)
    for step in STEPS:

        def blank_column(step=step):
            for dr in range(3):
                kvs[dr, 1 + step] = nothing

        def blank_row(step=step):
            for dc in range(3):
                kvs[1 + step, dc] = nothing

        on(jnp.logical_not(c_ok(step)), blank_column)
        on(jnp.logical_not(r_ok(step)), blank_row)

    for h in range(2):
        kvl[h, 0] = normed(hk, LOCAL + h, kgain)
        kvl[h, 1] = raw(hv, LOCAL + h)
        kvh[h, 0] = normed(hk, TIME + h, kgain)
        kvh[h, 1] = raw(hv, TIME + h)
        for n, s in ((0, LOCAL + h), (2, SPACE + h)):
            qs[n + h, 0] = normed(hq, s, qgain)
            qs[n + h, 1] = raw(ho, s)
    stats[...] = jnp.zeros_like(stats)
    dqt[...] = jnp.zeros_like(dqt)
    gacc[...] = jnp.zeros_like(gacc)

    def at_time(h, b):
        return 4 + 3 * h + b

    def pass_one(idx, row, qd, kv, count):
        query, up = qd[0], qd[1]
        sum_l, sum_d = stats[row, 0:8], stats[row, 8:16]
        for j in range(0, tile, chunk):
            s = dot(kv[0, j : j + chunk], query, NT)
            p = jnp.where(rows_iota < count - j, jnp.exp2(s * (SCALE * LOG2E)), 0.0)
            dp = dot(kv[1, j : j + chunk], up, NT)
            pp[idx, j : j + chunk] = p
            dd[idx, j : j + chunk] = dp
            sum_l = sum_l + fold(p)
            sum_d = sum_d + fold(p * dp)
        stats[row, 0:8] = sum_l
        stats[row, 8:16] = sum_d

    def put_stats(row, total, dot_total, ok_lanes):
        inv = 1.0 / total
        stats[row, 0:8] = jnp.broadcast_to(jnp.where(ok_lanes, inv, 0.0), (8, tile))
        stats[row, 8:16] = jnp.broadcast_to(dot_total * inv, (8, tile))

    def partial(row):
        total = jnp.sum(stats[row, 0:8], axis=0, keepdims=True)
        return total, jnp.sum(stats[row, 8:16], axis=0, keepdims=True)

    def finish_stats(row):
        put_stats(row, *partial(row), query_ok)

    def pass_two(idx, row, qd, kv, slot, emit):
        query, up = qd[0], qd[1]
        inv, out_dot = stats[row, 0:1], stats[row, 8:9]
        key_sum = gacc[slot]
        dq = dqt[row]
        for j in range(0, tile, chunk):
            w = pp[idx, j : j + chunk] * inv
            g = (w * (dd[idx, j : j + chunk] - out_dot)).astype(BF16)
            keys = kv[0, j : j + chunk]
            dk = dot(g, query, NN)
            dv = dot(w.astype(BF16), up, NN)
            dq = dq + dot(keys, g, TN)
            key_sum = key_sum + fold(dk * keys.astype(F32))
            emit(j, dk, dv)
        gacc[slot] = key_sum
        dqt[row] = dq

    def at_space(h, dr, dc):
        return 10 + 9 * h + 3 * dr + dc

    def space_one(dr, dc):
        count = count_at(t, c + dc - 1, r + dr - 1)
        for h in range(2):
            pass_one(at_space(h, dr, dc), 2 + h, qs.at[2 + h], kvs.at[dr, dc, h], count)

    def space_two(dr, dc, h, emit):
        pass_two(at_space(h, dr, dc), 2 + h, qs.at[2 + h], kvs.at[dr, dc, h], SPACE + h, emit)

    far_count = jnp.where((td - t) * (td - t) == 1, own_count, 0)
    tile_ok = (query_ok, lanes < count_at(tz, c, r), lanes < count_at(td, c, r))

    def time_one(h, b):
        pass_one(at_time(h, b), at_time(h, b), qdt.at[b, h], kvh.at[h], far_count if b == 2 else own_count)

    def time_two(h, b):
        def emit(j, dk, dv):
            if b == 2:
                fk[TIME + h, j : j + chunk] = dk
                fv[TIME + h, j : j + chunk] = dv
            else:
                fk[TIME + h, j : j + chunk] += dk
                fv[TIME + h, j : j + chunk] += dv

        pass_two(at_time(h, b), at_time(h, b), qdt.at[b, h], kvh.at[h], TIME + h, emit)

    def time_partial(h):
        for b in range(3):
            total, dot_total = partial(at_time(h, b))
            sto[h, 2 * b : 2 * b + 1] = total
            sto[h, 2 * b + 1 : 2 * b + 2] = dot_total
        sto[h, 6:8] = jnp.zeros((2, tile), F32)
        for n in range(3):
            stat_copy(h, n).start()

    def time_total(h):
        for n in range(3):
            stat_copy(h, n).wait_recv()
        for b, (n, i), (m, k) in ((0, (0, 2), (2, 4)), (1, (0, 0), (1, 4)), (2, (2, 0), (1, 2))):

            def row(q, b=b, n=n, i=i, m=m, k=k):
                mine = sto[h, 2 * b + q : 2 * b + q + 1]
                return mine + sti[h, n, i + q : i + q + 1] + sti[h, m, k + q : k + q + 1]

            put_stats(at_time(h, b), row(0), row(1), tile_ok[b])

    def time_send_far(h):
        time_two(h, 2)
        xout[h] = dqt[at_time(h, 2)].astype(BF16)
        x_bwd(h).start()

    def time_send_back(h):
        x_bwd(h).wait_recv()
        back = (dqt[at_time(h, 1)] + xin[h].astype(F32)).astype(BF16)
        for n in range(2):
            zout[h, n] = back[n * (HD // 2) : (n + 1) * (HD // 2)]
        begin(back_first, h)

    def loop(n, body):
        def step(i, carry):
            body(i)
            return carry

        lax.fori_loop(0, n, step, 0)

    def query_out(s, grad_t):
        grad = jnp.transpose(grad_t) * SCALE
        unit, inv = unit_of(raw(hq, s))
        scaled = grad * qgain[...]
        mean = jnp.mean(scaled * unit, axis=1, keepdims=True)
        oq[s] = (inv * (scaled - unit * mean)).astype(BF16)

    def key_out(s):
        grad = fk[s] * SCALE
        unit, inv = unit_of(raw(hk, s))
        scaled = grad * kgain[...]
        mean = jnp.mean(scaled * unit, axis=1, keepdims=True)
        ok[s] = (inv * (scaled - unit * mean)).astype(BF16)
        ov[s] = fv[s].astype(BF16)

    space_one(1, 1)
    for h in range(2):
        pass_one(h, h, qs.at[h], kvl.at[h], own_count)
        finish_stats(h)
    relay(z_first, z_second, 0)
    begin(z_first, 1)
    for h in range(2):

        def emit_local(j, dk, dv, h=h):
            fk[LOCAL + h, j : j + chunk] = dk
            fv[LOCAL + h, j : j + chunk] = dv

        pass_two(h, h, qs.at[h], kvl.at[h], LOCAL + h, emit_local)
    for h in range(2):
        time_one(h, 0)

    for dc in STEPS:
        on(c_ok(dc), col_fwd(-dc).wait_recv)
    for dc in STEPS:
        for step in STEPS:
            on(c_ok(dc) & r_ok(step), row_fwd(step, dc).start)
    loop(2, lambda i: space_one(1, 2 * i))
    for dr in STEPS:
        on(r_ok(dr), row_fwd(-dr, 0).wait_recv)
    loop(2, lambda i: space_one(2 * i, 1))
    relay(z_first, z_second, 1)

    arrived(z_second, 0)
    x_fwd(0).start()
    time_one(0, 1)
    for dr in STEPS:
        for dc in STEPS:
            on(r_ok(dr) & c_ok(dc), row_fwd(-dr, dc).wait_recv)

    def corner(i):
        dr = lax.div(i, 2)
        space_one(2 * dr, 2 * (i - 2 * dr))

    loop(4, corner)
    x_fwd(0).wait_recv()
    time_one(0, 2)
    time_partial(0)
    for h in range(2):
        finish_stats(2 + h)

    def outer_rows(h):
        def step(i):
            d = lax.div(i, 3)
            dc = i - 3 * d

            def emit(j, dk, dv):
                rowo[h, d, dc, 0, pl.ds(j, chunk)] = dk.astype(BF16)
                rowo[h, d, dc, 1, pl.ds(j, chunk)] = dv.astype(BF16)

            space_two(2 * d, dc, h, emit)

        loop(6, step)
        for step in STEPS:
            on(r_ok(step), row_bwd(step, h).start)

    outer_rows(0)
    time_total(0)
    time_send_far(0)
    time_two(0, 1)

    arrived(z_second, 1)
    x_fwd(1).start()
    time_one(1, 1)
    time_send_back(0)
    outer_rows(1)
    x_fwd(1).wait_recv()
    time_one(1, 2)
    time_partial(1)

    def middle_row(i):
        for h in range(2):

            def emit(j, dk, dv, h=h):
                sacc[i, h, 0, pl.ds(j, chunk)] = dk
                sacc[i, h, 1, pl.ds(j, chunk)] = dv

            space_two(1, i, h, emit)

    loop(3, middle_row)
    time_two(0, 0)
    relay(back_first, back_second, 0)
    time_total(1)
    time_send_far(1)
    time_two(1, 1)
    time_send_back(1)

    def rows_back(h):
        for dr in STEPS:

            def add_row(dr=dr):
                row_bwd(-dr, h).wait_recv()
                for dc in range(3):
                    sacc[dc, h] = sacc[dc, h] + rowi[h, side(dr), dc].astype(F32)

            on(r_ok(dr), add_row)
        for step in STEPS:

            def send_column(step=step):
                colo[h, side(step)] = sacc[1 + step, h].astype(BF16)
                col_bwd(step, h).start()

            on(c_ok(step), send_column)

    for h in range(2):
        rows_back(h)

    time_two(1, 0)

    pair_sum = gacc[0]
    for s in range(1, 6):
        pair_sum = pair_sum + gacc[s]

    def gain_copy(n, j):
        _, mine, peer = groups[n]
        return copy(gbuf.at[n, mine], gbuf.at[n, mine], g_s.at[n, j], g_r.at[n, mine], peer(j))

    def gain_send(n, value):
        size, mine, _ = groups[n]
        gbuf[n, mine] = value
        for j in range(1, size):
            gain_copy(n, j).start()

    def gain_sum(n):
        size, mine, peer = groups[n]
        for j in range(1, size):
            other = lax.rem(mine + j, size)
            copy(gbuf.at[n, other], gbuf.at[n, other], g_s.at[n, j], g_r.at[n, other], peer(j)).wait_recv()
        total = gbuf[n, 0]
        for i in range(1, size):
            total = total + gbuf[n, i]
        return total

    gain_send(0, pair_sum)
    for h in range(2):
        query_out(LOCAL + h, dqt[h])
        query_out(SPACE + h, dqt[2 + h])
        key_out(LOCAL + h)
    relay(back_first, back_second, 1)
    for h in range(2):
        key_out(TIME + h)
    for h in range(2):
        for dc in STEPS:

            def add_column(dc=dc, h=h):
                col_bwd(-dc, h).wait_recv()
                sacc[1, h] = sacc[1, h] + coli[h, side(dc)].astype(F32)

            on(c_ok(dc), add_column)
        fk[SPACE + h] = sacc[1, h, 0]
        fv[SPACE + h] = sacc[1, h, 1]
        key_out(SPACE + h)
        if h == 0:
            gain_send(1, gain_sum(0))
    gain_send(2, gain_sum(1))
    for h in range(2):
        arrived(back_second, h)
        query_out(TIME + h, dqt[at_time(h, 0)] + jnp.concatenate([zin[h, 0], zin[h, 1]], axis=0).astype(F32))
    total = jnp.sum(gain_sum(2), axis=0, keepdims=True) * SCALE
    og[...] = jnp.concatenate([total / qgain[...], total / kgain[...]], axis=0)

    for h in range(2):
        x_fwd(h).wait_send()
        x_bwd(h).wait_send()
        for hop in (z_first, z_second, back_first, back_second):
            for n in range(2):
                hop(h, n).wait_send()
        for n in range(3):
            stat_copy(h, n).wait_send()
    for step in STEPS:
        on(c_ok(step), col_fwd(step).wait_send)
        on(r_ok(step), row_fwd(step, 0).wait_send)
        for dc in STEPS:
            on(c_ok(dc) & r_ok(step), row_fwd(step, dc).wait_send)
        for h in range(2):
            on(r_ok(step), row_bwd(step, h).wait_send)
            on(c_ok(step), col_bwd(step, h).wait_send)
    for n, (size, _, _) in enumerate(groups):
        for j in range(1, size):
            gain_copy(n, j).wait_send()


def hand_over(we, q, k, v, gains, oq, ok, ov, og):
    kinds = [we[0, h] + 2 * we[1, h] for h in range(6)]
    for h in range(6):
        slot = 2 * kinds[h]
        for g in range(h):
            slot = slot + jnp.where(kinds[g] == kinds[h], 1, 0)
        for src, dst in ((q, oq), (k, ok), (v, ov)):
            dst[:, h * HD : (h + 1) * HD] = src[slot]
    og[...] = gains[...]


def on_device(T, C, R, H, query_raw, key_raw, values, out_grad, query_gain, key_gain, window_extent, tile_counts):
    tile, width = query_raw.shape[2], query_raw.shape[3]
    chunk = min(128, tile)
    flat = lambda x: x.reshape(tile, width)
    most = max(T * H, C, R)
    dma = pltpu.SemaphoreType.DMA
    vmem = pl.BlockSpec(memory_space=pltpu.VMEM)
    smem = pl.BlockSpec(memory_space=pltpu.SMEM)
    heads = lambda n: pltpu.VMEM((n, tile, HD), BF16)
    pairs = lambda *n: pltpu.VMEM(n + (2, tile, HD), BF16)
    scratch = [
        heads(6), heads(6), heads(6), heads(6),
        pairs(4), pairs(2), pairs(2), pairs(3, 2), pairs(3, 3, 2),
        pltpu.VMEM((28, tile, tile), F32),
        pltpu.VMEM((28, tile, tile), F32),
        pltpu.VMEM((10, 16, tile), F32),
        pltpu.VMEM((2, 8, tile), F32),
        pltpu.VMEM((2, 3, 8, tile), F32),
        pltpu.VMEM((10, HD, tile), F32),
        pltpu.VMEM((6, tile, HD), F32),
        pltpu.VMEM((6, tile, HD), F32),
        pltpu.VMEM((2, HD, tile), BF16),
        pltpu.VMEM((2, HD, tile), BF16),
        pltpu.VMEM((2, 2, HD // 2, tile), BF16),
        pltpu.VMEM((2, 2, HD // 2, tile), BF16),
        pairs(2),
        pltpu.VMEM((2, 2, HD // 2, tile), BF16),
        pltpu.VMEM((3, 2, 2, tile, HD), F32),
        pairs(2, 2, 3), pairs(2, 2, 3), pairs(2, 2), pairs(2, 2),
        pltpu.VMEM((6, 8, HD), F32),
        pltpu.VMEM((3, most, 8, HD), F32),
        dma((2, 2)), dma((2, 2)), dma((2, 2)), dma((2, 2)), dma((2,)), dma((2,)),
        dma((2,)), dma((2,)), dma((2, 3)), dma((2, 3)),
        dma((2, 2)), dma((2, 2)), dma((2, 2)), dma((2, 2)), dma((2,)), dma((2,)),
        dma((2, 2)), dma((2, 2)), dma((2, 2)), dma((2, 2)),
        dma((2, 3)), dma((2, 3)),
        dma((3, most)), dma((3, most)),
    ]
    wide = jax.ShapeDtypeStruct((6, tile, HD), BF16)
    extent = window_extent.T
    grad_q, grad_k, grad_v, gains = pl.pallas_call(
        functools.partial(kernel, T, C, R, H, tile, chunk),
        out_shape=(wide, wide, wide, jax.ShapeDtypeStruct((2, HD), F32)),
        in_specs=[smem, smem] + [vmem] * 6,
        out_specs=(vmem,) * 4,
        scratch_shapes=scratch,
        compiler_params=pltpu.CompilerParams(
            collective_id=0, has_side_effects=True, vmem_limit_bytes=60 * 1024 * 1024
        ),
    )(
        extent,
        tile_counts,
        query_gain.reshape(1, HD),
        key_gain.reshape(1, HD),
        flat(query_raw),
        flat(key_raw),
        flat(values),
        flat(out_grad),
    )
    whole = jax.ShapeDtypeStruct((tile, width), BF16)
    outs = pl.pallas_call(
        hand_over,
        out_shape=(whole, whole, whole, jax.ShapeDtypeStruct((2, HD), F32)),
        in_specs=[smem] + [vmem] * 4,
        out_specs=(vmem,) * 4,
        compiler_params=pltpu.CompilerParams(vmem_limit_bytes=60 * 1024 * 1024),
    )(extent, grad_q, grad_k, grad_v, gains)
    shape = (1, 1, tile, width)
    return tuple(x.reshape(shape) for x in outs[:3]) + (outs[3],)


def solution(mesh):
    tile_spec = P("tm", "space", None, "head")

    def program(*args):
        T = args[7].shape[0]
        C = mesh.shape["tm"] // T
        return on_device(T, C, mesh.shape["space"], mesh.shape["head"], *args)

    return jax.shard_map(
        program,
        mesh=mesh,
        in_specs=(tile_spec,) * 4 + (P(), P(), P("head", None), P()),
        out_specs=(tile_spec,) * 3 + (P(),),
        check_vma=False,
    )
```

```python
import functools

import jax
import jax.numpy as jnp
from jax import lax
from jax.experimental import pallas as pl
from jax.experimental.pallas import tpu as pltpu
from jax.sharding import PartitionSpec as P

MESH = pl.DeviceIdType.MESH
HD = 128
F32 = jnp.float32
BF16 = jnp.bfloat16
SCALE = HD**-0.5
LOG2E = 1.4426950408889634
NT = (((1,), (1,)), ((), ()))
NN = (((1,), (0,)), ((), ()))
TN = (((0,), (0,)), ((), ()))

TIME, SPACE = 2, 4


def dot(a, b, dims):
    return lax.dot_general(a, b, dims, preferred_element_type=F32)


def unit_of(raw):
    x = raw.astype(F32)
    inv = lax.rsqrt(jnp.mean(x * x, axis=1, keepdims=True) + 1e-6)
    return x * inv, inv


def fold(x):
    return jnp.sum(x.reshape(x.shape[0] // 8, 8, x.shape[1]), axis=0)


def kernel(
    T, C, R, H, tile, chunk,
    we, counts, qgain, kgain, qraw, kraw, vals, ograd,
    oq, ok, ov, og,
    hq, hk, hv, ho, qd, kv, pp, dd, stats, sto, sti, dqt, fk, fv,
    xout, xin, zout, zin, rowo, rowi, colo, coli, gacc, gbuf,
    zf_s, zf_r, xf_s, xf_r, cf_s, cf_r, rf_s, rf_r,
    zb_s, zb_r, xb_s, xb_r, cb_s, cb_r, rb_s, rb_r, st_s, st_r, g_s, g_r,
):
    tm = lax.axis_index("tm")
    r = lax.axis_index("space")
    hd = lax.axis_index("head")
    t = lax.div(tm, C)
    c = lax.rem(tm, C)
    tz = t + 1 - 2 * lax.rem(t, 2)
    tx = lax.rem(t + 2, T)
    td = lax.rem(tz + 2, T)

    def dev(t_, c_, r_, h_):
        return (t_ * C + c_, r_, h_)

    def loop(n, body):
        def step(i, carry):
            body(i)
            return carry

        lax.fori_loop(0, n, step, 0)

    def on(condition, action):
        pl.when(condition)(action)

    G0 = T * H
    gi = t * H + hd

    def peer0(j):
        g = lax.rem(gi + j, G0)
        return dev(lax.div(g, H), c, r, lax.rem(g, H))

    def peer1(j):
        return dev(t, lax.rem(c + j, C), r, hd)

    def peer2(j):
        return dev(t, c, lax.rem(r + j, R), hd)

    groups = ((G0, gi, peer0), (C, c, peer1), (R, r, peer2))
    barrier = pltpu.get_barrier_semaphore()
    for size, _, peer in groups:

        def greet(j, peer=peer):
            pl.semaphore_signal(barrier, inc=1, device_id=peer(j + 1), device_id_type=MESH)

        loop(size - 1, greet)

    kinds = [we[0, h] + 2 * we[1, h] for h in range(6)]
    head_of = []
    for kind in range(3):
        low, high = jnp.int32(5), jnp.int32(0)
        for h in range(6):
            low = jnp.minimum(low, jnp.where(kinds[h] == kind, h, 5))
            high = jnp.maximum(high, jnp.where(kinds[h] == kind, h, 0))
        head_of += [low, high]

    def split(h):
        cut = pl.ds(pl.multiple_of(h * HD, HD), HD)
        for by_head, whole in ((hk, kraw), (hv, vals), (hq, qraw), (ho, ograd)):
            by_head[h] = whole[:, cut]

    loop(6, split)

    def raw(ref, slot):
        at = head_of[0]
        for s in range(1, 6):
            at = jnp.where(slot == s, head_of[s], at)
        return ref[at]

    def normed(x, gain):
        unit, _ = unit_of(x)
        return (unit * gain[...]).astype(BF16)

    def count_at(t_, c_, r_):
        inside = (c_ >= 0) & (c_ < C) & (r_ >= 0) & (r_ < R)
        got = counts[t_, lax.rem(c_ + C, C), lax.rem(r_ + R, R)]
        return jnp.where(inside, got, 0)

    own_count = count_at(t, c, r)
    lanes = lax.broadcasted_iota(jnp.int32, (1, tile), 1)
    query_ok = lanes < own_count
    rows_iota = lax.broadcasted_iota(jnp.int32, (chunk, tile), 0)

    def time_row(h, b):
        return 4 + 3 * h + b

    def kv_pair(p):
        return kv.at[pl.ds(4 + 2 * p, 2)]

    def side(step):
        return (step + 1) // 2

    def c_ok(step):
        return (c + step >= 0) & (c + step < C)

    def r_ok(step):
        return (r + step >= 0) & (r + step < R)

    def c_dev(step):
        return dev(t, lax.rem(c + step + C, C), r, hd)

    def r_dev(step):
        return dev(t, c, lax.rem(r + step + R, R), hd)

    def copy(src, dst, send, recv, where):
        return pltpu.make_async_remote_copy(
            src_ref=src, dst_ref=dst, send_sem=send, recv_sem=recv, device_id=where, device_id_type=MESH
        )

    def col_fwd(step):
        return copy(kv_pair(4), kv_pair(4 - step), cf_s.at[side(step)], cf_r.at[side(-step)], c_dev(step))

    def row_fwd(step, dc):
        return copy(
            kv_pair(4 + dc), kv_pair(4 + dc - 3 * step),
            rf_s.at[side(step), 1 + dc], rf_r.at[side(-step), 1 + dc], r_dev(step),
        )

    def z_fwd(h):
        return copy(qd.at[4 + 3 * h], qd.at[5 + 3 * h], zf_s.at[h], zf_r.at[h], dev(tz, c, r, hd))

    def x_fwd(h):
        return copy(qd.at[5 + 3 * h], qd.at[6 + 3 * h], xf_s.at[h], xf_r.at[h], dev(tx, c, r, hd))

    def x_bwd(h):
        return copy(xout.at[h], xin.at[h], xb_s.at[h], xb_r.at[h], dev(tx, c, r, hd))

    def z_bwd(h):
        return copy(zout.at[h], zin.at[h], zb_s.at[h], zb_r.at[h], dev(tz, c, r, hd))

    def row_bwd(step, h):
        return copy(
            rowo.at[h, side(step)], rowi.at[h, side(-step)],
            rb_s.at[h, side(step)], rb_r.at[h, side(-step)], r_dev(step),
        )

    def col_bwd(step, h):
        return copy(
            colo.at[h, side(step)], coli.at[h, side(-step)],
            cb_s.at[h, side(step)], cb_r.at[h, side(-step)], c_dev(step),
        )

    others = (tz, tx, td)

    def stat_copy(h, n):
        return copy(sto.at[h], sti.at[h, n], st_s.at[h, n], st_r.at[h, n], dev(others[n], c, r, hd))

    STEPS = (-1, 1)

    pl.semaphore_wait(barrier, G0 - 1 + C - 1 + R - 1)

    def norm_step(i):
        slot = jnp.where(i < 2, i + 4, jnp.where(i < 4, i, i - 4))
        row = jnp.where(i < 2, i + 2, jnp.where(i < 4, 3 * i - 2, i - 4))
        at = jnp.where(i < 2, i + 12, jnp.where(i < 4, i, i - 4))
        kv[at, 0] = normed(raw(hk, slot), kgain)
        kv[at, 1] = raw(hv, slot)
        qd[row, 0] = normed(raw(hq, slot), qgain)
        qd[row, 1] = raw(ho, slot)

        @pl.when(i == 1)
        def _():
            for step in STEPS:
                on(c_ok(step), col_fwd(step).start)
            for step in STEPS:
                on(r_ok(step), row_fwd(step, 0).start)

        on(i == 2, z_fwd(0).start)

    loop(6, norm_step)

    nothing = jnp.zeros((2, 2, tile, HD), BF16)
    for step in STEPS:

        def blank_column(i, step=step):
            kv[pl.ds(4 + 2 * (3 * i + 1 + step), 2)] = nothing

        def blank_row(i, step=step):
            kv[pl.ds(4 + 2 * (3 + 3 * step + i), 2)] = nothing

        on(jnp.logical_not(c_ok(step)), functools.partial(loop, 3, blank_column))
        on(jnp.logical_not(r_ok(step)), functools.partial(loop, 3, blank_row))

    def clear(i):
        stats[i] = jnp.zeros((16, tile), F32)
        dqt[i] = jnp.zeros((HD, tile), F32)
        fk[i] = jnp.zeros((tile, HD), F32)
        fv[i] = jnp.zeros((tile, HD), F32)

    loop(10, clear)
    gacc[...] = jnp.zeros_like(gacc)

    def pass_one(idx, row, at, count):
        query, up = qd[row, 0], qd[row, 1]
        sum_l, sum_d = stats[row, 0:8], stats[row, 8:16]
        for j in range(0, tile, chunk):
            s = dot(kv[at, 0, j : j + chunk], query, NT)
            p = jnp.where(rows_iota < count - j, jnp.exp2(s * (SCALE * LOG2E)), 0.0)
            dp = dot(kv[at, 1, j : j + chunk], up, NT)
            pp[idx, j : j + chunk] = p
            dd[idx, j : j + chunk] = dp
            sum_l = sum_l + fold(p)
            sum_d = sum_d + fold(p * dp)
        stats[row, 0:8] = sum_l
        stats[row, 8:16] = sum_d

    def pass_two(idx, row, at, slot, emit):
        query, up = qd[row, 0], qd[row, 1]
        inv, out_dot = stats[row, 0:1], stats[row, 8:9]
        key_sum = gacc[slot]
        dq = dqt[row]
        for j in range(0, tile, chunk):
            w = pp[idx, j : j + chunk] * inv
            g = (w * (dd[idx, j : j + chunk] - out_dot)).astype(BF16)
            keys = kv[at, 0, j : j + chunk]
            dk = dot(g, query, NN)
            dv = dot(w.astype(BF16), up, NN)
            dq = dq + dot(keys, g, TN)
            key_sum = key_sum + fold(dk * keys.astype(F32))
            emit(j, dk, dv)
        gacc[slot] = key_sum
        dqt[row] = dq

    def added_to(place):
        def emit(j, dk, dv):
            fk[place, pl.ds(j, chunk)] += dk
            fv[place, pl.ds(j, chunk)] += dv

        return emit

    def put_stats(row, total, dot_total, ok_lanes):
        inv = 1.0 / total
        stats[row, 0:8] = jnp.broadcast_to(jnp.where(ok_lanes, inv, 0.0), (8, tile))
        stats[row, 8:16] = jnp.broadcast_to(dot_total * inv, (8, tile))

    def partial(row):
        total = jnp.sum(stats[row, 0:8], axis=0, keepdims=True)
        return total, jnp.sum(stats[row, 8:16], axis=0, keepdims=True)

    def first(i):
        @pl.when(i == 3)
        def _():
            z_fwd(1).start()
            for dc in STEPS:
                on(c_ok(dc), col_fwd(-dc).wait_recv)
            for dc in STEPS:
                for step in STEPS:
                    on(c_ok(dc) & r_ok(step), row_fwd(step, dc).start)

        @pl.when(i == 5)
        def _():
            for dr in STEPS:
                on(r_ok(dr), row_fwd(-dr, 0).wait_recv)

        @pl.when(i == 7)
        def _():
            z_fwd(0).wait_recv()
            x_fwd(0).start()
            for dr in STEPS:
                for dc in STEPS:
                    on(r_ok(dr) & c_ok(dc), row_fwd(-dr, dc).wait_recv)

        p = jnp.int32(4)
        for n, q in ((3, 3), (4, 5), (5, 1), (6, 7), (7, 0), (8, 2), (9, 6), (10, 8)):
            p = jnp.where(i == n, q, p)
        dr = lax.div(p, 3)
        count = count_at(t, c + p - 3 * dr - 1, r + dr - 1)
        for h in range(2):
            row = jnp.where(i == 1, h, jnp.where(i == 2, 4 + 3 * h, 2 + h))
            at = jnp.where(i == 1, h, jnp.where(i == 2, 2 + h, 4 + 2 * p + h))
            idx = jnp.where(i == 1, h, jnp.where(i == 2, 4 + 3 * h, 10 + 2 * p + h))
            pass_one(idx, row, at, count)

    loop(11, first)

    far_count = jnp.where((td - t) * (td - t) == 1, own_count, 0)
    tile_ok = (query_ok, lanes < count_at(tz, c, r), lanes < count_at(td, c, r))

    def time_first(h):
        def step(i):
            on(i == 1, x_fwd(h).wait_recv)
            row = time_row(h, 1 + i)
            pass_one(row, row, 2 + h, jnp.where(i == 1, far_count, own_count))

        loop(2, step)
        for b in range(3):
            total, dot_total = partial(time_row(h, b))
            sto[h, 2 * b : 2 * b + 1] = total
            sto[h, 2 * b + 1 : 2 * b + 2] = dot_total
        sto[h, 6:8] = jnp.zeros((2, tile), F32)
        for n in range(3):
            stat_copy(h, n).start()

    def time_total(h):
        for n in range(3):
            stat_copy(h, n).wait_recv()
        for b, (n, i), (m, k) in ((0, (0, 2), (2, 4)), (1, (0, 0), (1, 4)), (2, (2, 0), (1, 2))):

            def row(q, b=b, n=n, i=i, m=m, k=k):
                mine = sto[h, 2 * b + q : 2 * b + q + 1]
                return mine + sti[h, n, i + q : i + q + 1] + sti[h, m, k + q : k + q + 1]

            put_stats(time_row(h, b), row(0), row(1), tile_ok[b])

    def time_second(h):
        time_total(h)

        def step(i):
            @pl.when(i == 1)
            def _():
                xout[h] = dqt[time_row(h, 2)].astype(BF16)
                x_bwd(h).start()

            row = time_row(h, 2 - i)
            pass_two(row, row, 2 + h, TIME + h, added_to(TIME + h))

        loop(3, step)

    def time_send_back(h):
        x_bwd(h).wait_recv()
        zout[h] = (dqt[time_row(h, 1)] + xin[h].astype(F32)).astype(BF16)
        z_bwd(h).start()

    time_first(0)
    loop(4, lambda row: put_stats(row, *partial(row), query_ok))

    def outer(i):
        d = lax.div(i, 3)
        dc = i - 3 * d

        @pl.when(i == 3)
        def _():
            for h in range(2):
                on(r_ok(-1), row_bwd(-1, h).start)

        for h in range(2):

            def emit(j, dk, dv, h=h):
                rowo[h, d, dc, 0, pl.ds(j, chunk)] = dk.astype(BF16)
                rowo[h, d, dc, 1, pl.ds(j, chunk)] = dv.astype(BF16)

            p = 6 * d + dc
            pass_two(10 + 2 * p + h, 2 + h, 4 + 2 * p + h, SPACE + h, emit)

    loop(6, outer)
    for h in range(2):
        on(r_ok(1), row_bwd(1, h).start)

    time_second(0)
    z_fwd(1).wait_recv()
    x_fwd(1).start()
    time_send_back(0)
    time_first(1)

    def middle(i):
        p = 2 + i
        for h in range(2):
            idx = jnp.where(i == 0, h, 10 + 2 * p + h)
            row = jnp.where(i == 0, h, 2 + h)
            at = jnp.where(i == 0, h, 4 + 2 * p + h)
            slot = jnp.where(i == 0, h, SPACE + h)
            place = jnp.where(i == 0, h, jnp.where(i == 1, 6 + h, jnp.where(i == 2, SPACE + h, 8 + h)))
            pass_two(idx, row, at, slot, added_to(place))

    loop(4, middle)

    for h in range(2):
        for dr in STEPS:

            def add_row(dr=dr, h=h):
                row_bwd(-dr, h).wait_recv()

                def add(i):
                    place = jnp.where(i == 1, SPACE + h, 6 + i + h)
                    fk[place] += rowi[h, side(dr), i, 0].astype(F32)
                    fv[place] += rowi[h, side(dr), i, 1].astype(F32)

                loop(3, add)

            on(r_ok(dr), add_row)
        for step in STEPS:

            def send_column(step=step, h=h):
                colo[h, side(step), 0] = fk[7 + step + h].astype(BF16)
                colo[h, side(step), 1] = fv[7 + step + h].astype(BF16)
                col_bwd(step, h).start()

            on(c_ok(step), send_column)

    time_second(1)
    time_send_back(1)

    pair_sum = gacc[0]
    for s in range(1, 6):
        pair_sum = pair_sum + gacc[s]

    def gain_copy(n, j):
        _, mine, peer = groups[n]
        return copy(gbuf.at[n, mine], gbuf.at[n, mine], g_s.at[n, j], g_r.at[n, mine], peer(j))

    def gain_send(n, value):
        size, mine, _ = groups[n]
        gbuf[n, mine] = value
        loop(size - 1, lambda j: gain_copy(n, j + 1).start())

    def gain_sum(n):
        size, mine, peer = groups[n]

        def wait(j):
            other = lax.rem(mine + j + 1, size)
            copy(gbuf.at[n, other], gbuf.at[n, other], g_s.at[n, j + 1], g_r.at[n, other], peer(j + 1)).wait_recv()

        loop(size - 1, wait)
        total = gbuf[n, 0]
        for i in range(1, size):
            total = total + gbuf[n, i]
        return total

    def query_out(s, grad_t):
        grad = jnp.transpose(grad_t) * SCALE
        unit, inv = unit_of(raw(hq, s))
        scaled = grad * qgain[...]
        mean = jnp.mean(scaled * unit, axis=1, keepdims=True)
        oq[s] = (inv * (scaled - unit * mean)).astype(BF16)

    def key_out(s):
        grad = fk[s] * SCALE
        unit, inv = unit_of(raw(hk, s))
        scaled = grad * kgain[...]
        mean = jnp.mean(scaled * unit, axis=1, keepdims=True)
        ok[s] = (inv * (scaled - unit * mean)).astype(BF16)
        ov[s] = fv[s].astype(BF16)

    gain_send(0, pair_sum)
    loop(4, lambda i: query_out(jnp.where(i < 2, i, i + 2), dqt[i]))
    gain_send(1, gain_sum(0))
    for h in range(2):
        for dc in STEPS:

            def add_column(dc=dc, h=h):
                col_bwd(-dc, h).wait_recv()
                fk[SPACE + h] += coli[h, side(dc), 0].astype(F32)
                fv[SPACE + h] += coli[h, side(dc), 1].astype(F32)

            on(c_ok(dc), add_column)
    loop(6, key_out)
    gain_send(2, gain_sum(1))
    for h in range(2):
        z_bwd(h).wait_recv()
    loop(2, lambda h: query_out(TIME + h, dqt[time_row(h, 0)] + zin[h].astype(F32)))
    total = jnp.sum(gain_sum(2), axis=0, keepdims=True) * SCALE
    og[...] = jnp.concatenate([total / qgain[...], total / kgain[...]], axis=0)

    for h in range(2):
        for made in (z_fwd, x_fwd, x_bwd, z_bwd):
            made(h).wait_send()
        for n in range(3):
            stat_copy(h, n).wait_send()
    for step in STEPS:
        on(c_ok(step), col_fwd(step).wait_send)
        on(r_ok(step), row_fwd(step, 0).wait_send)
        for dc in STEPS:
            on(c_ok(dc) & r_ok(step), row_fwd(step, dc).wait_send)
        for h in range(2):
            on(r_ok(step), row_bwd(step, h).wait_send)
            on(c_ok(step), col_bwd(step, h).wait_send)
    for n, (size, _, _) in enumerate(groups):
        loop(size - 1, lambda j, n=n: gain_copy(n, j + 1).wait_send())


def hand_over(we, q, k, v, gains, oq, ok, ov, og):
    kinds = [we[0, h] + 2 * we[1, h] for h in range(6)]
    for h in range(6):
        slot = 2 * kinds[h]
        for g in range(h):
            slot = slot + jnp.where(kinds[g] == kinds[h], 1, 0)
        for src, dst in ((q, oq), (k, ok), (v, ov)):
            dst[:, h * HD : (h + 1) * HD] = src[slot]
    og[...] = gains[...]


def on_device(T, C, R, H, query_raw, key_raw, values, out_grad, query_gain, key_gain, window_extent, tile_counts):
    tile, width = query_raw.shape[2], query_raw.shape[3]
    chunk = min(128, tile)
    flat = lambda x: x.reshape(tile, width)
    most = max(T * H, C, R)
    dma = pltpu.SemaphoreType.DMA
    vmem = pl.BlockSpec(memory_space=pltpu.VMEM)
    smem = pl.BlockSpec(memory_space=pltpu.SMEM)
    heads = lambda n: pltpu.VMEM((n, tile, HD), BF16)
    pairs = lambda *n: pltpu.VMEM(n + (2, tile, HD), BF16)
    scratch = [
        heads(6), heads(6), heads(6), heads(6),
        pairs(10), pairs(22),
        pltpu.VMEM((28, tile, tile), F32),
        pltpu.VMEM((28, tile, tile), F32),
        pltpu.VMEM((10, 16, tile), F32),
        pltpu.VMEM((2, 8, tile), F32),
        pltpu.VMEM((2, 3, 8, tile), F32),
        pltpu.VMEM((10, HD, tile), F32),
        pltpu.VMEM((10, tile, HD), F32),
        pltpu.VMEM((10, tile, HD), F32),
        pltpu.VMEM((2, HD, tile), BF16),
        pltpu.VMEM((2, HD, tile), BF16),
        pltpu.VMEM((2, HD, tile), BF16),
        pltpu.VMEM((2, HD, tile), BF16),
        pairs(2, 2, 3), pairs(2, 2, 3), pairs(2, 2), pairs(2, 2),
        pltpu.VMEM((6, 8, HD), F32),
        pltpu.VMEM((3, most, 8, HD), F32),
        dma((2,)), dma((2,)), dma((2,)), dma((2,)),
        dma((2,)), dma((2,)), dma((2, 3)), dma((2, 3)),
        dma((2,)), dma((2,)), dma((2,)), dma((2,)),
        dma((2, 2)), dma((2, 2)), dma((2, 2)), dma((2, 2)),
        dma((2, 3)), dma((2, 3)),
        dma((3, most)), dma((3, most)),
    ]
    wide = jax.ShapeDtypeStruct((6, tile, HD), BF16)
    extent = window_extent.T
    grad_q, grad_k, grad_v, gains = pl.pallas_call(
        functools.partial(kernel, T, C, R, H, tile, chunk),
        out_shape=(wide, wide, wide, jax.ShapeDtypeStruct((2, HD), F32)),
        in_specs=[smem, smem] + [vmem] * 6,
        out_specs=(vmem,) * 4,
        scratch_shapes=scratch,
        compiler_params=pltpu.CompilerParams(
            collective_id=0, has_side_effects=True, vmem_limit_bytes=60 * 1024 * 1024
        ),
    )(
        extent,
        tile_counts,
        query_gain.reshape(1, HD),
        key_gain.reshape(1, HD),
        flat(query_raw),
        flat(key_raw),
        flat(values),
        flat(out_grad),
    )
    whole = jax.ShapeDtypeStruct((tile, width), BF16)
    outs = pl.pallas_call(
        hand_over,
        out_shape=(whole, whole, whole, jax.ShapeDtypeStruct((2, HD), F32)),
        in_specs=[smem] + [vmem] * 4,
        out_specs=(vmem,) * 4,
        compiler_params=pltpu.CompilerParams(vmem_limit_bytes=60 * 1024 * 1024),
    )(extent, grad_q, grad_k, grad_v, gains)
    shape = (1, 1, tile, width)
    return tuple(x.reshape(shape) for x in outs[:3]) + (outs[3],)


def solution(mesh):
    tile_spec = P("tm", "space", None, "head")

    def program(*args):
        T = args[7].shape[0]
        C = mesh.shape["tm"] // T
        return on_device(T, C, mesh.shape["space"], mesh.shape["head"], *args)

    return jax.shard_map(
        program,
        mesh=mesh,
        in_specs=(tile_spec,) * 4 + (P(), P(), P("head", None), P()),
        out_specs=(tile_spec,) * 3 + (P(),),
        check_vma=False,
    )
```

```python
import functools

import jax
import jax.numpy as jnp
from jax import lax
from jax.experimental import pallas as pl
from jax.experimental.pallas import tpu as pltpu
from jax.sharding import PartitionSpec as P

MESH = pl.DeviceIdType.MESH
HD = 128
F32 = jnp.float32
BF16 = jnp.bfloat16
SCALE = HD**-0.5
LOG2E = 1.4426950408889634
NT = (((1,), (1,)), ((), ()))
NN = (((1,), (0,)), ((), ()))
TN = (((0,), (0,)), ((), ()))

TIME, SPACE = 2, 4


def dot(a, b, dims):
    return lax.dot_general(a, b, dims, preferred_element_type=F32)


def unit_of(raw):
    x = raw.astype(F32)
    inv = lax.rsqrt(jnp.mean(x * x, axis=1, keepdims=True) + 1e-6)
    return x * inv, inv


def fold(x):
    return jnp.sum(x.reshape(x.shape[0] // 8, 8, x.shape[1]), axis=0)


def kernel(
    T, C, R, H, tile, chunk,
    we, counts, qgain, kgain, qraw, kraw, vals, ograd,
    oq, ok, ov, og,
    hq, hk, hv, ho, qd, kv, pp, dd, stats, sto, sti, dqt, fk, fv,
    xout, xin, zout, zin, rowo, rowi, colo, coli, gacc, gbuf,
    zf_s, zf_r, xf_s, xf_r, cf_s, cf_r, rf_s, rf_r,
    zb_s, zb_r, xb_s, xb_r, cb_s, cb_r, rb_s, rb_r, st_s, st_r, g_s, g_r,
):
    tm = lax.axis_index("tm")
    r = lax.axis_index("space")
    hd = lax.axis_index("head")
    t = lax.div(tm, C)
    c = lax.rem(tm, C)
    tz = t + 1 - 2 * lax.rem(t, 2)
    tx = lax.rem(t + 2, T)
    td = lax.rem(tz + 2, T)

    def dev(t_, c_, r_, h_):
        return (t_ * C + c_, r_, h_)

    def loop(n, body):
        def step(i, carry):
            body(i)
            return carry

        lax.fori_loop(0, n, step, 0)

    def on(condition, action):
        pl.when(condition)(action)

    G0 = T * H
    gi = t * H + hd

    def peer0(j):
        g = lax.rem(gi + j, G0)
        return dev(lax.div(g, H), c, r, lax.rem(g, H))

    def peer1(j):
        return dev(t, lax.rem(c + j, C), r, hd)

    def peer2(j):
        return dev(t, c, lax.rem(r + j, R), hd)

    groups = ((G0, gi, peer0), (C, c, peer1), (R, r, peer2))
    barrier = pltpu.get_barrier_semaphore()
    for size, _, peer in groups:

        def greet(j, peer=peer):
            pl.semaphore_signal(barrier, inc=1, device_id=peer(j + 1), device_id_type=MESH)

        loop(size - 1, greet)

    kinds = [we[0, h] + 2 * we[1, h] for h in range(6)]
    head_of = []
    for kind in range(3):
        low, high = jnp.int32(5), jnp.int32(0)
        for h in range(6):
            low = jnp.minimum(low, jnp.where(kinds[h] == kind, h, 5))
            high = jnp.maximum(high, jnp.where(kinds[h] == kind, h, 0))
        head_of += [low, high]

    def split(h):
        cut = pl.ds(pl.multiple_of(h * HD, HD), HD)
        for by_head, whole in ((hk, kraw), (hv, vals), (hq, qraw), (ho, ograd)):
            by_head[h] = whole[:, cut]

    loop(6, split)

    def raw(ref, slot):
        at = head_of[0]
        for s in range(1, 6):
            at = jnp.where(slot == s, head_of[s], at)
        return ref[at]

    def normed(x, gain):
        unit, _ = unit_of(x)
        return (unit * gain[...]).astype(BF16)

    def count_at(t_, c_, r_):
        inside = (c_ >= 0) & (c_ < C) & (r_ >= 0) & (r_ < R)
        got = counts[t_, lax.rem(c_ + C, C), lax.rem(r_ + R, R)]
        return jnp.where(inside, got, 0)

    own_count = count_at(t, c, r)
    lanes = lax.broadcasted_iota(jnp.int32, (1, tile), 1)
    query_ok = lanes < own_count
    rows_iota = lax.broadcasted_iota(jnp.int32, (chunk, tile), 0)

    def time_row(h, b):
        return 4 + 3 * h + b

    def tile_of(p, h):
        return kv.at[4 + 2 * p + h]

    def side(step):
        return (step + 1) // 2

    def c_ok(step):
        return (c + step >= 0) & (c + step < C)

    def r_ok(step):
        return (r + step >= 0) & (r + step < R)

    def c_dev(step):
        return dev(t, lax.rem(c + step + C, C), r, hd)

    def r_dev(step):
        return dev(t, c, lax.rem(r + step + R, R), hd)

    def copy(src, dst, send, recv, where):
        return pltpu.make_async_remote_copy(
            src_ref=src, dst_ref=dst, send_sem=send, recv_sem=recv, device_id=where, device_id_type=MESH
        )

    def col_fwd(step, h):
        return copy(
            tile_of(4, h), tile_of(4 - step, h), cf_s.at[h, side(step)], cf_r.at[h, side(-step)], c_dev(step)
        )

    def row_fwd(step, dc, h):
        return copy(
            tile_of(4 + dc, h), tile_of(4 + dc - 3 * step, h),
            rf_s.at[h, side(step), 1 + dc], rf_r.at[h, side(-step), 1 + dc], r_dev(step),
        )

    def z_fwd(h):
        return copy(qd.at[4 + 3 * h], qd.at[5 + 3 * h], zf_s.at[h], zf_r.at[h], dev(tz, c, r, hd))

    def x_fwd(h):
        return copy(qd.at[5 + 3 * h], qd.at[6 + 3 * h], xf_s.at[h], xf_r.at[h], dev(tx, c, r, hd))

    def x_bwd(h):
        return copy(xout.at[h], xin.at[h], xb_s.at[h], xb_r.at[h], dev(tx, c, r, hd))

    def z_bwd(h):
        return copy(zout.at[h], zin.at[h], zb_s.at[h], zb_r.at[h], dev(tz, c, r, hd))

    def row_bwd(step, h, i):
        return copy(
            rowo.at[h, side(step), i], rowi.at[h, side(-step), i],
            rb_s.at[h, side(step), i], rb_r.at[h, side(-step), i], r_dev(step),
        )

    def col_bwd(step, h):
        return copy(
            colo.at[h, side(step)], coli.at[h, side(-step)],
            cb_s.at[h, side(step)], cb_r.at[h, side(-step)], c_dev(step),
        )

    others = (tz, tx, td)

    def stat_copy(h, n):
        return copy(sto.at[h], sti.at[h, n], st_s.at[h, n], st_r.at[h, n], dev(others[n], c, r, hd))

    STEPS = (-1, 1)

    pl.semaphore_wait(barrier, G0 - 1 + C - 1 + R - 1)

    def norm_step(i):
        slot = jnp.where(i < 2, i + 4, jnp.where(i < 4, i, i - 4))
        row = jnp.where(i < 2, i + 2, jnp.where(i < 4, 3 * i - 2, i - 4))
        at = jnp.where(i < 2, i + 12, jnp.where(i < 4, i, i - 4))
        kv[at, 0] = normed(raw(hk, slot), kgain)
        kv[at, 1] = raw(hv, slot)
        qd[row, 0] = normed(raw(hq, slot), qgain)
        qd[row, 1] = raw(ho, slot)

        @pl.when(i < 2)
        def _():
            for step in STEPS:
                on(c_ok(step), col_fwd(step, i).start)
            for step in STEPS:
                on(r_ok(step), row_fwd(step, 0, i).start)

    loop(6, norm_step)

    nothing = jnp.zeros((2, 2, tile, HD), BF16)
    for step in STEPS:

        def blank_column(i, step=step):
            kv[pl.ds(4 + 2 * (3 * i + 1 + step), 2)] = nothing

        def blank_row(i, step=step):
            kv[pl.ds(4 + 2 * (3 + 3 * step + i), 2)] = nothing

        on(jnp.logical_not(c_ok(step)), functools.partial(loop, 3, blank_column))
        on(jnp.logical_not(r_ok(step)), functools.partial(loop, 3, blank_row))

    def clear(i):
        stats[i] = jnp.zeros((16, tile), F32)
        dqt[i] = jnp.zeros((HD, tile), F32)
        fk[i] = jnp.zeros((tile, HD), F32)
        fv[i] = jnp.zeros((tile, HD), F32)

    loop(10, clear)
    gacc[...] = jnp.zeros_like(gacc)

    def pass_one(idx, row, at, count):
        query, up = qd[row, 0], qd[row, 1]
        sum_l, sum_d = stats[row, 0:8], stats[row, 8:16]
        for j in range(0, tile, chunk):
            s = dot(kv[at, 0, j : j + chunk], query, NT)
            p = jnp.where(rows_iota < count - j, jnp.exp2(s * (SCALE * LOG2E)), 0.0)
            dp = dot(kv[at, 1, j : j + chunk], up, NT)
            pp[idx, j : j + chunk] = p
            dd[idx, j : j + chunk] = dp
            sum_l = sum_l + fold(p)
            sum_d = sum_d + fold(p * dp)
        stats[row, 0:8] = sum_l
        stats[row, 8:16] = sum_d

    def pass_two(idx, row, at, slot, emit):
        query, up = qd[row, 0], qd[row, 1]
        inv, out_dot = stats[row, 0:1], stats[row, 8:9]
        key_sum = gacc[slot]
        dq = dqt[row]
        for j in range(0, tile, chunk):
            w = pp[idx, j : j + chunk] * inv
            g = (w * (dd[idx, j : j + chunk] - out_dot)).astype(BF16)
            keys = kv[at, 0, j : j + chunk]
            dk = dot(g, query, NN)
            dv = dot(w.astype(BF16), up, NN)
            dq = dq + dot(keys, g, TN)
            key_sum = key_sum + fold(dk * keys.astype(F32))
            emit(j, dk, dv)
        gacc[slot] = key_sum
        dqt[row] = dq

    def added_to(place):
        def emit(j, dk, dv):
            fk[place, pl.ds(j, chunk)] += dk
            fv[place, pl.ds(j, chunk)] += dv

        return emit

    def put_stats(row, total, dot_total, ok_lanes):
        inv = 1.0 / total
        stats[row, 0:8] = jnp.broadcast_to(jnp.where(ok_lanes, inv, 0.0), (8, tile))
        stats[row, 8:16] = jnp.broadcast_to(dot_total * inv, (8, tile))

    def partial(row):
        total = jnp.sum(stats[row, 0:8], axis=0, keepdims=True)
        return total, jnp.sum(stats[row, 8:16], axis=0, keepdims=True)

    def own(i):
        for h in range(2):
            row = jnp.where(i == 1, h, jnp.where(i == 2, 4 + 3 * h, 2 + h))
            at = jnp.where(i == 1, h, jnp.where(i == 2, 2 + h, 12 + h))
            idx = jnp.where(i == 1, h, jnp.where(i == 2, 4 + 3 * h, 18 + h))
            pass_one(idx, row, at, own_count)

    loop(3, own)

    def space_count(p):
        dr = lax.div(p, 3)
        return count_at(t, c + p - 3 * dr - 1, r + dr - 1)

    def cross(i):
        @pl.when(i == 0)
        def _():
            for h in range(2):
                for dc in STEPS:
                    on(c_ok(dc), col_fwd(-dc, h).wait_recv)
                for dc in STEPS:
                    for step in STEPS:
                        on(c_ok(dc) & r_ok(step), row_fwd(step, dc, h).start)
            for h in range(2):
                z_fwd(h).start()

        @pl.when(i == 2)
        def _():
            for h in range(2):
                for dr in STEPS:
                    on(r_ok(dr), row_fwd(-dr, 0, h).wait_recv)

        p = jnp.where(i < 2, 3 + 2 * i, 6 * i - 11)
        count = space_count(p)
        for h in range(2):
            pass_one(10 + 2 * p + h, 2 + h, 4 + 2 * p + h, count)

    loop(4, cross)

    far_count = jnp.where((td - t) * (td - t) == 1, own_count, 0)
    tile_ok = (query_ok, lanes < count_at(tz, c, r), lanes < count_at(td, c, r))

    def time_first(h):
        def step(i):
            on(i == 1, x_fwd(h).wait_recv)
            row = time_row(h, 1 + i)
            pass_one(row, row, 2 + h, jnp.where(i == 1, far_count, own_count))

        loop(2, step)
        for b in range(3):
            total, dot_total = partial(time_row(h, b))
            sto[h, 2 * b : 2 * b + 1] = total
            sto[h, 2 * b + 1 : 2 * b + 2] = dot_total
        sto[h, 6:8] = jnp.zeros((2, tile), F32)
        for n in range(3):
            stat_copy(h, n).start()

    def time_total(h):
        for n in range(3):
            stat_copy(h, n).wait_recv()
        for b, (n, i), (m, k) in ((0, (0, 2), (2, 4)), (1, (0, 0), (1, 4)), (2, (2, 0), (1, 2))):

            def row(q, b=b, n=n, i=i, m=m, k=k):
                mine = sto[h, 2 * b + q : 2 * b + q + 1]
                return mine + sti[h, n, i + q : i + q + 1] + sti[h, m, k + q : k + q + 1]

            put_stats(time_row(h, b), row(0), row(1), tile_ok[b])

    def time_second(h):
        time_total(h)

        def step(i):
            @pl.when(i == 1)
            def _():
                xout[h] = dqt[time_row(h, 2)].astype(BF16)
                x_bwd(h).start()

            row = time_row(h, 2 - i)
            pass_two(row, row, 2 + h, TIME + h, added_to(TIME + h))

        loop(3, step)

    def time_send_back(h):
        x_bwd(h).wait_recv()
        zout[h] = (dqt[time_row(h, 1)] + xin[h].astype(F32)).astype(BF16)
        z_bwd(h).start()

    def corners(h):
        @pl.when(h == 1)
        def _():
            z_fwd(0).wait_recv()
            x_fwd(0).start()

        for dr in STEPS:
            for dc in STEPS:
                on(r_ok(dr) & c_ok(dc), row_fwd(-dr, dc, h).wait_recv)

        def corner(i):
            for dc in range(0, 3, 2):
                p = 6 * i + dc
                pass_one(10 + 2 * p + h, 2 + h, 4 + 2 * p + h, space_count(p))

        loop(2, corner)
        put_stats(2 + h, *partial(2 + h), query_ok)

        def outer(i):
            dc = jnp.where(i == 0, 0, 3 - i)
            for d in range(2):

                def emit(j, dk, dv, d=d):
                    rowo[h, d, dc, 0, pl.ds(j, chunk)] = dk.astype(BF16)
                    rowo[h, d, dc, 1, pl.ds(j, chunk)] = dv.astype(BF16)

                p = 6 * d + dc
                pass_two(10 + 2 * p + h, 2 + h, 4 + 2 * p + h, SPACE + h, emit)
            for step in STEPS:
                on(r_ok(step), row_bwd(step, h, dc).start)

        loop(3, outer)

    loop(2, corners)
    loop(2, lambda row: put_stats(row, *partial(row), query_ok))

    def middle(i):
        p = 2 + i
        for h in range(2):
            idx = jnp.where(i == 0, h, 10 + 2 * p + h)
            row = jnp.where(i == 0, h, 2 + h)
            at = jnp.where(i == 0, h, 4 + 2 * p + h)
            slot = jnp.where(i == 0, h, SPACE + h)
            place = jnp.where(i == 0, h, jnp.where(i == 1, 6 + h, jnp.where(i == 2, SPACE + h, 8 + h)))
            pass_two(idx, row, at, slot, added_to(place))

    loop(4, middle)

    def rows_back(h):
        for i in (0, 2, 1):
            place = SPACE + h if i == 1 else 6 + i + h
            for dr in STEPS:

                def add_row(dr=dr, i=i, place=place):
                    row_bwd(-dr, h, i).wait_recv()
                    fk[place] += rowi[h, side(dr), i, 0].astype(F32)
                    fv[place] += rowi[h, side(dr), i, 1].astype(F32)

                on(r_ok(dr), add_row)
            if i != 1:

                def send_column(step=i - 1, place=place):
                    colo[h, side(step), 0] = fk[place].astype(BF16)
                    colo[h, side(step), 1] = fv[place].astype(BF16)
                    col_bwd(step, h).start()

                on(c_ok(i - 1), send_column)

    z_fwd(1).wait_recv()
    x_fwd(1).start()
    time_first(0)
    rows_back(0)
    time_second(0)
    time_first(1)
    time_send_back(0)
    rows_back(1)
    time_second(1)
    time_send_back(1)

    pair_sum = gacc[0]
    for s in range(1, 6):
        pair_sum = pair_sum + gacc[s]

    def gain_copy(n, j):
        _, mine, peer = groups[n]
        return copy(gbuf.at[n, mine], gbuf.at[n, mine], g_s.at[n, j], g_r.at[n, mine], peer(j))

    def gain_send(n, value):
        size, mine, _ = groups[n]
        gbuf[n, mine] = value
        loop(size - 1, lambda j: gain_copy(n, j + 1).start())

    def gain_sum(n):
        size, mine, peer = groups[n]

        def wait(j):
            other = lax.rem(mine + j + 1, size)
            copy(gbuf.at[n, other], gbuf.at[n, other], g_s.at[n, j + 1], g_r.at[n, other], peer(j + 1)).wait_recv()

        loop(size - 1, wait)
        total = gbuf[n, 0]
        for i in range(1, size):
            total = total + gbuf[n, i]
        return total

    def query_out(s, grad_t):
        grad = jnp.transpose(grad_t) * SCALE
        unit, inv = unit_of(raw(hq, s))
        scaled = grad * qgain[...]
        mean = jnp.mean(scaled * unit, axis=1, keepdims=True)
        oq[s] = (inv * (scaled - unit * mean)).astype(BF16)

    def key_out(s):
        grad = fk[s] * SCALE
        unit, inv = unit_of(raw(hk, s))
        scaled = grad * kgain[...]
        mean = jnp.mean(scaled * unit, axis=1, keepdims=True)
        ok[s] = (inv * (scaled - unit * mean)).astype(BF16)
        ov[s] = fv[s].astype(BF16)

    gain_send(0, pair_sum)
    loop(4, lambda i: query_out(jnp.where(i < 2, i, i + 2), dqt[i]))
    gain_send(1, gain_sum(0))
    loop(4, key_out)
    for h in range(2):
        for dc in STEPS:

            def add_column(dc=dc, h=h):
                col_bwd(-dc, h).wait_recv()
                fk[SPACE + h] += coli[h, side(dc), 0].astype(F32)
                fv[SPACE + h] += coli[h, side(dc), 1].astype(F32)

            on(c_ok(dc), add_column)
    gain_send(2, gain_sum(1))
    loop(2, lambda h: key_out(SPACE + h))
    for h in range(2):
        z_bwd(h).wait_recv()
    loop(2, lambda h: query_out(TIME + h, dqt[time_row(h, 0)] + zin[h].astype(F32)))
    total = jnp.sum(gain_sum(2), axis=0, keepdims=True) * SCALE
    og[...] = jnp.concatenate([total / qgain[...], total / kgain[...]], axis=0)

    for h in range(2):
        for made in (z_fwd, x_fwd, x_bwd, z_bwd):
            made(h).wait_send()
        for n in range(3):
            stat_copy(h, n).wait_send()
    for step in STEPS:
        for h in range(2):
            on(c_ok(step), col_fwd(step, h).wait_send)
            on(r_ok(step), row_fwd(step, 0, h).wait_send)
            for dc in STEPS:
                on(c_ok(dc) & r_ok(step), row_fwd(step, dc, h).wait_send)
            for i in range(3):
                on(r_ok(step), row_bwd(step, h, i).wait_send)
            on(c_ok(step), col_bwd(step, h).wait_send)
    for n, (size, _, _) in enumerate(groups):
        loop(size - 1, lambda j, n=n: gain_copy(n, j + 1).wait_send())


def hand_over(we, q, k, v, gains, oq, ok, ov, og):
    kinds = [we[0, h] + 2 * we[1, h] for h in range(6)]
    for h in range(6):
        slot = 2 * kinds[h]
        for g in range(h):
            slot = slot + jnp.where(kinds[g] == kinds[h], 1, 0)
        for src, dst in ((q, oq), (k, ok), (v, ov)):
            dst[:, h * HD : (h + 1) * HD] = src[slot]
    og[...] = gains[...]


def on_device(T, C, R, H, query_raw, key_raw, values, out_grad, query_gain, key_gain, window_extent, tile_counts):
    tile, width = query_raw.shape[2], query_raw.shape[3]
    chunk = min(128, tile)
    flat = lambda x: x.reshape(tile, width)
    most = max(T * H, C, R)
    dma = pltpu.SemaphoreType.DMA
    vmem = pl.BlockSpec(memory_space=pltpu.VMEM)
    smem = pl.BlockSpec(memory_space=pltpu.SMEM)
    heads = lambda n: pltpu.VMEM((n, tile, HD), BF16)
    pairs = lambda *n: pltpu.VMEM(n + (2, tile, HD), BF16)
    scratch = [
        heads(6), heads(6), heads(6), heads(6),
        pairs(10), pairs(22),
        pltpu.VMEM((28, tile, tile), F32),
        pltpu.VMEM((28, tile, tile), F32),
        pltpu.VMEM((10, 16, tile), F32),
        pltpu.VMEM((2, 8, tile), F32),
        pltpu.VMEM((2, 3, 8, tile), F32),
        pltpu.VMEM((10, HD, tile), F32),
        pltpu.VMEM((10, tile, HD), F32),
        pltpu.VMEM((10, tile, HD), F32),
        pltpu.VMEM((2, HD, tile), BF16),
        pltpu.VMEM((2, HD, tile), BF16),
        pltpu.VMEM((2, HD, tile), BF16),
        pltpu.VMEM((2, HD, tile), BF16),
        pairs(2, 2, 3), pairs(2, 2, 3), pairs(2, 2), pairs(2, 2),
        pltpu.VMEM((6, 8, HD), F32),
        pltpu.VMEM((3, most, 8, HD), F32),
        dma((2,)), dma((2,)), dma((2,)), dma((2,)),
        dma((2, 2)), dma((2, 2)), dma((2, 2, 3)), dma((2, 2, 3)),
        dma((2,)), dma((2,)), dma((2,)), dma((2,)),
        dma((2, 2)), dma((2, 2)), dma((2, 2, 3)), dma((2, 2, 3)),
        dma((2, 3)), dma((2, 3)),
        dma((3, most)), dma((3, most)),
    ]
    wide = jax.ShapeDtypeStruct((6, tile, HD), BF16)
    extent = window_extent.T
    grad_q, grad_k, grad_v, gains = pl.pallas_call(
        functools.partial(kernel, T, C, R, H, tile, chunk),
        out_shape=(wide, wide, wide, jax.ShapeDtypeStruct((2, HD), F32)),
        in_specs=[smem, smem] + [vmem] * 6,
        out_specs=(vmem,) * 4,
        scratch_shapes=scratch,
        compiler_params=pltpu.CompilerParams(
            collective_id=0, has_side_effects=True, vmem_limit_bytes=60 * 1024 * 1024
        ),
    )(
        extent,
        tile_counts,
        query_gain.reshape(1, HD),
        key_gain.reshape(1, HD),
        flat(query_raw),
        flat(key_raw),
        flat(values),
        flat(out_grad),
    )
    whole = jax.ShapeDtypeStruct((tile, width), BF16)
    outs = pl.pallas_call(
        hand_over,
        out_shape=(whole, whole, whole, jax.ShapeDtypeStruct((2, HD), F32)),
        in_specs=[smem] + [vmem] * 4,
        out_specs=(vmem,) * 4,
        compiler_params=pltpu.CompilerParams(vmem_limit_bytes=60 * 1024 * 1024),
    )(extent, grad_q, grad_k, grad_v, gains)
    shape = (1, 1, tile, width)
    return tuple(x.reshape(shape) for x in outs[:3]) + (outs[3],)


def solution(mesh):
    tile_spec = P("tm", "space", None, "head")

    def program(*args):
        T = args[7].shape[0]
        C = mesh.shape["tm"] // T
        return on_device(T, C, mesh.shape["space"], mesh.shape["head"], *args)

    return jax.shard_map(
        program,
        mesh=mesh,
        in_specs=(tile_spec,) * 4 + (P(), P(), P("head", None), P()),
        out_specs=(tile_spec,) * 3 + (P(),),
        check_vma=False,
    )
```

```python
import functools

import jax
import jax.numpy as jnp
from jax import lax
from jax.experimental import pallas as pl
from jax.experimental.pallas import tpu as pltpu
from jax.sharding import PartitionSpec as P

MESH = pl.DeviceIdType.MESH
HD = 128
F32 = jnp.float32
BF16 = jnp.bfloat16
SCALE = HD**-0.5
LOG2E = 1.4426950408889634
NT = (((1,), (1,)), ((), ()))
NN = (((1,), (0,)), ((), ()))
TN = (((0,), (0,)), ((), ()))

TIME, SPACE = 2, 4


def dot(a, b, dims):
    return lax.dot_general(a, b, dims, preferred_element_type=F32)


def unit_of(raw):
    x = raw.astype(F32)
    inv = lax.rsqrt(jnp.mean(x * x, axis=1, keepdims=True) + 1e-6)
    return x * inv, inv


def fold(x):
    return jnp.sum(x.reshape(x.shape[0] // 8, 8, x.shape[1]), axis=0)


def kernel(
    T, C, R, H, tile, chunk,
    we, counts, qgain, kgain, qraw, kraw, vals, ograd,
    oq, ok, ov, og,
    hq, hk, hv, ho, qd, kv, pp, dd, stats, sto, sti, dqt, fk, fv,
    xout, xin, zout, zin, rowo, rowi, colo, coli, gacc, gbuf,
    zf_s, zf_r, xf_s, xf_r, cf_s, cf_r, rf_s, rf_r,
    zb_s, zb_r, xb_s, xb_r, cb_s, cb_r, rb_s, rb_r, st_s, st_r, g_s, g_r,
):
    tm = lax.axis_index("tm")
    r = lax.axis_index("space")
    hd = lax.axis_index("head")
    t = lax.div(tm, C)
    c = lax.rem(tm, C)
    tz = t + 1 - 2 * lax.rem(t, 2)
    tx = lax.rem(t + 2, T)
    td = lax.rem(tz + 2, T)

    def dev(t_, c_, r_, h_):
        return (t_ * C + c_, r_, h_)

    def loop(n, body):
        def step(i, carry):
            body(i)
            return carry

        lax.fori_loop(0, n, step, 0)

    def on(condition, action):
        pl.when(condition)(action)

    G0 = T * H
    gi = t * H + hd

    def peer0(j):
        g = lax.rem(gi + j, G0)
        return dev(lax.div(g, H), c, r, lax.rem(g, H))

    def peer1(j):
        return dev(t, lax.rem(c + j, C), r, hd)

    def peer2(j):
        return dev(t, c, lax.rem(r + j, R), hd)

    groups = ((G0, gi, peer0), (C, c, peer1), (R, r, peer2))
    barrier = pltpu.get_barrier_semaphore()
    for size, _, peer in groups:

        def greet(j, peer=peer):
            pl.semaphore_signal(barrier, inc=1, device_id=peer(j + 1), device_id_type=MESH)

        loop(size - 1, greet)

    kinds = [we[0, h] + 2 * we[1, h] for h in range(6)]
    head_of = []
    for kind in range(3):
        low, high = jnp.int32(5), jnp.int32(0)
        for h in range(6):
            low = jnp.minimum(low, jnp.where(kinds[h] == kind, h, 5))
            high = jnp.maximum(high, jnp.where(kinds[h] == kind, h, 0))
        head_of += [low, high]

    def split(h):
        cut = pl.ds(pl.multiple_of(h * HD, HD), HD)
        for by_head, whole in ((hk, kraw), (hv, vals), (hq, qraw), (ho, ograd)):
            by_head[h] = whole[:, cut]

    loop(6, split)

    def raw(ref, slot):
        at = head_of[0]
        for s in range(1, 6):
            at = jnp.where(slot == s, head_of[s], at)
        return ref[at]

    def normed(x, gain):
        unit, _ = unit_of(x)
        return (unit * gain[...]).astype(BF16)

    def count_at(t_, c_, r_):
        inside = (c_ >= 0) & (c_ < C) & (r_ >= 0) & (r_ < R)
        got = counts[t_, lax.rem(c_ + C, C), lax.rem(r_ + R, R)]
        return jnp.where(inside, got, 0)

    own_count = count_at(t, c, r)
    lanes = lax.broadcasted_iota(jnp.int32, (1, tile), 1)
    query_ok = lanes < own_count
    rows_iota = lax.broadcasted_iota(jnp.int32, (chunk, tile), 0)

    def time_row(h, b):
        return 4 + 3 * h + b

    def tile_of(p, h):
        return kv.at[4 + 2 * p + h]

    def side(step):
        return (step + 1) // 2

    def c_ok(step):
        return (c + step >= 0) & (c + step < C)

    def r_ok(step):
        return (r + step >= 0) & (r + step < R)

    def c_dev(step):
        return dev(t, lax.rem(c + step + C, C), r, hd)

    def r_dev(step):
        return dev(t, c, lax.rem(r + step + R, R), hd)

    def copy(src, dst, send, recv, where):
        return pltpu.make_async_remote_copy(
            src_ref=src, dst_ref=dst, send_sem=send, recv_sem=recv, device_id=where, device_id_type=MESH
        )

    def col_fwd(step, h):
        return copy(
            tile_of(4, h), tile_of(4 - step, h), cf_s.at[h, side(step)], cf_r.at[h, side(-step)], c_dev(step)
        )

    def row_fwd(step, dc, h):
        return copy(
            tile_of(4 + dc, h), tile_of(4 + dc - 3 * step, h),
            rf_s.at[h, side(step), 1 + dc], rf_r.at[h, side(-step), 1 + dc], r_dev(step),
        )

    def z_fwd(h):
        return copy(qd.at[4 + 3 * h], qd.at[5 + 3 * h], zf_s.at[h], zf_r.at[h], dev(tz, c, r, hd))

    def x_fwd(h):
        return copy(qd.at[5 + 3 * h], qd.at[6 + 3 * h], xf_s.at[h], xf_r.at[h], dev(tx, c, r, hd))

    def x_bwd(h):
        return copy(xout.at[h], xin.at[h], xb_s.at[h], xb_r.at[h], dev(tx, c, r, hd))

    def z_bwd(h):
        return copy(zout.at[h], zin.at[h], zb_s.at[h], zb_r.at[h], dev(tz, c, r, hd))

    def row_bwd(step, h, i):
        return copy(
            rowo.at[h, side(step), i], rowi.at[h, side(-step), i],
            rb_s.at[h, side(step), i], rb_r.at[h, side(-step), i], r_dev(step),
        )

    def col_bwd(step, h):
        return copy(
            colo.at[h, side(step)], coli.at[h, side(-step)],
            cb_s.at[h, side(step)], cb_r.at[h, side(-step)], c_dev(step),
        )

    others = (tz, tx, td)

    def stat_copy(h, n):
        return copy(sto.at[h], sti.at[h, n], st_s.at[h, n], st_r.at[h, n], dev(others[n], c, r, hd))

    STEPS = (-1, 1)

    pl.semaphore_wait(barrier, G0 - 1 + C - 1 + R - 1)

    def norm_step(i):
        slot = jnp.where(i < 2, i + 4, jnp.where(i < 4, i, i - 4))
        row = jnp.where(i < 2, i + 2, jnp.where(i < 4, 3 * i - 2, i - 4))
        at = jnp.where(i < 2, i + 12, jnp.where(i < 4, i, i - 4))
        kv[at, 0] = normed(raw(hk, slot), kgain)
        kv[at, 1] = raw(hv, slot)
        qd[row, 0] = normed(raw(hq, slot), qgain)
        qd[row, 1] = raw(ho, slot)

        @pl.when(i < 2)
        def _():
            for step in STEPS:
                on(c_ok(step), col_fwd(step, i).start)
            for step in STEPS:
                on(r_ok(step), row_fwd(step, 0, i).start)

    loop(6, norm_step)

    nothing = jnp.zeros((2, 2, tile, HD), BF16)
    for step in STEPS:

        def blank_column(i, step=step):
            kv[pl.ds(4 + 2 * (3 * i + 1 + step), 2)] = nothing

        def blank_row(i, step=step):
            kv[pl.ds(4 + 2 * (3 + 3 * step + i), 2)] = nothing

        on(jnp.logical_not(c_ok(step)), functools.partial(loop, 3, blank_column))
        on(jnp.logical_not(r_ok(step)), functools.partial(loop, 3, blank_row))

    def clear(i):
        stats[i] = jnp.zeros((16, tile), F32)
        dqt[i] = jnp.zeros((HD, tile), F32)
        fk[i] = jnp.zeros((tile, HD), F32)
        fv[i] = jnp.zeros((tile, HD), F32)

    loop(10, clear)
    gacc[...] = jnp.zeros_like(gacc)

    def pass_one(idx, row, at, count):
        query, up = qd[row, 0], qd[row, 1]
        sum_l, sum_d = stats[row, 0:8], stats[row, 8:16]
        for j in range(0, tile, chunk):
            s = dot(kv[at, 0, j : j + chunk], query, NT)
            p = jnp.where(rows_iota < count - j, jnp.exp2(s * (SCALE * LOG2E)), 0.0)
            dp = dot(kv[at, 1, j : j + chunk], up, NT)
            pp[idx, j : j + chunk] = p
            dd[idx, j : j + chunk] = dp
            sum_l = sum_l + fold(p)
            sum_d = sum_d + fold(p * dp)
        stats[row, 0:8] = sum_l
        stats[row, 8:16] = sum_d

    def pass_two(idx, row, at, slot, emit):
        query, up = qd[row, 0], qd[row, 1]
        inv, out_dot = stats[row, 0:1], stats[row, 8:9]
        key_sum = gacc[slot]
        dq = dqt[row]
        for j in range(0, tile, chunk):
            w = pp[idx, j : j + chunk] * inv
            g = (w * (dd[idx, j : j + chunk] - out_dot)).astype(BF16)
            keys = kv[at, 0, j : j + chunk]
            dk = dot(g, query, NN)
            dv = dot(w.astype(BF16), up, NN)
            dq = dq + dot(keys, g, TN)
            key_sum = key_sum + fold(dk * keys.astype(F32))
            emit(j, dk, dv)
        gacc[slot] = key_sum
        dqt[row] = dq

    def added_to(place):
        def emit(j, dk, dv):
            fk[place, pl.ds(j, chunk)] += dk
            fv[place, pl.ds(j, chunk)] += dv

        return emit

    def put_stats(row, total, dot_total, ok_lanes):
        inv = 1.0 / total
        stats[row, 0:8] = jnp.broadcast_to(jnp.where(ok_lanes, inv, 0.0), (8, tile))
        stats[row, 8:16] = jnp.broadcast_to(dot_total * inv, (8, tile))

    def partial(row):
        total = jnp.sum(stats[row, 0:8], axis=0, keepdims=True)
        return total, jnp.sum(stats[row, 8:16], axis=0, keepdims=True)

    def own(i):
        on(i == 2, z_fwd(0).start)
        for h in range(2):
            row = jnp.where(i == 1, h, jnp.where(i == 2, 4 + 3 * h, 2 + h))
            at = jnp.where(i == 1, h, jnp.where(i == 2, 2 + h, 12 + h))
            idx = jnp.where(i == 1, h, jnp.where(i == 2, 4 + 3 * h, 18 + h))
            pass_one(idx, row, at, own_count)

    loop(3, own)

    def space_count(p):
        dr = lax.div(p, 3)
        return count_at(t, c + p - 3 * dr - 1, r + dr - 1)

    def cross(i):
        @pl.when(i == 0)
        def _():
            for h in range(2):
                for dc in STEPS:
                    on(c_ok(dc), col_fwd(-dc, h).wait_recv)
                for dc in STEPS:
                    for step in STEPS:
                        on(c_ok(dc) & r_ok(step), row_fwd(step, dc, h).start)
            z_fwd(1).start()

        @pl.when(i == 2)
        def _():
            for h in range(2):
                for dr in STEPS:
                    on(r_ok(dr), row_fwd(-dr, 0, h).wait_recv)

        p = jnp.where(i < 2, 3 + 2 * i, 6 * i - 11)
        count = space_count(p)
        for h in range(2):
            pass_one(10 + 2 * p + h, 2 + h, 4 + 2 * p + h, count)

    loop(4, cross)

    far_count = jnp.where((td - t) * (td - t) == 1, own_count, 0)
    tile_ok = (query_ok, lanes < count_at(tz, c, r), lanes < count_at(td, c, r))

    def time_first(h):
        def step(i):
            on(i == 1, x_fwd(h).wait_recv)
            row = time_row(h, 1 + i)
            pass_one(row, row, 2 + h, jnp.where(i == 1, far_count, own_count))

        loop(2, step)
        for b in range(3):
            total, dot_total = partial(time_row(h, b))
            sto[h, 2 * b : 2 * b + 1] = total
            sto[h, 2 * b + 1 : 2 * b + 2] = dot_total
        sto[h, 6:8] = jnp.zeros((2, tile), F32)
        for n in range(3):
            stat_copy(h, n).start()

    def time_total(h):
        for n in range(3):
            stat_copy(h, n).wait_recv()
        for b, (n, i), (m, k) in ((0, (0, 2), (2, 4)), (1, (0, 0), (1, 4)), (2, (2, 0), (1, 2))):

            def row(q, b=b, n=n, i=i, m=m, k=k):
                mine = sto[h, 2 * b + q : 2 * b + q + 1]
                return mine + sti[h, n, i + q : i + q + 1] + sti[h, m, k + q : k + q + 1]

            put_stats(time_row(h, b), row(0), row(1), tile_ok[b])

    def time_second(h):
        time_total(h)

        def step(i):
            @pl.when(i == 1)
            def _():
                xout[h] = dqt[time_row(h, 2)].astype(BF16)
                x_bwd(h).start()

            row = time_row(h, 2 - i)
            pass_two(row, row, 2 + h, TIME + h, added_to(TIME + h))

        loop(3, step)

    def time_send_back(h):
        x_bwd(h).wait_recv()
        zout[h] = (dqt[time_row(h, 1)] + xin[h].astype(F32)).astype(BF16)
        z_bwd(h).start()

    def corners(h):
        for dr in STEPS:
            for dc in STEPS:
                on(r_ok(dr) & c_ok(dc), row_fwd(-dr, dc, h).wait_recv)

        def corner(i):
            for dc in range(0, 3, 2):
                p = 6 * i + dc
                pass_one(10 + 2 * p + h, 2 + h, 4 + 2 * p + h, space_count(p))

        loop(2, corner)
        put_stats(2 + h, *partial(2 + h), query_ok)

        @pl.when(h == 0)
        def _():
            z_fwd(0).wait_recv()
            x_fwd(0).start()

        def outer(i):
            dc = jnp.where(i == 0, 0, 3 - i)
            for d in range(2):

                def emit(j, dk, dv, d=d):
                    rowo[h, d, dc, 0, pl.ds(j, chunk)] = dk.astype(BF16)
                    rowo[h, d, dc, 1, pl.ds(j, chunk)] = dv.astype(BF16)

                p = 6 * d + dc
                pass_two(10 + 2 * p + h, 2 + h, 4 + 2 * p + h, SPACE + h, emit)
            for step in STEPS:
                on(r_ok(step), row_bwd(step, h, dc).start)

        loop(3, outer)

        @pl.when(h == 0)
        def _():
            time_first(0)

    loop(2, corners)
    time_second(0)
    z_fwd(1).wait_recv()
    x_fwd(1).start()
    loop(2, lambda row: put_stats(row, *partial(row), query_ok))

    def middle(i):
        p = 2 + i
        for h in range(2):
            idx = jnp.where(i == 0, h, 10 + 2 * p + h)
            row = jnp.where(i == 0, h, 2 + h)
            at = jnp.where(i == 0, h, 4 + 2 * p + h)
            slot = jnp.where(i == 0, h, SPACE + h)
            place = jnp.where(i == 0, h, jnp.where(i == 1, 6 + h, jnp.where(i == 2, SPACE + h, 8 + h)))
            pass_two(idx, row, at, slot, added_to(place))

    loop(4, middle)

    def rows_back(h):
        for i in (0, 2, 1):
            place = SPACE + h if i == 1 else 6 + i + h
            for dr in STEPS:

                def add_row(dr=dr, i=i, place=place):
                    row_bwd(-dr, h, i).wait_recv()
                    fk[place] += rowi[h, side(dr), i, 0].astype(F32)
                    fv[place] += rowi[h, side(dr), i, 1].astype(F32)

                on(r_ok(dr), add_row)
            if i != 1:

                def send_column(step=i - 1, place=place):
                    colo[h, side(step), 0] = fk[place].astype(BF16)
                    colo[h, side(step), 1] = fv[place].astype(BF16)
                    col_bwd(step, h).start()

                on(c_ok(i - 1), send_column)

    time_send_back(0)
    time_first(1)
    rows_back(0)
    time_second(1)
    rows_back(1)
    time_send_back(1)

    pair_sum = gacc[0]
    for s in range(1, 6):
        pair_sum = pair_sum + gacc[s]

    def gain_copy(n, j):
        _, mine, peer = groups[n]
        return copy(gbuf.at[n, mine], gbuf.at[n, mine], g_s.at[n, j], g_r.at[n, mine], peer(j))

    def gain_send(n, value):
        size, mine, _ = groups[n]
        gbuf[n, mine] = value
        loop(size - 1, lambda j: gain_copy(n, j + 1).start())

    def gain_sum(n):
        size, mine, peer = groups[n]

        def wait(j):
            other = lax.rem(mine + j + 1, size)
            copy(gbuf.at[n, other], gbuf.at[n, other], g_s.at[n, j + 1], g_r.at[n, other], peer(j + 1)).wait_recv()

        loop(size - 1, wait)
        total = gbuf[n, 0]
        for i in range(1, size):
            total = total + gbuf[n, i]
        return total

    def query_out(s, grad_t):
        grad = jnp.transpose(grad_t) * SCALE
        unit, inv = unit_of(raw(hq, s))
        scaled = grad * qgain[...]
        mean = jnp.mean(scaled * unit, axis=1, keepdims=True)
        oq[s] = (inv * (scaled - unit * mean)).astype(BF16)

    def key_out(s):
        grad = fk[s] * SCALE
        unit, inv = unit_of(raw(hk, s))
        scaled = grad * kgain[...]
        mean = jnp.mean(scaled * unit, axis=1, keepdims=True)
        ok[s] = (inv * (scaled - unit * mean)).astype(BF16)
        ov[s] = fv[s].astype(BF16)

    gain_send(0, pair_sum)
    loop(4, lambda i: query_out(jnp.where(i < 2, i, i + 2), dqt[i]))
    gain_send(1, gain_sum(0))
    loop(4, key_out)
    for h in range(2):
        for dc in STEPS:

            def add_column(dc=dc, h=h):
                col_bwd(-dc, h).wait_recv()
                fk[SPACE + h] += coli[h, side(dc), 0].astype(F32)
                fv[SPACE + h] += coli[h, side(dc), 1].astype(F32)

            on(c_ok(dc), add_column)
    gain_send(2, gain_sum(1))
    loop(2, lambda h: key_out(SPACE + h))
    for h in range(2):
        z_bwd(h).wait_recv()
    loop(2, lambda h: query_out(TIME + h, dqt[time_row(h, 0)] + zin[h].astype(F32)))
    total = jnp.sum(gain_sum(2), axis=0, keepdims=True) * SCALE
    og[...] = jnp.concatenate([total / qgain[...], total / kgain[...]], axis=0)

    for h in range(2):
        for made in (z_fwd, x_fwd, x_bwd, z_bwd):
            made(h).wait_send()
        for n in range(3):
            stat_copy(h, n).wait_send()
    for step in STEPS:
        for h in range(2):
            on(c_ok(step), col_fwd(step, h).wait_send)
            on(r_ok(step), row_fwd(step, 0, h).wait_send)
            for dc in STEPS:
                on(c_ok(dc) & r_ok(step), row_fwd(step, dc, h).wait_send)
            for i in range(3):
                on(r_ok(step), row_bwd(step, h, i).wait_send)
            on(c_ok(step), col_bwd(step, h).wait_send)
    for n, (size, _, _) in enumerate(groups):
        loop(size - 1, lambda j, n=n: gain_copy(n, j + 1).wait_send())


def hand_over(we, q, k, v, gains, oq, ok, ov, og):
    kinds = [we[0, h] + 2 * we[1, h] for h in range(6)]
    for h in range(6):
        slot = 2 * kinds[h]
        for g in range(h):
            slot = slot + jnp.where(kinds[g] == kinds[h], 1, 0)
        for src, dst in ((q, oq), (k, ok), (v, ov)):
            dst[:, h * HD : (h + 1) * HD] = src[slot]
    og[...] = gains[...]


def on_device(T, C, R, H, query_raw, key_raw, values, out_grad, query_gain, key_gain, window_extent, tile_counts):
    tile, width = query_raw.shape[2], query_raw.shape[3]
    chunk = min(256, tile)
    flat = lambda x: x.reshape(tile, width)
    most = max(T * H, C, R)
    dma = pltpu.SemaphoreType.DMA
    vmem = pl.BlockSpec(memory_space=pltpu.VMEM)
    smem = pl.BlockSpec(memory_space=pltpu.SMEM)
    heads = lambda n: pltpu.VMEM((n, tile, HD), BF16)
    pairs = lambda *n: pltpu.VMEM(n + (2, tile, HD), BF16)
    scratch = [
        heads(6), heads(6), heads(6), heads(6),
        pairs(10), pairs(22),
        pltpu.VMEM((28, tile, tile), F32),
        pltpu.VMEM((28, tile, tile), F32),
        pltpu.VMEM((10, 16, tile), F32),
        pltpu.VMEM((2, 8, tile), F32),
        pltpu.VMEM((2, 3, 8, tile), F32),
        pltpu.VMEM((10, HD, tile), F32),
        pltpu.VMEM((10, tile, HD), F32),
        pltpu.VMEM((10, tile, HD), F32),
        pltpu.VMEM((2, HD, tile), BF16),
        pltpu.VMEM((2, HD, tile), BF16),
        pltpu.VMEM((2, HD, tile), BF16),
        pltpu.VMEM((2, HD, tile), BF16),
        pairs(2, 2, 3), pairs(2, 2, 3), pairs(2, 2), pairs(2, 2),
        pltpu.VMEM((6, 8, HD), F32),
        pltpu.VMEM((3, most, 8, HD), F32),
        dma((2,)), dma((2,)), dma((2,)), dma((2,)),
        dma((2, 2)), dma((2, 2)), dma((2, 2, 3)), dma((2, 2, 3)),
        dma((2,)), dma((2,)), dma((2,)), dma((2,)),
        dma((2, 2)), dma((2, 2)), dma((2, 2, 3)), dma((2, 2, 3)),
        dma((2, 3)), dma((2, 3)),
        dma((3, most)), dma((3, most)),
    ]
    wide = jax.ShapeDtypeStruct((6, tile, HD), BF16)
    extent = window_extent.T
    grad_q, grad_k, grad_v, gains = pl.pallas_call(
        functools.partial(kernel, T, C, R, H, tile, chunk),
        out_shape=(wide, wide, wide, jax.ShapeDtypeStruct((2, HD), F32)),
        in_specs=[smem, smem] + [vmem] * 6,
        out_specs=(vmem,) * 4,
        scratch_shapes=scratch,
        compiler_params=pltpu.CompilerParams(
            collective_id=0, has_side_effects=True, vmem_limit_bytes=60 * 1024 * 1024
        ),
    )(
        extent,
        tile_counts,
        query_gain.reshape(1, HD),
        key_gain.reshape(1, HD),
        flat(query_raw),
        flat(key_raw),
        flat(values),
        flat(out_grad),
    )
    whole = jax.ShapeDtypeStruct((tile, width), BF16)
    outs = pl.pallas_call(
        hand_over,
        out_shape=(whole, whole, whole, jax.ShapeDtypeStruct((2, HD), F32)),
        in_specs=[smem] + [vmem] * 4,
        out_specs=(vmem,) * 4,
        compiler_params=pltpu.CompilerParams(vmem_limit_bytes=60 * 1024 * 1024),
    )(extent, grad_q, grad_k, grad_v, gains)
    shape = (1, 1, tile, width)
    return tuple(x.reshape(shape) for x in outs[:3]) + (outs[3],)


def solution(mesh):
    tile_spec = P("tm", "space", None, "head")

    def program(*args):
        T = args[7].shape[0]
        C = mesh.shape["tm"] // T
        return on_device(T, C, mesh.shape["space"], mesh.shape["head"], *args)

    return jax.shard_map(
        program,
        mesh=mesh,
        in_specs=(tile_spec,) * 4 + (P(), P(), P("head", None), P()),
        out_specs=(tile_spec,) * 3 + (P(),),
        check_vma=False,
    )
```

```python
import functools

import jax
import jax.numpy as jnp
from jax import lax
from jax.experimental import pallas as pl
from jax.experimental.pallas import tpu as pltpu
from jax.sharding import PartitionSpec as P

MESH = pl.DeviceIdType.MESH
HD = 128
F32 = jnp.float32
BF16 = jnp.bfloat16
SCALE = HD**-0.5
LOG2E = 1.4426950408889634
NT = (((1,), (1,)), ((), ()))
NN = (((1,), (0,)), ((), ()))
TN = (((0,), (0,)), ((), ()))

TIME, SPACE = 2, 4


def dot(a, b, dims):
    return lax.dot_general(a, b, dims, preferred_element_type=F32)


def unit_of(raw):
    x = raw.astype(F32)
    inv = lax.rsqrt(jnp.mean(x * x, axis=1, keepdims=True) + 1e-6)
    return x * inv, inv


def fold(x):
    return jnp.sum(x.reshape(x.shape[0] // 8, 8, x.shape[1]), axis=0)


def kernel(
    T, C, R, H, tile, chunk,
    we, counts, qgain, kgain, qraw, kraw, vals, ograd,
    oq, ok, ov, og,
    hq, hk, hv, ho, qd, kv, pp, dd, stats, sto, sti, dqt, fk, fv,
    xout, xin, zout, zin, rowo, rowi, colo, coli, gacc, gbuf,
    zf_s, zf_r, xf_s, xf_r, cf_s, cf_r, rf_s, rf_r,
    zb_s, zb_r, xb_s, xb_r, cb_s, cb_r, rb_s, rb_r, st_s, st_r, g_s, g_r,
):
    tm = lax.axis_index("tm")
    r = lax.axis_index("space")
    hd = lax.axis_index("head")
    t = lax.div(tm, C)
    c = lax.rem(tm, C)
    tz = t + 1 - 2 * lax.rem(t, 2)
    tx = lax.rem(t + 2, T)
    td = lax.rem(tz + 2, T)

    def dev(t_, c_, r_, h_):
        return (t_ * C + c_, r_, h_)

    def loop(n, body):
        def step(i, carry):
            body(i)
            return carry

        lax.fori_loop(0, n, step, 0)

    def on(condition, action):
        pl.when(condition)(action)

    G0 = T * H
    gi = t * H + hd

    def peer0(j):
        g = lax.rem(gi + j, G0)
        return dev(lax.div(g, H), c, r, lax.rem(g, H))

    def peer1(j):
        return dev(t, lax.rem(c + j, C), r, hd)

    def peer2(j):
        return dev(t, c, lax.rem(r + j, R), hd)

    groups = ((G0, gi, peer0), (C, c, peer1), (R, r, peer2))
    barrier = pltpu.get_barrier_semaphore()
    for size, _, peer in groups:

        def greet(j, peer=peer):
            pl.semaphore_signal(barrier, inc=1, device_id=peer(j + 1), device_id_type=MESH)

        loop(size - 1, greet)

    kinds = [we[0, h] + 2 * we[1, h] for h in range(6)]
    head_of = []
    for kind in range(3):
        low, high = jnp.int32(5), jnp.int32(0)
        for h in range(6):
            low = jnp.minimum(low, jnp.where(kinds[h] == kind, h, 5))
            high = jnp.maximum(high, jnp.where(kinds[h] == kind, h, 0))
        head_of += [low, high]

    def split(h):
        cut = pl.ds(pl.multiple_of(h * HD, HD), HD)
        for by_head, whole in ((hk, kraw), (hv, vals), (hq, qraw), (ho, ograd)):
            by_head[h] = whole[:, cut]

    loop(6, split)

    def raw(ref, slot):
        at = head_of[0]
        for s in range(1, 6):
            at = jnp.where(slot == s, head_of[s], at)
        return ref[at]

    def normed(x, gain):
        unit, _ = unit_of(x)
        return (unit * gain[...]).astype(BF16)

    def count_at(t_, c_, r_):
        inside = (c_ >= 0) & (c_ < C) & (r_ >= 0) & (r_ < R)
        got = counts[t_, lax.rem(c_ + C, C), lax.rem(r_ + R, R)]
        return jnp.where(inside, got, 0)

    own_count = count_at(t, c, r)
    lanes = lax.broadcasted_iota(jnp.int32, (1, tile), 1)
    query_ok = lanes < own_count
    rows_iota = lax.broadcasted_iota(jnp.int32, (chunk, tile), 0)

    def time_row(h, b):
        return 4 + 3 * h + b

    def tile_of(p, h):
        return kv.at[4 + 2 * p + h]

    def side(step):
        return (step + 1) // 2

    def c_ok(step):
        return (c + step >= 0) & (c + step < C)

    def r_ok(step):
        return (r + step >= 0) & (r + step < R)

    def c_dev(step):
        return dev(t, lax.rem(c + step + C, C), r, hd)

    def r_dev(step):
        return dev(t, c, lax.rem(r + step + R, R), hd)

    def copy(src, dst, send, recv, where):
        return pltpu.make_async_remote_copy(
            src_ref=src, dst_ref=dst, send_sem=send, recv_sem=recv, device_id=where, device_id_type=MESH
        )

    def col_fwd(step, h):
        return copy(
            tile_of(4, h), tile_of(4 - step, h), cf_s.at[h, side(step)], cf_r.at[h, side(-step)], c_dev(step)
        )

    def row_fwd(step, dc, h):
        return copy(
            tile_of(4 + dc, h), tile_of(4 + dc - 3 * step, h),
            rf_s.at[h, side(step), 1 + dc], rf_r.at[h, side(-step), 1 + dc], r_dev(step),
        )

    def z_fwd(h):
        return copy(qd.at[4 + 3 * h], qd.at[5 + 3 * h], zf_s.at[h], zf_r.at[h], dev(tz, c, r, hd))

    def x_fwd(h):
        return copy(qd.at[5 + 3 * h], qd.at[6 + 3 * h], xf_s.at[h], xf_r.at[h], dev(tx, c, r, hd))

    def x_bwd(h):
        return copy(xout.at[h], xin.at[h], xb_s.at[h], xb_r.at[h], dev(tx, c, r, hd))

    def z_bwd(h):
        return copy(zout.at[h], zin.at[h], zb_s.at[h], zb_r.at[h], dev(tz, c, r, hd))

    def row_bwd(step, h, i):
        return copy(
            rowo.at[h, side(step), i], rowi.at[h, side(-step), i],
            rb_s.at[h, side(step), i], rb_r.at[h, side(-step), i], r_dev(step),
        )

    def col_bwd(step, h):
        return copy(
            colo.at[h, side(step)], coli.at[h, side(-step)],
            cb_s.at[h, side(step)], cb_r.at[h, side(-step)], c_dev(step),
        )

    others = (tz, tx, td)

    def stat_copy(h, n):
        return copy(sto.at[h], sti.at[h, n], st_s.at[h, n], st_r.at[h, n], dev(others[n], c, r, hd))

    STEPS = (-1, 1)

    pl.semaphore_wait(barrier, G0 - 1 + C - 1 + R - 1)

    def norm_step(i):
        slot = jnp.where(i < 2, i + 4, jnp.where(i < 4, i, i - 4))
        row = jnp.where(i < 2, i + 2, jnp.where(i < 4, 3 * i - 2, i - 4))
        at = jnp.where(i < 2, i + 12, jnp.where(i < 4, i, i - 4))
        kv[at, 0] = normed(raw(hk, slot), kgain)
        kv[at, 1] = raw(hv, slot)
        qd[row, 0] = normed(raw(hq, slot), qgain)
        qd[row, 1] = raw(ho, slot)

        @pl.when(i < 2)
        def _():
            for step in STEPS:
                on(c_ok(step), col_fwd(step, i).start)
            for step in STEPS:
                on(r_ok(step), row_fwd(step, 0, i).start)

    loop(6, norm_step)

    nothing = jnp.zeros((2, 2, tile, HD), BF16)
    for step in STEPS:

        def blank_column(i, step=step):
            kv[pl.ds(4 + 2 * (3 * i + 1 + step), 2)] = nothing

        def blank_row(i, step=step):
            kv[pl.ds(4 + 2 * (3 + 3 * step + i), 2)] = nothing

        on(jnp.logical_not(c_ok(step)), functools.partial(loop, 3, blank_column))
        on(jnp.logical_not(r_ok(step)), functools.partial(loop, 3, blank_row))

    def clear(i):
        stats[i] = jnp.zeros((16, tile), F32)
        dqt[i] = jnp.zeros((HD, tile), F32)
        fk[i] = jnp.zeros((tile, HD), F32)
        fv[i] = jnp.zeros((tile, HD), F32)

    loop(10, clear)
    gacc[...] = jnp.zeros_like(gacc)

    def pass_one(idx, row, at, count):
        query, up = qd[row, 0], qd[row, 1]
        sum_l, sum_d = stats[row, 0:8], stats[row, 8:16]
        for j in range(0, tile, chunk):
            s = dot(kv[at, 0, j : j + chunk], query, NT)
            p = jnp.where(rows_iota < count - j, jnp.exp2(s * (SCALE * LOG2E)), 0.0)
            dp = dot(kv[at, 1, j : j + chunk], up, NT)
            pp[idx, j : j + chunk] = p
            dd[idx, j : j + chunk] = dp
            sum_l = sum_l + fold(p)
            sum_d = sum_d + fold(p * dp)
        stats[row, 0:8] = sum_l
        stats[row, 8:16] = sum_d

    def pass_two(idx, row, at, slot, emit):
        query, up = qd[row, 0], qd[row, 1]
        inv, out_dot = stats[row, 0:1], stats[row, 8:9]
        key_sum = gacc[slot]
        dq = dqt[row]
        for j in range(0, tile, chunk):
            w = pp[idx, j : j + chunk] * inv
            g = (w * (dd[idx, j : j + chunk] - out_dot)).astype(BF16)
            keys = kv[at, 0, j : j + chunk]
            dk = dot(g, query, NN)
            dv = dot(w.astype(BF16), up, NN)
            dq = dq + dot(keys, g, TN)
            key_sum = key_sum + fold(dk * keys.astype(F32))
            emit(j, dk, dv)
        gacc[slot] = key_sum
        dqt[row] = dq

    def added_to(place):
        def emit(j, dk, dv):
            fk[place, pl.ds(j, chunk)] += dk
            fv[place, pl.ds(j, chunk)] += dv

        return emit

    def put_stats(row, total, dot_total, ok_lanes):
        inv = 1.0 / total
        stats[row, 0:8] = jnp.broadcast_to(jnp.where(ok_lanes, inv, 0.0), (8, tile))
        stats[row, 8:16] = jnp.broadcast_to(dot_total * inv, (8, tile))

    def partial(row):
        total = jnp.sum(stats[row, 0:8], axis=0, keepdims=True)
        return total, jnp.sum(stats[row, 8:16], axis=0, keepdims=True)

    def own(i):
        for h in range(2):
            row = jnp.where(i == 1, h, jnp.where(i == 2, 4 + 3 * h, 2 + h))
            at = jnp.where(i == 1, h, jnp.where(i == 2, 2 + h, 12 + h))
            idx = jnp.where(i == 1, h, jnp.where(i == 2, 4 + 3 * h, 18 + h))
            pass_one(idx, row, at, own_count)

    loop(3, own)

    def space_count(p):
        dr = lax.div(p, 3)
        return count_at(t, c + p - 3 * dr - 1, r + dr - 1)

    def cross(i):
        @pl.when(i == 0)
        def _():
            for h in range(2):
                for dc in STEPS:
                    on(c_ok(dc), col_fwd(-dc, h).wait_recv)
                for dc in STEPS:
                    for step in STEPS:
                        on(c_ok(dc) & r_ok(step), row_fwd(step, dc, h).start)
            z_fwd(0).start()

        @pl.when(i == 2)
        def _():
            z_fwd(1).start()
            for h in range(2):
                for dr in STEPS:
                    on(r_ok(dr), row_fwd(-dr, 0, h).wait_recv)

        p = jnp.where(i < 2, 3 + 2 * i, 6 * i - 11)
        count = space_count(p)
        for h in range(2):
            pass_one(10 + 2 * p + h, 2 + h, 4 + 2 * p + h, count)

    loop(4, cross)

    far_count = jnp.where((td - t) * (td - t) == 1, own_count, 0)
    tile_ok = (query_ok, lanes < count_at(tz, c, r), lanes < count_at(td, c, r))

    def time_first(h):
        def step(i):
            on(i == 1, x_fwd(h).wait_recv)
            row = time_row(h, 1 + i)
            pass_one(row, row, 2 + h, jnp.where(i == 1, far_count, own_count))

        loop(2, step)
        for b in range(3):
            total, dot_total = partial(time_row(h, b))
            sto[h, 2 * b : 2 * b + 1] = total
            sto[h, 2 * b + 1 : 2 * b + 2] = dot_total
        sto[h, 6:8] = jnp.zeros((2, tile), F32)
        for n in range(3):
            stat_copy(h, n).start()

    def time_total(h):
        for n in range(3):
            stat_copy(h, n).wait_recv()
        for b, (n, i), (m, k) in ((0, (0, 2), (2, 4)), (1, (0, 0), (1, 4)), (2, (2, 0), (1, 2))):

            def row(q, b=b, n=n, i=i, m=m, k=k):
                mine = sto[h, 2 * b + q : 2 * b + q + 1]
                return mine + sti[h, n, i + q : i + q + 1] + sti[h, m, k + q : k + q + 1]

            put_stats(time_row(h, b), row(0), row(1), tile_ok[b])

    def time_second(h):
        time_total(h)

        def step(i):
            @pl.when(i == 1)
            def _():
                xout[h] = dqt[time_row(h, 2)].astype(BF16)
                x_bwd(h).start()

            row = time_row(h, 2 - i)
            pass_two(row, row, 2 + h, TIME + h, added_to(TIME + h))

        loop(3, step)

    def time_send_back(h):
        x_bwd(h).wait_recv()
        zout[h] = (dqt[time_row(h, 1)] + xin[h].astype(F32)).astype(BF16)
        z_bwd(h).start()

    def corners(h):
        for dr in STEPS:
            for dc in STEPS:
                on(r_ok(dr) & c_ok(dc), row_fwd(-dr, dc, h).wait_recv)

        def corner(i):
            for dc in range(0, 3, 2):
                p = 6 * i + dc
                pass_one(10 + 2 * p + h, 2 + h, 4 + 2 * p + h, space_count(p))

        loop(2, corner)
        put_stats(2 + h, *partial(2 + h), query_ok)

        def outer(i):
            dc = jnp.where(i == 0, 0, 3 - i)
            for d in range(2):

                def emit(j, dk, dv, d=d):
                    rowo[h, d, dc, 0, pl.ds(j, chunk)] = dk.astype(BF16)
                    rowo[h, d, dc, 1, pl.ds(j, chunk)] = dv.astype(BF16)

                p = 6 * d + dc
                pass_two(10 + 2 * p + h, 2 + h, 4 + 2 * p + h, SPACE + h, emit)
            for step in STEPS:
                on(r_ok(step), row_bwd(step, h, dc).start)

        loop(3, outer)

    loop(2, corners)
    z_fwd(0).wait_recv()
    x_fwd(0).start()
    loop(2, lambda row: put_stats(row, *partial(row), query_ok))

    def middle(i):
        p = 2 + i
        for h in range(2):
            idx = jnp.where(i == 0, h, 10 + 2 * p + h)
            row = jnp.where(i == 0, h, 2 + h)
            at = jnp.where(i == 0, h, 4 + 2 * p + h)
            slot = jnp.where(i == 0, h, SPACE + h)
            place = jnp.where(i == 0, h, jnp.where(i == 1, 6 + h, jnp.where(i == 2, SPACE + h, 8 + h)))
            pass_two(idx, row, at, slot, added_to(place))

    loop(4, middle)

    def rows_back(h):
        for i in (0, 2, 1):
            place = SPACE + h if i == 1 else 6 + i + h
            for dr in STEPS:

                def add_row(dr=dr, i=i, place=place):
                    row_bwd(-dr, h, i).wait_recv()
                    fk[place] += rowi[h, side(dr), i, 0].astype(F32)
                    fv[place] += rowi[h, side(dr), i, 1].astype(F32)

                on(r_ok(dr), add_row)
            if i != 1:

                def send_column(step=i - 1, place=place):
                    colo[h, side(step), 0] = fk[place].astype(BF16)
                    colo[h, side(step), 1] = fv[place].astype(BF16)
                    col_bwd(step, h).start()

                on(c_ok(i - 1), send_column)

    z_fwd(1).wait_recv()
    x_fwd(1).start()
    time_first(0)
    rows_back(0)
    time_first(1)
    time_second(0)
    rows_back(1)
    time_send_back(0)
    time_second(1)
    time_send_back(1)

    pair_sum = gacc[0]
    for s in range(1, 6):
        pair_sum = pair_sum + gacc[s]

    def gain_copy(n, j):
        _, mine, peer = groups[n]
        return copy(gbuf.at[n, mine], gbuf.at[n, mine], g_s.at[n, j], g_r.at[n, mine], peer(j))

    def gain_send(n, value):
        size, mine, _ = groups[n]
        gbuf[n, mine] = value
        loop(size - 1, lambda j: gain_copy(n, j + 1).start())

    def gain_sum(n):
        size, mine, peer = groups[n]

        def wait(j):
            other = lax.rem(mine + j + 1, size)
            copy(gbuf.at[n, other], gbuf.at[n, other], g_s.at[n, j + 1], g_r.at[n, other], peer(j + 1)).wait_recv()

        loop(size - 1, wait)
        total = gbuf[n, 0]
        for i in range(1, size):
            total = total + gbuf[n, i]
        return total

    def query_out(s, grad_t):
        grad = jnp.transpose(grad_t) * SCALE
        unit, inv = unit_of(raw(hq, s))
        scaled = grad * qgain[...]
        mean = jnp.mean(scaled * unit, axis=1, keepdims=True)
        oq[s] = (inv * (scaled - unit * mean)).astype(BF16)

    def key_out(s):
        grad = fk[s] * SCALE
        unit, inv = unit_of(raw(hk, s))
        scaled = grad * kgain[...]
        mean = jnp.mean(scaled * unit, axis=1, keepdims=True)
        ok[s] = (inv * (scaled - unit * mean)).astype(BF16)
        ov[s] = fv[s].astype(BF16)

    gain_send(0, pair_sum)
    loop(4, lambda i: query_out(jnp.where(i < 2, i, i + 2), dqt[i]))
    gain_send(1, gain_sum(0))
    loop(4, key_out)
    for h in range(2):
        for dc in STEPS:

            def add_column(dc=dc, h=h):
                col_bwd(-dc, h).wait_recv()
                fk[SPACE + h] += coli[h, side(dc), 0].astype(F32)
                fv[SPACE + h] += coli[h, side(dc), 1].astype(F32)

            on(c_ok(dc), add_column)
    gain_send(2, gain_sum(1))
    loop(2, lambda h: key_out(SPACE + h))
    for h in range(2):
        z_bwd(h).wait_recv()
    loop(2, lambda h: query_out(TIME + h, dqt[time_row(h, 0)] + zin[h].astype(F32)))
    total = jnp.sum(gain_sum(2), axis=0, keepdims=True) * SCALE
    og[...] = jnp.concatenate([total / qgain[...], total / kgain[...]], axis=0)

    for h in range(2):
        for made in (z_fwd, x_fwd, x_bwd, z_bwd):
            made(h).wait_send()
        for n in range(3):
            stat_copy(h, n).wait_send()
    for step in STEPS:
        for h in range(2):
            on(c_ok(step), col_fwd(step, h).wait_send)
            on(r_ok(step), row_fwd(step, 0, h).wait_send)
            for dc in STEPS:
                on(c_ok(dc) & r_ok(step), row_fwd(step, dc, h).wait_send)
            for i in range(3):
                on(r_ok(step), row_bwd(step, h, i).wait_send)
            on(c_ok(step), col_bwd(step, h).wait_send)
    for n, (size, _, _) in enumerate(groups):
        loop(size - 1, lambda j, n=n: gain_copy(n, j + 1).wait_send())


def hand_over(we, q, k, v, gains, oq, ok, ov, og):
    kinds = [we[0, h] + 2 * we[1, h] for h in range(6)]
    for h in range(6):
        slot = 2 * kinds[h]
        for g in range(h):
            slot = slot + jnp.where(kinds[g] == kinds[h], 1, 0)
        for src, dst in ((q, oq), (k, ok), (v, ov)):
            dst[:, h * HD : (h + 1) * HD] = src[slot]
    og[...] = gains[...]


def on_device(T, C, R, H, query_raw, key_raw, values, out_grad, query_gain, key_gain, window_extent, tile_counts):
    tile, width = query_raw.shape[2], query_raw.shape[3]
    chunk = min(128, tile)
    flat = lambda x: x.reshape(tile, width)
    most = max(T * H, C, R)
    dma = pltpu.SemaphoreType.DMA
    vmem = pl.BlockSpec(memory_space=pltpu.VMEM)
    smem = pl.BlockSpec(memory_space=pltpu.SMEM)
    heads = lambda n: pltpu.VMEM((n, tile, HD), BF16)
    pairs = lambda *n: pltpu.VMEM(n + (2, tile, HD), BF16)
    scratch = [
        heads(6), heads(6), heads(6), heads(6),
        pairs(10), pairs(22),
        pltpu.VMEM((28, tile, tile), F32),
        pltpu.VMEM((28, tile, tile), F32),
        pltpu.VMEM((10, 16, tile), F32),
        pltpu.VMEM((2, 8, tile), F32),
        pltpu.VMEM((2, 3, 8, tile), F32),
        pltpu.VMEM((10, HD, tile), F32),
        pltpu.VMEM((10, tile, HD), F32),
        pltpu.VMEM((10, tile, HD), F32),
        pltpu.VMEM((2, HD, tile), BF16),
        pltpu.VMEM((2, HD, tile), BF16),
        pltpu.VMEM((2, HD, tile), BF16),
        pltpu.VMEM((2, HD, tile), BF16),
        pairs(2, 2, 3), pairs(2, 2, 3), pairs(2, 2), pairs(2, 2),
        pltpu.VMEM((6, 8, HD), F32),
        pltpu.VMEM((3, most, 8, HD), F32),
        dma((2,)), dma((2,)), dma((2,)), dma((2,)),
        dma((2, 2)), dma((2, 2)), dma((2, 2, 3)), dma((2, 2, 3)),
        dma((2,)), dma((2,)), dma((2,)), dma((2,)),
        dma((2, 2)), dma((2, 2)), dma((2, 2, 3)), dma((2, 2, 3)),
        dma((2, 3)), dma((2, 3)),
        dma((3, most)), dma((3, most)),
    ]
    wide = jax.ShapeDtypeStruct((6, tile, HD), BF16)
    extent = window_extent.T
    grad_q, grad_k, grad_v, gains = pl.pallas_call(
        functools.partial(kernel, T, C, R, H, tile, chunk),
        out_shape=(wide, wide, wide, jax.ShapeDtypeStruct((2, HD), F32)),
        in_specs=[smem, smem] + [vmem] * 6,
        out_specs=(vmem,) * 4,
        scratch_shapes=scratch,
        compiler_params=pltpu.CompilerParams(
            collective_id=0, has_side_effects=True, vmem_limit_bytes=60 * 1024 * 1024
        ),
    )(
        extent,
        tile_counts,
        query_gain.reshape(1, HD),
        key_gain.reshape(1, HD),
        flat(query_raw),
        flat(key_raw),
        flat(values),
        flat(out_grad),
    )
    whole = jax.ShapeDtypeStruct((tile, width), BF16)
    outs = pl.pallas_call(
        hand_over,
        out_shape=(whole, whole, whole, jax.ShapeDtypeStruct((2, HD), F32)),
        in_specs=[smem] + [vmem] * 4,
        out_specs=(vmem,) * 4,
        compiler_params=pltpu.CompilerParams(vmem_limit_bytes=60 * 1024 * 1024),
    )(extent, grad_q, grad_k, grad_v, gains)
    shape = (1, 1, tile, width)
    return tuple(x.reshape(shape) for x in outs[:3]) + (outs[3],)


def solution(mesh):
    tile_spec = P("tm", "space", None, "head")

    def program(*args):
        T = args[7].shape[0]
        C = mesh.shape["tm"] // T
        return on_device(T, C, mesh.shape["space"], mesh.shape["head"], *args)

    return jax.shard_map(
        program,
        mesh=mesh,
        in_specs=(tile_spec,) * 4 + (P(), P(), P("head", None), P()),
        out_specs=(tile_spec,) * 3 + (P(),),
        check_vma=False,
    )
```

```python
import functools

import jax
import jax.numpy as jnp
from jax import lax
from jax.experimental import pallas as pl
from jax.experimental.pallas import tpu as pltpu
from jax.sharding import PartitionSpec as P

MESH = pl.DeviceIdType.MESH
HD = 128
F32 = jnp.float32
BF16 = jnp.bfloat16
SCALE = HD**-0.5
LOG2E = 1.4426950408889634
NT = (((1,), (1,)), ((), ()))
NN = (((1,), (0,)), ((), ()))
TN = (((0,), (0,)), ((), ()))

TIME, SPACE = 2, 4


def dot(a, b, dims):
    return lax.dot_general(a, b, dims, preferred_element_type=F32)


def unit_of(raw):
    x = raw.astype(F32)
    inv = lax.rsqrt(jnp.mean(x * x, axis=1, keepdims=True) + 1e-6)
    return x * inv, inv


def fold(x):
    return jnp.sum(x.reshape(x.shape[0] // 8, 8, x.shape[1]), axis=0)


def kernel(
    T, C, R, H, tile, chunk,
    we, counts, qgain, kgain, qraw, kraw, vals, ograd,
    oq, ok, ov, og,
    hq, hk, hv, ho, qd, kv, pp, dd, stats, sto, sti, dqt, fk, fv,
    xout, xin, zout, zin, rowo, rowi, colo, coli, gacc, gbuf,
    zf_s, zf_r, xf_s, xf_r, cf_s, cf_r, rf_s, rf_r,
    zb_s, zb_r, xb_s, xb_r, cb_s, cb_r, rb_s, rb_r, st_s, st_r, g_s, g_r,
):
    tm = lax.axis_index("tm")
    r = lax.axis_index("space")
    hd = lax.axis_index("head")
    t = lax.div(tm, C)
    c = lax.rem(tm, C)
    tz = t + 1 - 2 * lax.rem(t, 2)
    tx = lax.rem(t + 2, T)
    td = lax.rem(tz + 2, T)

    def dev(t_, c_, r_, h_):
        return (t_ * C + c_, r_, h_)

    def loop(n, body):
        def step(i, carry):
            body(i)
            return carry

        lax.fori_loop(0, n, step, 0)

    def on(condition, action):
        pl.when(condition)(action)

    G0 = T * H
    gi = t * H + hd

    def peer0(j):
        g = lax.rem(gi + j, G0)
        return dev(lax.div(g, H), c, r, lax.rem(g, H))

    def peer1(j):
        return dev(t, lax.rem(c + j, C), r, hd)

    def peer2(j):
        return dev(t, c, lax.rem(r + j, R), hd)

    groups = ((G0, gi, peer0), (C, c, peer1), (R, r, peer2))
    barrier = pltpu.get_barrier_semaphore()
    for size, _, peer in groups:

        def greet(j, peer=peer):
            pl.semaphore_signal(barrier, inc=1, device_id=peer(j + 1), device_id_type=MESH)

        loop(size - 1, greet)

    kinds = [we[0, h] + 2 * we[1, h] for h in range(6)]
    head_of = []
    for kind in range(3):
        low, high = jnp.int32(5), jnp.int32(0)
        for h in range(6):
            low = jnp.minimum(low, jnp.where(kinds[h] == kind, h, 5))
            high = jnp.maximum(high, jnp.where(kinds[h] == kind, h, 0))
        head_of += [low, high]

    def split(h):
        cut = pl.ds(pl.multiple_of(h * HD, HD), HD)
        for by_head, whole in ((hk, kraw), (hv, vals), (hq, qraw), (ho, ograd)):
            by_head[h] = whole[:, cut]

    loop(6, split)

    def raw(ref, slot):
        at = head_of[0]
        for s in range(1, 6):
            at = jnp.where(slot == s, head_of[s], at)
        return ref[at]

    def normed(x, gain):
        unit, _ = unit_of(x)
        return (unit * gain[...]).astype(BF16)

    def count_at(t_, c_, r_):
        inside = (c_ >= 0) & (c_ < C) & (r_ >= 0) & (r_ < R)
        got = counts[t_, lax.rem(c_ + C, C), lax.rem(r_ + R, R)]
        return jnp.where(inside, got, 0)

    own_count = count_at(t, c, r)
    lanes = lax.broadcasted_iota(jnp.int32, (1, tile), 1)
    query_ok = lanes < own_count
    rows_iota = lax.broadcasted_iota(jnp.int32, (chunk, tile), 0)

    def time_row(h, b):
        return 4 + 3 * h + b

    def tile_of(p, h):
        return kv.at[4 + 2 * p + h]

    def side(step):
        return (step + 1) // 2

    def c_ok(step):
        return (c + step >= 0) & (c + step < C)

    def r_ok(step):
        return (r + step >= 0) & (r + step < R)

    def c_dev(step):
        return dev(t, lax.rem(c + step + C, C), r, hd)

    def r_dev(step):
        return dev(t, c, lax.rem(r + step + R, R), hd)

    def copy(src, dst, send, recv, where):
        return pltpu.make_async_remote_copy(
            src_ref=src, dst_ref=dst, send_sem=send, recv_sem=recv, device_id=where, device_id_type=MESH
        )

    def col_fwd(step, h):
        return copy(
            tile_of(4, h), tile_of(4 - step, h), cf_s.at[h, side(step)], cf_r.at[h, side(-step)], c_dev(step)
        )

    def row_fwd(step, dc, h):
        return copy(
            tile_of(4 + dc, h), tile_of(4 + dc - 3 * step, h),
            rf_s.at[h, side(step), 1 + dc], rf_r.at[h, side(-step), 1 + dc], r_dev(step),
        )

    def z_fwd(h):
        return copy(qd.at[4 + 3 * h], qd.at[5 + 3 * h], zf_s.at[h], zf_r.at[h], dev(tz, c, r, hd))

    def x_fwd(h):
        return copy(qd.at[5 + 3 * h], qd.at[6 + 3 * h], xf_s.at[h], xf_r.at[h], dev(tx, c, r, hd))

    def x_bwd(h):
        return copy(xout.at[h], xin.at[h], xb_s.at[h], xb_r.at[h], dev(tx, c, r, hd))

    def z_bwd(h):
        return copy(zout.at[h], zin.at[h], zb_s.at[h], zb_r.at[h], dev(tz, c, r, hd))

    def row_bwd(step, h, i):
        return copy(
            rowo.at[h, side(step), i], rowi.at[h, side(-step), i],
            rb_s.at[h, side(step), i], rb_r.at[h, side(-step), i], r_dev(step),
        )

    def col_bwd(step, h):
        return copy(
            colo.at[h, side(step)], coli.at[h, side(-step)],
            cb_s.at[h, side(step)], cb_r.at[h, side(-step)], c_dev(step),
        )

    others = (tz, tx, td)

    def stat_copy(h, n):
        return copy(sto.at[h], sti.at[h, n], st_s.at[h, n], st_r.at[h, n], dev(others[n], c, r, hd))

    STEPS = (-1, 1)

    pl.semaphore_wait(barrier, G0 - 1 + C - 1 + R - 1)

    def norm_step(i):
        slot = jnp.where(i < 2, i + 4, jnp.where(i < 4, i, i - 4))
        row = jnp.where(i < 2, i + 2, jnp.where(i < 4, 3 * i - 2, i - 4))
        at = jnp.where(i < 2, i + 12, jnp.where(i < 4, i, i - 4))
        kv[at, 0] = normed(raw(hk, slot), kgain)
        kv[at, 1] = raw(hv, slot)
        qd[row, 0] = normed(raw(hq, slot), qgain)
        qd[row, 1] = raw(ho, slot)

        @pl.when(i < 2)
        def _():
            for step in STEPS:
                on(c_ok(step), col_fwd(step, i).start)
            for step in STEPS:
                on(r_ok(step), row_fwd(step, 0, i).start)

    loop(6, norm_step)

    nothing = jnp.zeros((2, 2, tile, HD), BF16)
    for step in STEPS:

        def blank_column(i, step=step):
            kv[pl.ds(4 + 2 * (3 * i + 1 + step), 2)] = nothing

        def blank_row(i, step=step):
            kv[pl.ds(4 + 2 * (3 + 3 * step + i), 2)] = nothing

        on(jnp.logical_not(c_ok(step)), functools.partial(loop, 3, blank_column))
        on(jnp.logical_not(r_ok(step)), functools.partial(loop, 3, blank_row))

    def clear(i):
        stats[i] = jnp.zeros((16, tile), F32)
        dqt[i] = jnp.zeros((HD, tile), F32)
        fk[i] = jnp.zeros((tile, HD), F32)
        fv[i] = jnp.zeros((tile, HD), F32)

    loop(10, clear)
    gacc[...] = jnp.zeros_like(gacc)

    def pass_one(idx, row, at, count):
        query, up = qd[row, 0], qd[row, 1]
        sum_l, sum_d = stats[row, 0:8], stats[row, 8:16]
        for j in range(0, tile, chunk):
            s = dot(kv[at, 0, j : j + chunk], query, NT)
            p = jnp.where(rows_iota < count - j, jnp.exp2(s * (SCALE * LOG2E)), 0.0)
            dp = dot(kv[at, 1, j : j + chunk], up, NT)
            pp[idx, j : j + chunk] = p
            dd[idx, j : j + chunk] = dp
            sum_l = sum_l + fold(p)
            sum_d = sum_d + fold(p * dp)
        stats[row, 0:8] = sum_l
        stats[row, 8:16] = sum_d

    def pass_two(idx, row, at, slot, emit):
        query, up = qd[row, 0], qd[row, 1]
        inv, out_dot = stats[row, 0:1], stats[row, 8:9]
        key_sum = gacc[slot]
        dq = dqt[row]
        for j in range(0, tile, chunk):
            w = pp[idx, j : j + chunk] * inv
            g = (w * (dd[idx, j : j + chunk] - out_dot)).astype(BF16)
            keys = kv[at, 0, j : j + chunk]
            dk = dot(g, query, NN)
            dv = dot(w.astype(BF16), up, NN)
            dq = dq + dot(keys, g, TN)
            key_sum = key_sum + fold(dk * keys.astype(F32))
            emit(j, dk, dv)
        gacc[slot] = key_sum
        dqt[row] = dq

    def added_to(place):
        def emit(j, dk, dv):
            fk[place, pl.ds(j, chunk)] += dk
            fv[place, pl.ds(j, chunk)] += dv

        return emit

    def put_stats(row, total, dot_total, ok_lanes):
        inv = 1.0 / total
        stats[row, 0:8] = jnp.broadcast_to(jnp.where(ok_lanes, inv, 0.0), (8, tile))
        stats[row, 8:16] = jnp.broadcast_to(dot_total * inv, (8, tile))

    def partial(row):
        total = jnp.sum(stats[row, 0:8], axis=0, keepdims=True)
        return total, jnp.sum(stats[row, 8:16], axis=0, keepdims=True)

    def own(i):
        for h in range(2):
            row = jnp.where(i == 1, h, jnp.where(i == 2, 4 + 3 * h, 2 + h))
            at = jnp.where(i == 1, h, jnp.where(i == 2, 2 + h, 12 + h))
            idx = jnp.where(i == 1, h, jnp.where(i == 2, 4 + 3 * h, 18 + h))
            pass_one(idx, row, at, own_count)

    loop(3, own)

    def space_count(p):
        dr = lax.div(p, 3)
        return count_at(t, c + p - 3 * dr - 1, r + dr - 1)

    def cross(i):
        @pl.when(i == 0)
        def _():
            for h in range(2):
                for dc in STEPS:
                    on(c_ok(dc), col_fwd(-dc, h).wait_recv)
                for dc in STEPS:
                    for step in STEPS:
                        on(c_ok(dc) & r_ok(step), row_fwd(step, dc, h).start)
            z_fwd(0).start()

        @pl.when(i == 2)
        def _():
            z_fwd(1).start()
            for h in range(2):
                for dr in STEPS:
                    on(r_ok(dr), row_fwd(-dr, 0, h).wait_recv)

        p = jnp.where(i < 2, 3 + 2 * i, 6 * i - 11)
        count = space_count(p)
        for h in range(2):
            pass_one(10 + 2 * p + h, 2 + h, 4 + 2 * p + h, count)

    loop(4, cross)

    far_count = jnp.where((td - t) * (td - t) == 1, own_count, 0)
    tile_ok = (query_ok, lanes < count_at(tz, c, r), lanes < count_at(td, c, r))

    def time_first(h):
        def step(i):
            on(i == 1, x_fwd(h).wait_recv)
            row = time_row(h, 1 + i)
            pass_one(row, row, 2 + h, jnp.where(i == 1, far_count, own_count))

        loop(2, step)
        for b in range(3):
            total, dot_total = partial(time_row(h, b))
            sto[h, 2 * b : 2 * b + 1] = total
            sto[h, 2 * b + 1 : 2 * b + 2] = dot_total
        sto[h, 6:8] = jnp.zeros((2, tile), F32)
        for n in range(3):
            stat_copy(h, n).start()

    def time_total(h):
        for n in range(3):
            stat_copy(h, n).wait_recv()
        for b, (n, i), (m, k) in ((0, (0, 2), (2, 4)), (1, (0, 0), (1, 4)), (2, (2, 0), (1, 2))):

            def row(q, b=b, n=n, i=i, m=m, k=k):
                mine = sto[h, 2 * b + q : 2 * b + q + 1]
                return mine + sti[h, n, i + q : i + q + 1] + sti[h, m, k + q : k + q + 1]

            put_stats(time_row(h, b), row(0), row(1), tile_ok[b])

    def time_second(h):
        time_total(h)

        def step(i):
            @pl.when(i == 1)
            def _():
                xout[h] = dqt[time_row(h, 2)].astype(BF16)
                x_bwd(h).start()

            row = time_row(h, 2 - i)
            pass_two(row, row, 2 + h, TIME + h, added_to(TIME + h))

        loop(3, step)

    def time_send_back(h):
        x_bwd(h).wait_recv()
        zout[h] = (dqt[time_row(h, 1)] + xin[h].astype(F32)).astype(BF16)
        z_bwd(h).start()

    def corners(h):
        for dr in STEPS:
            for dc in STEPS:
                on(r_ok(dr) & c_ok(dc), row_fwd(-dr, dc, h).wait_recv)

        def corner(i):
            for dc in range(0, 3, 2):
                p = 6 * i + dc
                pass_one(10 + 2 * p + h, 2 + h, 4 + 2 * p + h, space_count(p))

        loop(2, corner)
        put_stats(2 + h, *partial(2 + h), query_ok)

        def outer(i):
            dc = jnp.where(i == 0, 0, 3 - i)
            for d in range(2):

                def emit(j, dk, dv, d=d):
                    rowo[h, d, dc, 0, pl.ds(j, chunk)] = dk.astype(BF16)
                    rowo[h, d, dc, 1, pl.ds(j, chunk)] = dv.astype(BF16)

                p = 6 * d + dc
                pass_two(10 + 2 * p + h, 2 + h, 4 + 2 * p + h, SPACE + h, emit)
            for step in STEPS:
                on(r_ok(step), row_bwd(step, h, dc).start)

        loop(3, outer)

    loop(2, corners)
    z_fwd(0).wait_recv()
    x_fwd(0).start()
    loop(2, lambda row: put_stats(row, *partial(row), query_ok))

    def middle(i):
        p = 2 + i
        for h in range(2):
            idx = jnp.where(i == 0, h, 10 + 2 * p + h)
            row = jnp.where(i == 0, h, 2 + h)
            at = jnp.where(i == 0, h, 4 + 2 * p + h)
            slot = jnp.where(i == 0, h, SPACE + h)
            place = jnp.where(i == 0, h, jnp.where(i == 1, 6 + h, jnp.where(i == 2, SPACE + h, 8 + h)))
            pass_two(idx, row, at, slot, added_to(place))

    loop(4, middle)

    def rows_back(h):
        for i in (0, 2, 1):
            place = SPACE + h if i == 1 else 6 + i + h
            for dr in STEPS:

                def add_row(dr=dr, i=i, place=place):
                    row_bwd(-dr, h, i).wait_recv()
                    fk[place] += rowi[h, side(dr), i, 0].astype(F32)
                    fv[place] += rowi[h, side(dr), i, 1].astype(F32)

                on(r_ok(dr), add_row)
            if i != 1:

                def send_column(step=i - 1, place=place):
                    colo[h, side(step), 0] = fk[place].astype(BF16)
                    colo[h, side(step), 1] = fv[place].astype(BF16)
                    col_bwd(step, h).start()

                on(c_ok(i - 1), send_column)

    z_fwd(1).wait_recv()
    x_fwd(1).start()
    time_first(0)
    rows_back(0)
    time_first(1)
    time_second(0)
    rows_back(1)
    time_send_back(0)
    time_second(1)
    time_send_back(1)

    pair_sum = gacc[0]
    for s in range(1, 6):
        pair_sum = pair_sum + gacc[s]

    def gain_copy(n, j):
        _, mine, peer = groups[n]
        return copy(gbuf.at[n, mine], gbuf.at[n, mine], g_s.at[n, j], g_r.at[n, mine], peer(j))

    def gain_send(n, value):
        size, mine, _ = groups[n]
        gbuf[n, mine] = value
        loop(size - 1, lambda j: gain_copy(n, j + 1).start())

    def gain_sum(n):
        size, mine, peer = groups[n]

        def wait(j):
            other = lax.rem(mine + j + 1, size)
            copy(gbuf.at[n, other], gbuf.at[n, other], g_s.at[n, j + 1], g_r.at[n, other], peer(j + 1)).wait_recv()

        loop(size - 1, wait)
        total = gbuf[n, 0]
        for i in range(1, size):
            total = total + gbuf[n, i]
        return total

    def query_out(s, grad_t):
        grad = jnp.transpose(grad_t) * SCALE
        unit, inv = unit_of(raw(hq, s))
        scaled = grad * qgain[...]
        mean = jnp.mean(scaled * unit, axis=1, keepdims=True)
        oq[s] = (inv * (scaled - unit * mean)).astype(BF16)

    def key_out(s):
        grad = fk[s] * SCALE
        unit, inv = unit_of(raw(hk, s))
        scaled = grad * kgain[...]
        mean = jnp.mean(scaled * unit, axis=1, keepdims=True)
        ok[s] = (inv * (scaled - unit * mean)).astype(BF16)
        ov[s] = fv[s].astype(BF16)

    gain_send(0, pair_sum)
    loop(4, lambda i: query_out(jnp.where(i < 2, i, i + 2), dqt[i]))
    gain_send(1, gain_sum(0))
    loop(4, key_out)
    for h in range(2):
        for dc in STEPS:

            def add_column(dc=dc, h=h):
                col_bwd(-dc, h).wait_recv()
                fk[SPACE + h] += coli[h, side(dc), 0].astype(F32)
                fv[SPACE + h] += coli[h, side(dc), 1].astype(F32)

            on(c_ok(dc), add_column)
    gain_send(2, gain_sum(1))
    loop(2, lambda h: key_out(SPACE + h))
    for h in range(2):
        z_bwd(h).wait_recv()
    loop(2, lambda h: query_out(TIME + h, dqt[time_row(h, 0)] + zin[h].astype(F32)))
    total = jnp.sum(gain_sum(2), axis=0, keepdims=True) * SCALE
    og[...] = jnp.concatenate([total / qgain[...], total / kgain[...]], axis=0)

    for h in range(2):
        for made in (z_fwd, x_fwd, x_bwd, z_bwd):
            made(h).wait_send()
        for n in range(3):
            stat_copy(h, n).wait_send()
    for step in STEPS:
        for h in range(2):
            on(c_ok(step), col_fwd(step, h).wait_send)
            on(r_ok(step), row_fwd(step, 0, h).wait_send)
            for dc in STEPS:
                on(c_ok(dc) & r_ok(step), row_fwd(step, dc, h).wait_send)
            for i in range(3):
                on(r_ok(step), row_bwd(step, h, i).wait_send)
            on(c_ok(step), col_bwd(step, h).wait_send)
    for n, (size, _, _) in enumerate(groups):
        loop(size - 1, lambda j, n=n: gain_copy(n, j + 1).wait_send())


def hand_over(we, q, k, v, gains, oq, ok, ov, og):
    kinds = [we[0, h] + 2 * we[1, h] for h in range(6)]
    for h in range(6):
        slot = 2 * kinds[h]
        for g in range(h):
            slot = slot + jnp.where(kinds[g] == kinds[h], 1, 0)
        for src, dst in ((q, oq), (k, ok), (v, ov)):
            dst[:, h * HD : (h + 1) * HD] = src[slot]
    og[...] = gains[...]


def on_device(T, C, R, H, query_raw, key_raw, values, out_grad, query_gain, key_gain, window_extent, tile_counts):
    tile, width = query_raw.shape[2], query_raw.shape[3]
    chunk = min(256, tile)
    flat = lambda x: x.reshape(tile, width)
    most = max(T * H, C, R)
    dma = pltpu.SemaphoreType.DMA
    vmem = pl.BlockSpec(memory_space=pltpu.VMEM)
    smem = pl.BlockSpec(memory_space=pltpu.SMEM)
    heads = lambda n: pltpu.VMEM((n, tile, HD), BF16)
    pairs = lambda *n: pltpu.VMEM(n + (2, tile, HD), BF16)
    scratch = [
        heads(6), heads(6), heads(6), heads(6),
        pairs(10), pairs(22),
        pltpu.VMEM((28, tile, tile), F32),
        pltpu.VMEM((28, tile, tile), F32),
        pltpu.VMEM((10, 16, tile), F32),
        pltpu.VMEM((2, 8, tile), F32),
        pltpu.VMEM((2, 3, 8, tile), F32),
        pltpu.VMEM((10, HD, tile), F32),
        pltpu.VMEM((10, tile, HD), F32),
        pltpu.VMEM((10, tile, HD), F32),
        pltpu.VMEM((2, HD, tile), BF16),
        pltpu.VMEM((2, HD, tile), BF16),
        pltpu.VMEM((2, HD, tile), BF16),
        pltpu.VMEM((2, HD, tile), BF16),
        pairs(2, 2, 3), pairs(2, 2, 3), pairs(2, 2), pairs(2, 2),
        pltpu.VMEM((6, 8, HD), F32),
        pltpu.VMEM((3, most, 8, HD), F32),
        dma((2,)), dma((2,)), dma((2,)), dma((2,)),
        dma((2, 2)), dma((2, 2)), dma((2, 2, 3)), dma((2, 2, 3)),
        dma((2,)), dma((2,)), dma((2,)), dma((2,)),
        dma((2, 2)), dma((2, 2)), dma((2, 2, 3)), dma((2, 2, 3)),
        dma((2, 3)), dma((2, 3)),
        dma((3, most)), dma((3, most)),
    ]
    wide = jax.ShapeDtypeStruct((6, tile, HD), BF16)
    extent = window_extent.T
    grad_q, grad_k, grad_v, gains = pl.pallas_call(
        functools.partial(kernel, T, C, R, H, tile, chunk),
        out_shape=(wide, wide, wide, jax.ShapeDtypeStruct((2, HD), F32)),
        in_specs=[smem, smem] + [vmem] * 6,
        out_specs=(vmem,) * 4,
        scratch_shapes=scratch,
        compiler_params=pltpu.CompilerParams(
            collective_id=0, has_side_effects=True, vmem_limit_bytes=60 * 1024 * 1024
        ),
    )(
        extent,
        tile_counts,
        query_gain.reshape(1, HD),
        key_gain.reshape(1, HD),
        flat(query_raw),
        flat(key_raw),
        flat(values),
        flat(out_grad),
    )
    whole = jax.ShapeDtypeStruct((tile, width), BF16)
    outs = pl.pallas_call(
        hand_over,
        out_shape=(whole, whole, whole, jax.ShapeDtypeStruct((2, HD), F32)),
        in_specs=[smem] + [vmem] * 4,
        out_specs=(vmem,) * 4,
        compiler_params=pltpu.CompilerParams(vmem_limit_bytes=60 * 1024 * 1024),
    )(extent, grad_q, grad_k, grad_v, gains)
    shape = (1, 1, tile, width)
    return tuple(x.reshape(shape) for x in outs[:3]) + (outs[3],)


def solution(mesh):
    tile_spec = P("tm", "space", None, "head")

    def program(*args):
        T = args[7].shape[0]
        C = mesh.shape["tm"] // T
        return on_device(T, C, mesh.shape["space"], mesh.shape["head"], *args)

    return jax.shard_map(
        program,
        mesh=mesh,
        in_specs=(tile_spec,) * 4 + (P(), P(), P("head", None), P()),
        out_specs=(tile_spec,) * 3 + (P(),),
        check_vma=False,
    )
```
